32 devices in a mesh: dp: 8 (over y, x, core), mp: 4 (over z).
Axes of the slice: x: 2, y: 2, z: 4, core: 2. Of those that a mesh axis runs over, the one named last changes fastest.
Arguments:
- inputs: bfloat16 [512, 65536], P('mp', 'dp'), may hold values from -24 to 24
- cotangent: bfloat16 [512, 65536], P('mp', 'dp'), may hold values from -4 to 4
- member_mask: int32 [2048, 32], P('dp'), may hold values from 0 to 1, as said below
- members: float32 [6, 32, 512], P(None, 'dp', 'mp'), may hold values from -3 to 3
- first_moment: float32 [6, 32, 512], P(None, 'dp', 'mp')
- second_moment: float32 [6, 32, 512], P(None, 'dp', 'mp'), as said below
- first_weight: float32 [512, 512], P('dp', 'mp'), may hold values from -0.25 to 0.25
- second_weight: float32 [512, 512], P('mp', 'dp'), may hold values from -0.25 to 0.25
- first_left: float32 [512, 512], P('dp', 'mp')
- first_right: float32 [512, 512], P('dp', 'mp')
- second_left: float32 [512, 512], P('mp', 'dp')
- second_right: float32 [512, 512], P('mp', 'dp')
- first_left_root: float32 [512, 512], P('dp')
- first_right_root: float32 [512, 512], P('mp')
- second_left_root: float32 [512, 512], P('mp')
- second_right_root: float32 [512, 512], P('dp')
Outputs:
- logits: bfloat16 [512, 65536], P('mp', 'dp')
- input_grad: bfloat16 [512, 65536], P('mp', 'dp')
- rms_stats: float32 [2], replicated
- first_grad: float32 [512, 512], P('dp', 'mp')
- first_new: float32 [512, 512], P('dp', 'mp')
- first_left_new: float32 [512, 512], P('dp', 'mp')
- first_right_new: float32 [512, 512], P('dp', 'mp')
- second_grad: float32 [512, 512], P('mp', 'dp')
- second_new: float32 [512, 512], P('mp', 'dp')
- second_left_new: float32 [512, 512], P('mp', 'dp')
- second_right_new: float32 [512, 512], P('mp', 'dp')
- moment_one_new: float32 [6, 32, 512], P(None, 'dp', 'mp')
- moment_two_new: float32 [6, 32, 512], P(None, 'dp', 'mp')
- members_new: float32 [6, 32, 512], P(None, 'dp', 'mp')
The draws below stay inside these ranges and needn't reach their ends.
Inputs may be any that keep to these rules, and one draw needn't show every extreme that they name: `member_mask`: each object has between 8 and 32 trained members; some object has exactly 8 and some exactly 32. `second_moment`: positive.
All inputs are finite; a program needn't handle non-finite values.
Results may differ from the reference program's by a relative error of at most 0.0087.
Values may be sent and summed in bfloat16 or wider, within the bound.
A program may use at most 128 MiB of HBM per device.

```python
import math
import jax
import jax.numpy as jnp
from jax import lax

D = 512
K = 32
STEP = 10
OBJECTS = 2048
ROWS = 65536


def spread_factor(key, shape, low_value, high_value):
    return jnp.exp(jax.random.uniform(key, shape, jnp.float32, math.log(low_value), math.log(high_value)))


def draw_inputs(key, part):
    subkeys = jax.random.split(key, 3)
    base = jnp.clip(jax.random.normal(subkeys[0], (ROWS, D), jnp.float32), -4.0, 4.0)
    rise = 3.0
    row_pos = jnp.arange(ROWS, dtype=jnp.float32) / max(ROWS - 1, 1)
    col_pos = jnp.arange(D, dtype=jnp.float32) / max(D - 1, 1)
    row_scale = jnp.power(rise, 0.5 * row_pos) * spread_factor(subkeys[1], (ROWS,), 0.7, 1.4)
    col_scale = jnp.power(rise, 0.5 * col_pos) * spread_factor(subkeys[2], (D,), 0.7, 1.4)
    return (base * row_scale[:, None] * col_scale[None, :]).T.astype(jnp.bfloat16)


def draw_member_mask(key, part):
    subkeys = jax.random.split(key, 3)
    counts = jax.random.randint(subkeys[0], (OBJECTS,), 8, K + 1)
    chosen = jax.random.randint(subkeys[1], (), 0, OBJECTS)
    position = jnp.arange(OBJECTS)
    counts = jnp.where(position == chosen, K, jnp.where(position == (chosen + 1) % OBJECTS, 8, counts))
    scores = jax.random.randint(subkeys[2], (OBJECTS, K), 0, 1 << 20) * K + jnp.arange(K)[None, :]
    ranks = jnp.argsort(jnp.argsort(scores, axis=1), axis=1)
    return (ranks < counts[:, None]).astype(jnp.int32)


def draw_members(key, part):
    subkeys = jax.random.split(key, 2)
    col_pos = jnp.arange(D, dtype=jnp.float32) / max(D - 1, 1)
    gains = jax.random.uniform(subkeys[0], (4, K, D), jnp.float32, 0.6, 1.4)
    biases = 0.3 * jnp.clip(jax.random.normal(subkeys[1], (2, K, D), jnp.float32), -4.0, 4.0)
    rising = jnp.power(3.0, 0.5 * col_pos)
    return jnp.stack([gains[0], gains[1], biases[0], gains[2], gains[3] * rising[None, :], biases[1]])


def draw_first_moment(key, part):
    subkeys = jax.random.split(key, 2)
    base = jnp.clip(jax.random.normal(subkeys[0], (6, K, D), jnp.float32), -3.0, 3.0)
    return base * 0.11 * math.sqrt(OBJECTS) * jax.random.uniform(subkeys[1], (6, K, D), jnp.float32, 0.5, 1.5)


def draw_second_moment(key, part):
    return spread_factor(key, (6, K, D), 1.0, 4.0) * 0.001 * OBJECTS


def stat_matrix(key, salt):
    subkeys = jax.random.split(jax.random.fold_in(key, salt), 2)
    scale = 0.05 * D * K * OBJECTS
    position = jnp.arange(D)
    identity = (position[:, None] == position[None, :]).astype(jnp.float32)
    diagonal = spread_factor(subkeys[0], (D,), 1.0, 4.0)
    noise = jnp.clip(jax.random.normal(subkeys[1], (D, D), jnp.float32), -4.0, 4.0)
    symmetric = (noise + noise.T) * (0.3 / math.sqrt(2 * D))
    return scale * (identity * diagonal[None, :] + symmetric)


def root_matrix(key, salt):
    subkeys = jax.random.split(jax.random.fold_in(key, salt), 2)
    scale = (D * K * OBJECTS) ** (-0.25)
    position = jnp.arange(D)
    identity = (position[:, None] == position[None, :]).astype(jnp.float32)
    diagonal = jax.random.uniform(subkeys[0], (D,), jnp.float32, 0.5, 1.5)
    noise = jnp.clip(jax.random.normal(subkeys[1], (D, D), jnp.float32), -4.0, 4.0) * (0.5 / math.sqrt(D))
    return scale * (identity * diagonal[None, :] + noise)


def draw_first_left(key, part):
    return stat_matrix(key, 11)


def draw_first_right(key, part):
    return stat_matrix(key, 12)


def draw_second_left(key, part):
    return stat_matrix(key, 13)


def draw_second_right(key, part):
    return stat_matrix(key, 14)


def draw_first_left_root(key, part):
    return root_matrix(key, 21)


def draw_first_right_root(key, part):
    return root_matrix(key, 22)


def draw_second_left_root(key, part):
    return root_matrix(key, 23)


def draw_second_right_root(key, part):
    return root_matrix(key, 24)


def level_of(key, dims, pieces, smallest, top_value):
    gain, own = 1.0, jax.random.fold_in(key, 6)
    for dim, parts in pieces:
        steps = jnp.exp(jax.random.uniform(jax.random.fold_in(own, dim), (parts,), jnp.float32, smallest / len(pieces), top_value / len(pieces)))
        gain = gain * jnp.repeat(steps, dims[dim] // parts).reshape([-1 if axis == dim else 1 for axis in range(len(dims))])
    return gain


def normal_values(own_key, shape, deviation, bound, cuts=(), kind=jnp.bfloat16):
    loudness = level_of(own_key, shape, cuts, -0.22, 0.18) if cuts else 1.0
    entries = jax.random.normal(own_key, shape, jnp.float32) * deviation * loudness
    return jnp.minimum(jnp.maximum(entries, -bound), bound).astype(kind)


def setup_inputs(seed: int = 0) -> dict:
    key_list = jax.random.split(jax.random.key(seed), 17)
    return {
        "inputs": draw_inputs(jax.random.fold_in(key_list[16], 71), 0),
        "cotangent": normal_values(key_list[1], (D, ROWS), 1.0, 4.0, ((0, 4), (1, 8))),
        "member_mask": draw_member_mask(jax.random.fold_in(key_list[16], 71), 0),
        "members": draw_members(jax.random.fold_in(key_list[16], 71), 0),
        "first_moment": draw_first_moment(jax.random.fold_in(key_list[16], 71), 0),
        "second_moment": draw_second_moment(jax.random.fold_in(key_list[16], 71), 0),
        "first_weight": normal_values(key_list[6], (D, D), D ** -0.5, 0.25, ((0, 8), (1, 4)), jnp.float32),
        "second_weight": normal_values(key_list[7], (D, D), D ** -0.5, 0.25, ((0, 4), (1, 8)), jnp.float32),
        "first_left": draw_first_left(jax.random.fold_in(key_list[16], 71), 0),
        "first_right": draw_first_right(jax.random.fold_in(key_list[16], 71), 0),
        "second_left": draw_second_left(jax.random.fold_in(key_list[16], 71), 0),
        "second_right": draw_second_right(jax.random.fold_in(key_list[16], 71), 0),
        "first_left_root": draw_first_left_root(jax.random.fold_in(key_list[16], 71), 0),
        "first_right_root": draw_first_right_root(jax.random.fold_in(key_list[16], 71), 0),
        "second_left_root": draw_second_left_root(jax.random.fold_in(key_list[16], 71), 0),
        "second_right_root": draw_second_right_root(jax.random.fold_in(key_list[16], 71), 0),
    }


@jax.custom_vjp
def low(v):
    return lax.optimization_barrier(v.astype(jnp.bfloat16)).astype(jnp.float32)

@jax.custom_vjp
def low_back(v):
    return v

def low_keep(v):
    return (low(v), None)

def low_pass(kept, grad):
    return (grad,)

def back_keep(v):
    return (v, None)

def back_low(kept, grad):
    return (low(grad),)
low.defvjp(low_keep, low_pass)
low_back.defvjp(back_keep, back_low)
beta_first = 0.9
beta_second = 0.999
adam_eps = 1e-08
adam_rate = 0.2
stat_decay = 0.95
shampoo_rate = 1.0

def forward(values, members, first_weight, second_weight):
    high = lax.Precision.HIGHEST
    count = values.shape[0] // K
    tables = [jnp.tile(members[index], (count, 1)) for index in range(6)]
    row_in, gain_in, bias_in, row_mid, gain_out, bias_out = tables
    scaled = low(values * row_in)
    hidden_pre = low_back(jnp.dot(scaled, low(first_weight), precision=high))
    shifted = hidden_pre * gain_in + bias_in
    hidden = jax.nn.gelu(shifted)
    hidden_in = low(hidden * row_mid)
    projected = low_back(jnp.dot(hidden_in, low(second_weight), precision=high))
    branch = projected * gain_out + bias_out
    return (values + branch, branch)

def precondition(grad, left, right, left_root, right_root_t, weight):
    high = lax.Precision.HIGHEST
    left_new = stat_decay * left + (1.0 - stat_decay) * jnp.dot(grad, grad.T, precision=high)
    right_new = stat_decay * right + (1.0 - stat_decay) * jnp.dot(grad.T, grad, precision=high)
    update = jnp.dot(jnp.dot(left_root, grad, precision=high), right_root_t.T, precision=high)
    return (weight - shampoo_rate * update, left_new, right_new)

def reference(inputs, cotangent, member_mask, members, first_moment, second_moment, first_weight, second_weight, first_left, first_right, second_left, second_right, first_left_root, first_right_root, second_left_root, second_right_root):
    block_objects = math.gcd(OBJECTS, 128)
    blocks = OBJECTS // block_objects
    rows_block = block_objects * K
    all_values = inputs.astype(jnp.float32).T.reshape(blocks, rows_block, D)
    all_cots = cotangent.astype(jnp.float32).T.reshape(blocks, rows_block, D)
    all_masks = member_mask.astype(jnp.float32).reshape(blocks, rows_block, 1)

    def step(carry, block):
        values, cots, weights_row = block
        outputs, pull = jax.vjp(forward, values, members, first_weight, second_weight)
        grad_out = cots * weights_row
        grad_x, grad_mem, grad_first, grad_second = pull((grad_out, jnp.zeros_like(values)))
        sums = jnp.stack([jnp.sum(weights_row * values * values), jnp.sum(weights_row * outputs[1] * outputs[1]), jnp.sum(weights_row)])
        updated = (carry[0] + grad_first, carry[1] + grad_second, carry[2] + grad_mem, carry[3] + sums)
        return (updated, (outputs[0].astype(jnp.bfloat16), grad_x.astype(jnp.bfloat16)))
    start = (jnp.zeros((D, D), jnp.float32), jnp.zeros((D, D), jnp.float32), jnp.zeros((6, K, D), jnp.float32), jnp.zeros((3,), jnp.float32))
    final, (logit_blocks, grad_blocks) = lax.scan(step, start, (all_values, all_cots, all_masks))
    logits = logit_blocks.reshape(ROWS, D).T
    input_grad = grad_blocks.reshape(ROWS, D).T
    sums = final[3]
    rms_stats = jnp.sqrt(jnp.stack([sums[0], sums[1]]) / (sums[2] * D))
    grad_vec = final[2]
    moment_one = beta_first * first_moment + (1.0 - beta_first) * grad_vec
    moment_two = beta_second * second_moment + (1.0 - beta_second) * grad_vec * grad_vec
    corr_one = 1.0 - beta_first ** STEP
    corr_two = 1.0 - beta_second ** STEP
    members_new = members - adam_rate * (moment_one / corr_one) / (jnp.sqrt(moment_two / corr_two) + adam_eps)
    first_new, first_left_new, first_right_new = precondition(final[0], first_left, first_right, first_left_root, first_right_root, first_weight)
    second_new, second_left_new, second_right_new = precondition(final[1], second_left, second_right, second_left_root, second_right_root, second_weight)
    return (logits, input_grad, rms_stats, final[0], first_new, first_left_new, first_right_new, final[1], second_new, second_left_new, second_right_new, moment_one, moment_two, members_new)
```

```python
import functools

import jax
import jax.numpy as jnp
from jax import lax
from jax.experimental import pallas as pl
from jax.experimental.pallas import tpu as pltpu
from jax.sharding import PartitionSpec as P

K = 32
STEP = 10
LANES = 128
CHUNK = 256
ROWS = 32
AHEAD = 2

beta_first = 0.9
beta_second = 0.999
adam_eps = 1e-08
adam_rate = 0.2
stat_decay = 0.95
shampoo_rate = 1.0
curve_a = 0.7978845608028654
curve_b = 0.044715

MESH = pl.DeviceIdType.MESH
F32 = jnp.float32
BF16 = jnp.bfloat16
over_lanes = (((1,), (1,)), ((), ()))


def flip(index, mask):
    bit = 1
    while bit <= mask:
        if mask & bit:
            index = index + bit - 2 * bit * ((index // bit) % 2)
        bit *= 2
    return index


def mm(a, b):
    return jnp.dot(a, b, preferred_element_type=F32)


def mm_t(a, b, precision=None):
    return lax.dot_general(a, b, over_lanes, precision=precision, preferred_element_type=F32)


def multiple(value, by):
    return pl.multiple_of(value, by)


def kernel(
    N,
    M,
    x_hbm,
    cot_hbm,
    mask_hbm,
    mem_hbm,
    m1_hbm,
    m2_hbm,
    w1_hbm,
    w2_hbm,
    l1_hbm,
    r1_hbm,
    l2_hbm,
    r2_hbm,
    p1_hbm,
    q1_hbm,
    p2_hbm,
    q2_hbm,
    logits_hbm,
    igrad_hbm,
    rms_ref,
    g1_out,
    w1_out,
    l1_out,
    r1_out,
    g2_out,
    w2_out,
    l2_out,
    r2_out,
    m1_out,
    m2_out,
    mem_out,
    mask_v,
    mem_v,
    m1_v,
    m2_v,
    w1_v,
    w2_v,
    l1_v,
    r1_v,
    l2_v,
    r2_v,
    p1_v,
    q1_v,
    p2_v,
    q2_v,
    xb,
    cb,
    lgb,
    igb,
    wb,
    tb,
    w1,
    w1t,
    w2,
    w2t,
    tab,
    stage,
    mk,
    hp,
    hid,
    dgm,
    prod,
    sc,
    hi,
    gp,
    gpre,
    g1,
    g2t,
    vec,
    vt,
    stat,
    gb,
    rcore,
    rxy,
    rz,
    ga,
    g1f,
    g1ft,
    g2f,
    g2ft,
    local_sem,
    in_send,
    x_recv,
    c_recv,
    own_sem,
    out_send,
    out_own,
    out_recv,
    wz_send,
    wz_recv,
    wx_send,
    wx_recv,
    wc_send,
    wc_recv,
    gc_send,
    gc_recv,
    gx_send,
    gx_recv,
    gz_send,
    gz_recv,
    az_send,
    az_recv,
    ax_send,
    ax_recv,
    ac_send,
    ac_recv,
):
    F, R = x_hbm.shape
    D = F * M
    Q = N // 2
    mine = R // M
    w = min(CHUNK, mine)
    C = mine // w
    tiles = w // LANES
    kb = K // N
    dr = D // N
    tr = tb.shape[3]
    pr = gb.shape[3]
    blocks = D // ROWS
    high = lax.Precision.HIGHEST

    d, m = lax.axis_index("dp"), lax.axis_index("mp")
    c, q = d % 2, d // 2

    def z_peer(o):
        return (d, flip(m, o))

    def xy_peer(o):
        return (flip(q, o) * 2 + c, m)

    core_peer = (flip(d, 1), m)
    z_order = sorted(range(1, M), reverse=True)
    xy_order = sorted(range(1, Q), reverse=True)

    def remote(src, dst, send, recv, peer):
        return pltpu.make_async_remote_copy(
            src_ref=src, dst_ref=dst, send_sem=send, recv_sem=recv, device_id=peer, device_id_type=MESH
        )

    pairs = (
        (mask_hbm, mask_v),
        (mem_hbm, mem_v),
        (w1_hbm, w1_v),
        (w2_hbm, w2_v),
        (m1_hbm, m1_v),
        (m2_hbm, m2_v),
        (l1_hbm, l1_v),
        (r1_hbm, r1_v),
        (l2_hbm, l2_v),
        (r2_hbm, r2_v),
        (p1_hbm, p1_v),
        (q1_hbm, q1_v),
        (p2_hbm, p2_v),
        (q2_hbm, q2_v),
    )
    loads = [pltpu.make_async_copy(a, b, local_sem.at[i]) for i, (a, b) in enumerate(pairs)]
    for load in loads:
        load.start()

    with jax.named_scope("barrier"):
        entry = pltpu.get_barrier_semaphore()
        peers = [z_peer(o) for o in z_order] + [xy_peer(o) for o in xy_order] + [core_peer]
        for peer in peers:
            pl.semaphore_signal(entry, inc=1, device_id=peer, device_id_type=MESH)
        pl.semaphore_wait(entry, len(peers))

    def send_in(i):
        col = multiple(i * w, w)
        here = pl.ds(multiple(m * F, F), F)
        for hbm, buf, sem in ((x_hbm, xb, x_recv), (cot_hbm, cb, c_recv)):
            for o in z_order:
                to = flip(m, o)
                remote(
                    hbm.at[:, pl.ds(multiple(to * mine + i * w, w), w)],
                    buf.at[here, pl.ds(col, w)],
                    in_send,
                    sem.at[i],
                    (d, to),
                ).start()
        for hbm, buf, sem in ((x_hbm, xb, own_sem.at[0, i]), (cot_hbm, cb, own_sem.at[1, i])):
            pltpu.make_async_copy(
                hbm.at[:, pl.ds(multiple(m * mine + i * w, w), w)], buf.at[here, pl.ds(col, w)], sem
            ).start()

    others = (M - 1) * F

    def wait_in(i):
        for hbm, buf, sem, own in ((x_hbm, xb, x_recv, own_sem.at[0, i]), (cot_hbm, cb, c_recv, own_sem.at[1, i])):
            part = buf.at[pl.ds(0, others), pl.ds(0, w)]
            remote(part, part, in_send, sem.at[i], z_peer(1)).wait_recv()
            block = buf.at[pl.ds(0, F), pl.ds(0, w)]
            pltpu.make_async_copy(hbm.at[:, pl.ds(0, w)], block, own).wait()

    def send_out(kind, i):
        buf, hbm = ((lgb, logits_hbm), (igb, igrad_hbm))[kind]
        col = multiple(i * w, w)
        there = pl.ds(multiple(m * mine + i * w, w), w)
        for o in z_order:
            to = flip(m, o)
            remote(
                buf.at[pl.ds(multiple(to * F, F), F), pl.ds(col, w)],
                hbm.at[:, there],
                out_send.at[kind, i],
                out_recv.at[kind],
                (d, to),
            ).start()
        pltpu.make_async_copy(
            buf.at[pl.ds(multiple(m * F, F), F), pl.ds(col, w)], hbm.at[:, there], out_own.at[kind, i]
        ).start()

    def wait_out(kind, i):
        buf, hbm = ((lgb, logits_hbm), (igb, igrad_hbm))[kind]
        part = buf.at[pl.ds(0, others), pl.ds(0, w)]
        remote(part, part, out_send.at[kind, i], out_recv.at[kind], z_peer(1)).wait_send()
        pltpu.make_async_copy(buf.at[pl.ds(0, F), pl.ds(0, w)], hbm.at[:, pl.ds(0, w)], out_own.at[kind, i]).wait()

    for load in loads[:4]:
        load.wait()
    wb[c, q, m, 0:dr, :] = w1_v[...].astype(BF16)
    wb[c, q, m, dr : 2 * dr, :] = w2_v[...].T.astype(BF16)
    for t in range(6):
        tb[c, q, m, t * kb : (t + 1) * kb, :] = mem_v[t]

    bufs = (wb, tb)
    for o in z_order:
        for k, buf in enumerate(bufs):
            remote(buf.at[c, q, m], buf.at[c, q, m], wz_send.at[k, o], wz_recv.at[k, o], z_peer(o)).start()
    for i in range(min(AHEAD, C)):
        send_in(i)

    per_mask = LANES // K
    groups = mine // LANES
    start = multiple(m * groups * per_mask, groups * per_mask)
    mk[...] = jnp.concatenate(
        [mask_v[pl.ds(start + j, groups, stride=per_mask), :] for j in range(per_mask)], axis=1
    ).astype(F32)

    def clear(i, carry):
        rows = pl.ds(multiple(i * ROWS, ROWS), ROWS)
        g1[rows, :] = jnp.zeros((ROWS, D), F32)
        g2t[rows, :] = jnp.zeros((ROWS, D), F32)
        for t in range(6):
            vec[t, rows, :] = jnp.zeros((ROWS, LANES), F32)
        return carry

    lax.fori_loop(0, blocks, clear, 0)
    stat[...] = jnp.zeros_like(stat)

    with jax.named_scope("weights_z"):
        for o in z_order:
            for k, buf in enumerate(bufs):
                remote(buf.at[c, q, m], buf.at[c, q, flip(m, o)], wz_send.at[k, o], wz_recv.at[k, o], z_peer(o)).wait()
    with jax.named_scope("weights_xy"):
        for o in xy_order:
            for k, buf in enumerate(bufs):
                remote(buf.at[c, q], buf.at[c, q], wx_send.at[k, o], wx_recv.at[k, o], xy_peer(o)).start()
        for o in xy_order:
            for k, buf in enumerate(bufs):
                remote(buf.at[c, q], buf.at[c, flip(q, o)], wx_send.at[k, o], wx_recv.at[k, o], xy_peer(o)).wait()
    with jax.named_scope("weights_core"):
        for k, buf in enumerate(bufs):
            remote(buf.at[c], buf.at[c], wc_send.at[k], wc_recv.at[k], core_peer).start()
        for k, buf in enumerate(bufs):
            remote(buf.at[c], buf.at[1 - c], wc_send.at[k], wc_recv.at[k], core_peer).wait()

    with jax.named_scope("weights_spread"):

        def place(i, carry):
            rows = pl.ds(multiple(i * dr, dr), dr)
            for j in range(M):
                cols = slice(j * F, (j + 1) * F)
                w1[rows, cols] = wb[i % 2, i // 2, j, 0:dr, :]
                w2t[rows, cols] = wb[i % 2, i // 2, j, dr : 2 * dr, :]
            return carry

        lax.fori_loop(0, N, place, 0)

        def turn(i, carry):
            here = pl.ds(multiple(i * LANES, LANES), LANES)
            for j in range(D // LANES):
                there = slice(j * LANES, (j + 1) * LANES)
                w1t[there, here] = w1[here, there].astype(F32).T.astype(BF16)
                w2[there, here] = w2t[here, there].astype(F32).T.astype(BF16)
            return carry

        lax.fori_loop(0, D // LANES, turn, 0)
        for t in range(6):
            for i in range(N):
                for j in range(M):
                    stage[t, i * kb : (i + 1) * kb, j * F : (j + 1) * F] = tb[
                        i % 2, i // 2, j, t * kb : (t + 1) * kb, :
                    ]

        def table(t, carry):
            for j in range(D // LANES):
                cols = slice(j * LANES, (j + 1) * LANES)
                piece = stage[t, :, cols]
                tab[t, cols, :] = jnp.concatenate([piece] * per_mask, axis=0).T
            return carry

        lax.fori_loop(0, 6, table, 0)

    def eight(value):
        return value.reshape(ROWS // 8, 8, LANES).sum(0)

    def work(i, carry):
        col = multiple(i * w, w)
        with jax.named_scope("wait_in"):
            wait_in(i)

        @pl.when(i + AHEAD < C)
        def _():
            send_in(i + AHEAD)

        first_out = max(C - 2, 0)

        @pl.when(i >= first_out)
        def _():
            for kind in range(2):
                send_out(kind, i - first_out)

        masks = [mk[pl.ds(i * tiles + j, 1), :] for j in range(tiles)]

        def place_of(r):
            return pl.ds(multiple(r * ROWS, ROWS), ROWS)

        def lanes_of(j):
            return pl.ds(multiple(col + j * LANES, LANES), LANES)

        def scale_rows(r, sums):
            rows = place_of(r)
            row_in = tab[0, rows, :]
            new = []
            for j in range(tiles):
                x = xb[rows, lanes_of(j)].astype(F32)
                sc[rows, j * LANES : (j + 1) * LANES] = (x * row_in).astype(BF16)
                new.append(sums[j] + eight(x * x))
            return tuple(new)

        zero = tuple(jnp.zeros((8, LANES), F32) for _ in range(tiles))
        with jax.named_scope("scale"):
            x_sums = lax.fori_loop(0, blocks, scale_rows, zero)
        with jax.named_scope("mm_one"):
            hp[...] = mm(w1t[...], sc[...])

        def curve_rows(r, carry):
            rows = place_of(r)
            gain, bias, row_mid = tab[1, rows, :], tab[2, rows, :], tab[3, rows, :]
            for j in range(tiles):
                cols = slice(j * LANES, (j + 1) * LANES)
                s = hp[rows, cols] * gain + bias
                s2 = s * s
                th = jnp.tanh(curve_a * (s + curve_b * (s2 * s)))
                cdf = 0.5 * (1.0 + th)
                h = s * cdf
                slope = cdf + (0.5 * s) * (1.0 - th * th) * (curve_a + (3.0 * curve_a * curve_b) * s2)
                hid[rows, cols] = h
                dgm[rows, cols] = slope * row_mid
                hi[rows, cols] = (h * row_mid).astype(BF16)
            return carry

        with jax.named_scope("curve"):
            lax.fori_loop(0, blocks, curve_rows, 0)
        with jax.named_scope("mm_two"):
            prod[...] = mm(w2t[...], hi[...])

        def out_rows(r, sums):
            rows = place_of(r)
            gain, bias = tab[4, rows, :], tab[5, rows, :]
            v4, v5 = vec[4, rows, :], vec[5, rows, :]
            new = []
            for j in range(tiles):
                cols = slice(j * LANES, (j + 1) * LANES)
                x = xb[rows, lanes_of(j)].astype(F32)
                projected = prod[rows, cols]
                branch = projected * gain + bias
                lgb[rows, lanes_of(j)] = (x + branch).astype(BF16)
                new.append(sums[j] + eight(branch * branch))
                go = cb[rows, lanes_of(j)].astype(F32) * masks[j]
                v5 = v5 + go
                v4 = v4 + go * projected
                gp[rows, cols] = (go * gain).astype(BF16)
            vec[4, rows, :] = v4
            vec[5, rows, :] = v5
            return tuple(new)

        with jax.named_scope("out"):
            b_sums = lax.fori_loop(0, blocks, out_rows, zero)
        for j in range(tiles):
            stat[0:8, :] += x_sums[j] * masks[j]
            stat[8:16, :] += b_sums[j] * masks[j]

        with jax.named_scope("mm_three"):
            half = D // 2
            for k in range(2):
                part = slice(k * half, (k + 1) * half)
                g2t[part, :] += mm_t(gp[part, :], hi[...])
            prod[...] = mm(w2[...], gp[...])

        def back_rows(r, carry):
            rows = place_of(r)
            gain = tab[1, rows, :]
            v1, v2, v3 = vec[1, rows, :], vec[2, rows, :], vec[3, rows, :]
            for j in range(tiles):
                cols = slice(j * LANES, (j + 1) * LANES)
                gh = prod[rows, cols]
                v3 = v3 + gh * hid[rows, cols]
                gs = gh * dgm[rows, cols]
                v2 = v2 + gs
                v1 = v1 + gs * hp[rows, cols]
                gpre[rows, cols] = (gs * gain).astype(BF16)
            vec[1, rows, :] = v1
            vec[2, rows, :] = v2
            vec[3, rows, :] = v3
            return carry

        with jax.named_scope("back"):
            lax.fori_loop(0, blocks, back_rows, 0)
        with jax.named_scope("mm_four"):
            for k in range(2):
                part = slice(k * half, (k + 1) * half)
                g1[part, :] += mm_t(sc[part, :], gpre[...])
            prod[...] = mm(w1[...], gpre[...])

        def in_rows(r, carry):
            rows = place_of(r)
            row_in = tab[0, rows, :]
            v0 = vec[0, rows, :]
            for j in range(tiles):
                cols = slice(j * LANES, (j + 1) * LANES)
                gs = prod[rows, cols]
                v0 = v0 + gs * xb[rows, lanes_of(j)].astype(F32)
                go = cb[rows, lanes_of(j)].astype(F32) * masks[j]
                igb[rows, lanes_of(j)] = (gs * row_in + go).astype(BF16)
            vec[0, rows, :] = v0
            return carry

        with jax.named_scope("in"):
            lax.fori_loop(0, blocks, in_rows, 0)
        return carry

    lax.fori_loop(0, C, work, 0)

    items = [(kind, i) for i in range(C) for kind in range(2)]
    already = 2 * min(C, 2)
    state = {"sent": already, "done": 0}

    def pump(count=1):
        with jax.named_scope("pump"):
            for _ in range(count):
                if state["sent"] < len(items):
                    wait_out(*items[state["done"]])
                    state["done"] += 1
                    send_out(*items[state["sent"]])
                    state["sent"] += 1

    with jax.named_scope("pack"):

        def pack_g(i, carry):
            rows = pl.ds(multiple(i * dr, dr), dr)
            for j in range(M):
                cols = slice(j * F, (j + 1) * F)
                gb[i % 2, i // 2, j, 0:dr, :] = g1[rows, cols]
                gb[i % 2, i // 2, j, dr : 2 * dr, :] = g2t[rows, cols]
            return carry

        lax.fori_loop(0, N, pack_g, 0)

        def fold(t, carry):
            for j in range(D // LANES):
                cols = slice(j * LANES, (j + 1) * LANES)
                turned = vec[t, cols, :].T
                vt[t, :, cols] = sum(turned[k * K : (k + 1) * K, :] for k in range(per_mask))
            return carry

        lax.fori_loop(0, 6, fold, 0)
        for t in range(6):
            for i in range(N):
                for j in range(M):
                    row = 2 * dr + t * kb
                    gb[i % 2, i // 2, j, row : row + kb, :] = vt[t, i * kb : (i + 1) * kb, j * F : (j + 1) * F]
        totals = [stat[0:8, :], stat[8:16, :], jnp.pad(mk[...], ((0, -groups % 8), (0, 0)))]
        rows8 = [jnp.sum(v, keepdims=True).reshape(1, 1) for v in totals]
        row_id = lax.broadcasted_iota(jnp.int32, (8, F), 0)
        lines = sum(jnp.where(row_id == k, v, 0.0) for k, v in enumerate(rows8))

        def put(i, carry):
            for j in range(M):
                gb[i % 2, i // 2, j, 2 * dr + tr : pr, :] = lines
            return carry

        lax.fori_loop(0, N, put, 0)

    pump()
    with jax.named_scope("sum_core"):
        for o in xy_order + [0]:
            k = flip(q, o)
            remote(gb.at[1 - c, k], rcore.at[k], gc_send.at[o], gc_recv.at[o], core_peer).start()

        def add_core(k):
            def step(j, carry):
                gb[c, k, j] += rcore[k, j]
                return carry

            lax.fori_loop(0, M, step, 0)

        for o in xy_order + [0]:
            k = flip(q, o)
            remote(gb.at[1 - c, k], rcore.at[k], gc_send.at[o], gc_recv.at[o], core_peer).wait()
            add_core(k)
            if o:
                remote(gb.at[c, k], rxy.at[o], gx_send.at[o], gx_recv.at[o], xy_peer(o)).start()
    pump(2)
    with jax.named_scope("sum_xy"):
        for o in xy_order:
            k = flip(q, o)
            remote(gb.at[c, k], rxy.at[o], gx_send.at[o], gx_recv.at[o], xy_peer(o)).wait()

            def step(j, carry):
                gb[c, q, j] += rxy[o, j]
                return carry

            lax.fori_loop(0, M, step, 0)
    with jax.named_scope("sum_z"):
        for o in z_order:
            remote(gb.at[c, q, flip(m, o)], rz.at[o], gz_send.at[o], gz_recv.at[o], z_peer(o)).start()
        pump(2)
        for o in z_order:
            remote(gb.at[c, q, flip(m, o)], rz.at[o], gz_send.at[o], gz_recv.at[o], z_peer(o)).wait()
            gb[c, q, m] += rz[o]

    total = gb[c, q, m]
    ga[c, q, m] = total[0 : 2 * dr, :].astype(BF16)
    with jax.named_scope("spread_z"):
        for o in z_order:
            remote(ga.at[c, q, m], ga.at[c, q, m], az_send.at[o], az_recv.at[o], z_peer(o)).start()
        for load in loads[4:]:
            load.wait()
        g1_out[...] = total[0:dr, :]
        g2_out[...] = total[dr : 2 * dr, :].T
        corr_one = 1.0 - beta_first**STEP
        corr_two = 1.0 - beta_second**STEP
        for t in range(6):
            row = 2 * dr + t * kb
            grad = total[row : row + kb, :]
            one = beta_first * m1_v[t] + (1.0 - beta_first) * grad
            two = beta_second * m2_v[t] + (1.0 - beta_second) * grad * grad
            m1_out[t] = one
            m2_out[t] = two
            mem_out[t] = mem_v[t] - adam_rate * (one / corr_one) / (jnp.sqrt(two / corr_two) + adam_eps)
        row = 2 * dr + tr
        count = total[row + 2 : row + 3, 0:1] * D
        rms_ref[:, 0:1] = jnp.sqrt(total[row : row + 1, 0:1] / count)
        rms_ref[:, 1:2] = jnp.sqrt(total[row + 1 : row + 2, 0:1] / count)
        pump(2)
        for o in z_order:
            remote(ga.at[c, q, m], ga.at[c, q, flip(m, o)], az_send.at[o], az_recv.at[o], z_peer(o)).wait()
    with jax.named_scope("spread_xy"):
        for o in xy_order:
            remote(ga.at[c, q], ga.at[c, q], ax_send.at[o], ax_recv.at[o], xy_peer(o)).start()
        pump(1)
        for o in xy_order:
            remote(ga.at[c, q], ga.at[c, flip(q, o)], ax_send.at[o], ax_recv.at[o], xy_peer(o)).wait()
    with jax.named_scope("spread_core"):
        remote(ga.at[c], ga.at[c], ac_send, ac_recv, core_peer).start()
        remote(ga.at[c], ga.at[1 - c], ac_send, ac_recv, core_peer).wait()
    pump(1)

    with jax.named_scope("shampoo"):

        def place_g(i, carry):
            rows = pl.ds(multiple(i * dr, dr), dr)
            for j in range(M):
                cols = slice(j * F, (j + 1) * F)
                g1f[rows, cols] = ga[i % 2, i // 2, j, 0:dr, :]
                g2ft[rows, cols] = ga[i % 2, i // 2, j, dr : 2 * dr, :]
            return carry

        lax.fori_loop(0, N, place_g, 0)

        def turn_g(i, carry):
            here = pl.ds(multiple(i * LANES, LANES), LANES)
            for j in range(D // LANES):
                there = slice(j * LANES, (j + 1) * LANES)
                g1ft[there, here] = g1f[here, there].astype(F32).T.astype(BF16)
                g2f[there, here] = g2ft[here, there].astype(F32).T.astype(BF16)
            return carry

        lax.fori_loop(0, D // LANES, turn_g, 0)
        by_d = pl.ds(multiple(d * dr, dr), dr)
        by_m = pl.ds(multiple(m * F, F), F)

        def renewed(old, fresh):
            return stat_decay * old + (1.0 - stat_decay) * fresh

        l1_out[...] = renewed(l1_v[...], mm_t(g1f[by_d, :], g1f[by_m, :]))
        r1_out[...] = renewed(r1_v[...], mm_t(g1ft[by_d, :], g1ft[by_m, :]))
        l2_out[...] = renewed(l2_v[...], mm_t(g2f[by_m, :], g2f[by_d, :]))
        r2_out[...] = renewed(r2_v[...], mm_t(g2ft[by_m, :], g2ft[by_d, :]))

        def stepped(weight, left, grad_t, right):
            first = mm_t(left[...], grad_t[...].astype(F32), high)
            return weight[...] - shampoo_rate * mm_t(first, right[...], high)

        w1_out[...] = stepped(w1_v, p1_v, g1ft, q1_v)
        pump(1)
        w2_out[...] = stepped(w2_v, p2_v, g2ft, q2_v)

    with jax.named_scope("drain"):
        pump(len(items))
        while state["done"] < len(items):
            wait_out(*items[state["done"]])
            state["done"] += 1
        for kind, (buf, hbm) in enumerate(((lgb, logits_hbm), (igb, igrad_hbm))):
            part = hbm.at[:, pl.ds(0, (M - 1) * mine)]
            remote(part, part, in_send, out_recv.at[kind], z_peer(1)).wait_recv()
        for buf in (xb, cb):
            part = buf.at[pl.ds(0, others), pl.ds(0, mine)]
            remote(part, part, in_send, out_recv.at[0], z_peer(1)).wait_send()


def solution(mesh):
    N, M = mesh.shape["dp"], mesh.shape["mp"]
    Q = N // 2

    def on_device(*args):
        x, cot, mask, members, m1, m2, w1, w2, l1, r1, l2, r2, p1, q1, p2, q2 = args
        F, R = x.shape
        D = F * M
        mine = R // M
        w = min(CHUNK, mine)
        C = mine // w
        kb = members.shape[1]
        dr = w1.shape[0]
        tr = -(-6 * kb // 8) * 8
        pr = 2 * dr + tr + 8
        S = jax.ShapeDtypeStruct
        V = pltpu.VMEM
        dma = pltpu.SemaphoreType.DMA
        outs = [S(x.shape, BF16), S(x.shape, BF16), S((1, 2), F32)]
        outs += [S(a.shape, F32) for a in (w1, w1, l1, r1, w2, w2, l2, r2, m1, m2, members)]
        scratch = [V(a.shape, a.dtype) for a in (mask, members, m1, m2, w1, w2, l1, r1, l2, r2, p1, q1, p2, q2)]
        scratch += [V((D, mine), BF16)] * 4
        scratch += [V((2, Q, M, 2 * dr, F), BF16), V((2, Q, M, tr, F), F32)]
        scratch += [V((D, D), BF16)] * 4
        scratch += [V((6, D, LANES), F32), V((6, K, D), F32), V((mine // LANES, LANES), F32)]
        scratch += [V((D, w), F32)] * 4
        scratch += [V((D, w), BF16)] * 4
        scratch += [V((D, D), F32)] * 2
        scratch += [V((6, D, LANES), F32), V((6, K, D), F32), V((16, LANES), F32)]
        scratch += [V((2, Q, M, pr, F), F32), V((Q, M, pr, F), F32), V((Q, M, pr, F), F32), V((M, pr, F), F32)]
        scratch += [V((2, Q, M, 2 * dr, F), BF16)]
        scratch += [V((D, D), BF16)] * 4
        scratch += [dma((14,)), dma, dma((C,)), dma((C,)), dma((2, C)), dma((2, C)), dma((2, C)), dma((2,))]
        scratch += [dma((2, M)), dma((2, M)), dma((2, Q)), dma((2, Q)), dma((2,)), dma((2,))]
        scratch += [dma((Q,)), dma((Q,)), dma((Q,)), dma((Q,)), dma((M,)), dma((M,))]
        scratch += [dma((M,)), dma((M,)), dma((Q,)), dma((Q,)), dma, dma]
        hbm = pl.BlockSpec(memory_space=pl.ANY)
        vmem = pl.BlockSpec(memory_space=pltpu.VMEM)
        res = pl.pallas_call(
            functools.partial(kernel, N, M),
            out_shape=outs,
            in_specs=[hbm] * 16,
            out_specs=[hbm] * 2 + [vmem] * 12,
            scratch_shapes=scratch,
            compiler_params=pltpu.CompilerParams(
                collective_id=0, has_side_effects=True, vmem_limit_bytes=56 << 20
            ),
            name="block",
        )(*args)
        return (res[0], res[1], res[2].reshape(2), *res[3:])

    placed = (
        P("mp", "dp"),
        P("mp", "dp"),
        P("dp", None),
        P(None, "dp", "mp"),
        P(None, "dp", "mp"),
        P(None, "dp", "mp"),
        P("dp", "mp"),
        P("mp", "dp"),
        P("dp", "mp"),
        P("dp", "mp"),
        P("mp", "dp"),
        P("mp", "dp"),
        P("dp", None),
        P("mp", None),
        P("mp", None),
        P("dp", None),
    )
    return jax.shard_map(
        on_device,
        mesh=mesh,
        in_specs=placed,
        out_specs=(
            P("mp", "dp"),
            P("mp", "dp"),
            P(),
            P("dp", "mp"),
            P("dp", "mp"),
            P("dp", "mp"),
            P("dp", "mp"),
            P("mp", "dp"),
            P("mp", "dp"),
            P("mp", "dp"),
            P("mp", "dp"),
            P(None, "dp", "mp"),
            P(None, "dp", "mp"),
            P(None, "dp", "mp"),
        ),
        check_vma=False,
    )
```

```python
import functools

import jax
import jax.numpy as jnp
from jax import lax
from jax.experimental import pallas as pl
from jax.experimental.pallas import tpu as pltpu
from jax.sharding import PartitionSpec as P

K = 32
STEP = 10
LANES = 128
CHUNK = 256
ROWS = 32
AHEAD = 3

beta_first = 0.9
beta_second = 0.999
adam_eps = 1e-08
adam_rate = 0.2
stat_decay = 0.95
shampoo_rate = 1.0
curve_a = 0.7978845608028654
curve_b = 0.044715

MESH = pl.DeviceIdType.MESH
F32 = jnp.float32
BF16 = jnp.bfloat16
over_lanes = (((1,), (1,)), ((), ()))


def flip(index, mask):
    bit = 1
    while bit <= mask:
        if mask & bit:
            index = index + bit - 2 * bit * ((index // bit) % 2)
        bit *= 2
    return index


def mm(a, b):
    return jnp.dot(a, b, preferred_element_type=F32)


def mm_t(a, b, precision=None):
    return lax.dot_general(a, b, over_lanes, precision=precision, preferred_element_type=F32)


def multiple(value, by):
    return pl.multiple_of(value, by)


def kernel(
    N,
    M,
    x_hbm,
    cot_hbm,
    mask_hbm,
    mem_hbm,
    m1_hbm,
    m2_hbm,
    w1_hbm,
    w2_hbm,
    l1_hbm,
    r1_hbm,
    l2_hbm,
    r2_hbm,
    p1_hbm,
    q1_hbm,
    p2_hbm,
    q2_hbm,
    lg_out,
    ig_out,
    sums_out,
    g1_out,
    w1_out,
    l1_out,
    r1_out,
    g2_out,
    w2_out,
    l2_out,
    r2_out,
    m1_out,
    m2_out,
    mem_out,
    mask_v,
    mem_v,
    m1_v,
    m2_v,
    w1_v,
    w2_v,
    l1_v,
    r1_v,
    l2_v,
    r2_v,
    p1_v,
    q1_v,
    p2_v,
    q2_v,
    xb,
    cb,
    lgb,
    igb,
    wb,
    tb,
    w1,
    w1t,
    w2,
    w2t,
    tab,
    stage,
    mt,
    mk,
    hp,
    hid,
    dgm,
    prod,
    sc,
    hi,
    gp,
    gpre,
    g1,
    g2t,
    vec,
    vt,
    stat,
    gb,
    rcore,
    rxy,
    rzg,
    rzv,
    zs,
    ga,
    g1f,
    g1ft,
    g2f,
    g2ft,
    local_sem,
    in_send,
    x_recv,
    c_recv,
    own_sem,
    out_send,
    out_own,
    out_recv,
    wz_send,
    wz_recv,
    wx_send,
    wx_recv,
    wc_send,
    wc_recv,
    gc_send,
    gc_recv,
    gx_send,
    gx_recv,
    gz_send,
    gz_recv,
    az_send,
    az_recv,
    ax_send,
    ax_recv,
    ac_send,
    ac_recv,
):
    F, R = x_hbm.shape
    D = F * M
    Q = N // 2
    mine = R // M
    w = min(CHUNK, mine)
    C = mine // w
    tiles = w // LANES
    kb = K // N
    dr = D // N
    tr = tb.shape[3]
    pr = gb.shape[3]
    blocks = D // ROWS
    high = lax.Precision.HIGHEST

    d, m = lax.axis_index("dp"), lax.axis_index("mp")
    c, q = d % 2, d // 2

    def z_peer(o):
        return (d, flip(m, o))

    def xy_peer(o):
        return (flip(q, o) * 2 + c, m)

    core_peer = (flip(d, 1), m)
    z_order = sorted(range(1, M), reverse=True)
    bits = [1 << k for k in range(M.bit_length() - 1)]
    xy_order = sorted(range(1, Q), reverse=True)

    def remote(src, dst, send, recv, peer):
        return pltpu.make_async_remote_copy(
            src_ref=src, dst_ref=dst, send_sem=send, recv_sem=recv, device_id=peer, device_id_type=MESH
        )

    pairs = (
        (mask_hbm, mask_v),
        (mem_hbm, mem_v),
        (w1_hbm, w1_v),
        (w2_hbm, w2_v),
        (m1_hbm, m1_v),
        (m2_hbm, m2_v),
        (l1_hbm, l1_v),
        (r1_hbm, r1_v),
        (l2_hbm, l2_v),
        (r2_hbm, r2_v),
        (p1_hbm, p1_v),
        (q1_hbm, q1_v),
        (p2_hbm, p2_v),
        (q2_hbm, q2_v),
    )
    loads = [pltpu.make_async_copy(a, b, local_sem.at[i]) for i, (a, b) in enumerate(pairs)]
    for load in loads:
        load.start()

    with jax.named_scope("barrier"):
        entry = pltpu.get_barrier_semaphore()
        peers = [z_peer(o) for o in z_order] + [xy_peer(o) for o in xy_order] + [core_peer]
        for peer in peers:
            pl.semaphore_signal(entry, inc=1, device_id=peer, device_id_type=MESH)
        pl.semaphore_wait(entry, len(peers))

    def send_in(i):
        col = multiple(i * w, w)
        here = pl.ds(multiple(m * F, F), F)
        for hbm, buf, sem in ((x_hbm, xb, x_recv), (cot_hbm, cb, c_recv)):
            for o in z_order:
                to = flip(m, o)
                remote(
                    hbm.at[:, pl.ds(multiple(to * mine + i * w, w), w)],
                    buf.at[here, pl.ds(col, w)],
                    in_send,
                    sem.at[i],
                    (d, to),
                ).start()
        for hbm, buf, sem in ((x_hbm, xb, own_sem.at[0, i]), (cot_hbm, cb, own_sem.at[1, i])):
            pltpu.make_async_copy(
                hbm.at[:, pl.ds(multiple(m * mine + i * w, w), w)], buf.at[here, pl.ds(col, w)], sem
            ).start()

    others = (M - 1) * F

    def wait_in(i):
        for hbm, buf, sem, own in ((x_hbm, xb, x_recv, own_sem.at[0, i]), (cot_hbm, cb, c_recv, own_sem.at[1, i])):
            part = buf.at[pl.ds(0, others), pl.ds(0, w)]
            remote(part, part, in_send, sem.at[i], z_peer(1)).wait_recv()
            block = buf.at[pl.ds(0, F), pl.ds(0, w)]
            pltpu.make_async_copy(hbm.at[:, pl.ds(0, w)], block, own).wait()

    def send_out(kind, i):
        buf, hbm = ((lgb, lg_out), (igb, ig_out))[kind]
        col = multiple(i * w, w)
        there = pl.ds(multiple(m * mine + i * w, w), w)
        for o in z_order:
            to = flip(m, o)
            remote(
                buf.at[pl.ds(multiple(to * F, F), F), pl.ds(col, w)],
                hbm.at[:, there],
                out_send.at[kind, i],
                out_recv.at[kind],
                (d, to),
            ).start()
        pltpu.make_async_copy(
            buf.at[pl.ds(multiple(m * F, F), F), pl.ds(col, w)], hbm.at[:, there], out_own.at[kind, i]
        ).start()

    def wait_out(kind, i):
        buf, hbm = ((lgb, lg_out), (igb, ig_out))[kind]
        part = buf.at[pl.ds(0, others), pl.ds(0, w)]
        remote(part, part, out_send.at[kind, i], out_recv.at[kind], z_peer(1)).wait_send()
        pltpu.make_async_copy(buf.at[pl.ds(0, F), pl.ds(0, w)], hbm.at[:, pl.ds(0, w)], out_own.at[kind, i]).wait()

    for load in loads[:4]:
        load.wait()
    wb[c, q, m, 0:dr, :] = w1_v[...].astype(BF16)
    wb[c, q, m, dr : 2 * dr, :] = w2_v[...].astype(BF16)
    for t in range(6):
        tb[c, q, m, t * kb : (t + 1) * kb, :] = mem_v[t]

    def spread_z(bit, bufs, send, recv):
        for h in range(0, M, 2 * bit):
            slot, back = flip(m, h), flip(m, h + bit)
            for k, buf in enumerate(bufs):
                one, two = buf.at[c, q, slot], buf.at[c, q, back]
                sems = (send.at[k, h + bit], recv.at[k, h + bit], z_peer(bit))
                yield remote(one, one, *sems), remote(one, two, *sems)

    bufs = (wb, tb)
    first = list(spread_z(bits[-1], bufs, wz_send, wz_recv))
    for go, _ in first:
        go.start()
    send_in(0)

    per_mask = LANES // K
    groups = mine // LANES
    start = multiple(m * groups * per_mask, groups * per_mask)
    mt[...] = mask_v[...].astype(F32).T
    mk[...] = jnp.concatenate([mt[pl.ds(start + j, groups, stride=per_mask), :] for j in range(per_mask)], axis=1)

    def clear(i, carry):
        rows = pl.ds(multiple(i * ROWS, ROWS), ROWS)
        g1[rows, :] = jnp.zeros((ROWS, D), F32)
        g2t[rows, :] = jnp.zeros((ROWS, D), F32)
        for t in range(6):
            vec[t, rows, :] = jnp.zeros((ROWS, LANES), F32)
        return carry

    lax.fori_loop(0, blocks, clear, 0)
    stat[...] = jnp.zeros_like(stat)

    with jax.named_scope("weights_z"):
        for bit in bits[::-1]:
            if bit != bits[-1]:
                first = list(spread_z(bit, bufs, wz_send, wz_recv))
                for go, _ in first:
                    go.start()
            if bit == bits[0]:
                for i in range(1, min(AHEAD, C)):
                    send_in(i)
            for _, come in first:
                come.wait()
    with jax.named_scope("weights_xy"):
        for o in xy_order:
            for k, buf in enumerate(bufs):
                remote(buf.at[c, q], buf.at[c, q], wx_send.at[k, o], wx_recv.at[k, o], xy_peer(o)).start()
        for o in xy_order:
            for k, buf in enumerate(bufs):
                remote(buf.at[c, q], buf.at[c, flip(q, o)], wx_send.at[k, o], wx_recv.at[k, o], xy_peer(o)).wait()
    with jax.named_scope("weights_core"):
        for k, buf in enumerate(bufs):
            remote(buf.at[c], buf.at[c], wc_send.at[k], wc_recv.at[k], core_peer).start()
        for k, buf in enumerate(bufs):
            remote(buf.at[c], buf.at[1 - c], wc_send.at[k], wc_recv.at[k], core_peer).wait()

    with jax.named_scope("weights_spread"):

        def place(i, carry):
            rows = pl.ds(multiple(i * dr, dr), dr)
            for j in range(M):
                cols = slice(j * F, (j + 1) * F)
                w1[rows, cols] = wb[i % 2, i // 2, j, 0:dr, :]
                w2t[rows, cols] = wb[i % 2, i // 2, j, dr : 2 * dr, :]
            return carry

        lax.fori_loop(0, N, place, 0)

        def turn(i, carry):
            here = pl.ds(multiple(i * LANES, LANES), LANES)
            for j in range(D // LANES):
                there = slice(j * LANES, (j + 1) * LANES)
                w1t[there, here] = w1[here, there].astype(F32).T.astype(BF16)
                w2[there, here] = w2t[here, there].astype(F32).T.astype(BF16)
            return carry

        lax.fori_loop(0, D // LANES, turn, 0)
        for t in range(6):
            for i in range(N):
                for j in range(M):
                    stage[t, i * kb : (i + 1) * kb, j * F : (j + 1) * F] = tb[
                        i % 2, i // 2, j, t * kb : (t + 1) * kb, :
                    ]

        def table(t, carry):
            for j in range(D // LANES):
                cols = slice(j * LANES, (j + 1) * LANES)
                piece = stage[t, :, cols]
                tab[t, cols, :] = jnp.concatenate([piece] * per_mask, axis=0).T
            return carry

        lax.fori_loop(0, 6, table, 0)

    def eight(value):
        return value.reshape(ROWS // 8, 8, LANES).sum(0)

    def work(i, carry):
        col = multiple(i * w, w)
        with jax.named_scope("wait_in"):
            wait_in(i)

        @pl.when(i + AHEAD < C)
        def _():
            send_in(i + AHEAD)

        first_out = max(C - 2, 0)

        @pl.when(i >= first_out)
        def _():
            for kind in range(2):
                send_out(kind, i - first_out)

        masks = [mk[pl.ds(i * tiles + j, 1), :] for j in range(tiles)]

        def place_of(r):
            return pl.ds(multiple(r * ROWS, ROWS), ROWS)

        def lanes_of(j):
            return pl.ds(multiple(col + j * LANES, LANES), LANES)

        def scale_rows(r, sums):
            rows = place_of(r)
            row_in = tab[0, rows, :]
            new = []
            for j in range(tiles):
                x = xb[rows, lanes_of(j)].astype(F32)
                sc[rows, j * LANES : (j + 1) * LANES] = (x * row_in).astype(BF16)
                new.append(sums[j] + eight(x * x))
            return tuple(new)

        zero = tuple(jnp.zeros((8, LANES), F32) for _ in range(tiles))
        with jax.named_scope("scale"):
            x_sums = lax.fori_loop(0, blocks, scale_rows, zero)
        with jax.named_scope("mm_one"):
            hp[...] = mm(w1t[...], sc[...])

        def curve_rows(r, carry):
            rows = place_of(r)
            gain, bias, row_mid = tab[1, rows, :], tab[2, rows, :], tab[3, rows, :]
            for j in range(tiles):
                cols = slice(j * LANES, (j + 1) * LANES)
                s = hp[rows, cols] * gain + bias
                s2 = s * s
                th = jnp.tanh(curve_a * (s + curve_b * (s2 * s)))
                cdf = 0.5 * (1.0 + th)
                h = s * cdf
                slope = cdf + (0.5 * s) * (1.0 - th * th) * (curve_a + (3.0 * curve_a * curve_b) * s2)
                hid[rows, cols] = h
                dgm[rows, cols] = slope * row_mid
                hi[rows, cols] = (h * row_mid).astype(BF16)
            return carry

        with jax.named_scope("curve"):
            lax.fori_loop(0, blocks, curve_rows, 0)
        with jax.named_scope("mm_two"):
            prod[...] = mm(w2t[...], hi[...])

        def out_rows(r, sums):
            rows = place_of(r)
            gain, bias = tab[4, rows, :], tab[5, rows, :]
            v4, v5 = vec[4, rows, :], vec[5, rows, :]
            new = []
            for j in range(tiles):
                cols = slice(j * LANES, (j + 1) * LANES)
                x = xb[rows, lanes_of(j)].astype(F32)
                projected = prod[rows, cols]
                branch = projected * gain + bias
                lgb[rows, lanes_of(j)] = (x + branch).astype(BF16)
                new.append(sums[j] + eight(branch * branch))
                go = cb[rows, lanes_of(j)].astype(F32) * masks[j]
                v5 = v5 + go
                v4 = v4 + go * projected
                gp[rows, cols] = (go * gain).astype(BF16)
            vec[4, rows, :] = v4
            vec[5, rows, :] = v5
            return tuple(new)

        with jax.named_scope("out"):
            b_sums = lax.fori_loop(0, blocks, out_rows, zero)
        for j in range(tiles):
            stat[0:8, :] += x_sums[j] * masks[j]
            stat[8:16, :] += b_sums[j] * masks[j]

        with jax.named_scope("mm_three"):
            half = D // 2
            for k in range(2):
                part = slice(k * half, (k + 1) * half)
                g2t[part, :] += mm_t(gp[part, :], hi[...])
            prod[...] = mm(w2[...], gp[...])

        def back_rows(r, carry):
            rows = place_of(r)
            gain = tab[1, rows, :]
            v1, v2, v3 = vec[1, rows, :], vec[2, rows, :], vec[3, rows, :]
            for j in range(tiles):
                cols = slice(j * LANES, (j + 1) * LANES)
                gh = prod[rows, cols]
                v3 = v3 + gh * hid[rows, cols]
                gs = gh * dgm[rows, cols]
                v2 = v2 + gs
                v1 = v1 + gs * hp[rows, cols]
                gpre[rows, cols] = (gs * gain).astype(BF16)
            vec[1, rows, :] = v1
            vec[2, rows, :] = v2
            vec[3, rows, :] = v3
            return carry

        with jax.named_scope("back"):
            lax.fori_loop(0, blocks, back_rows, 0)
        with jax.named_scope("mm_four"):
            for k in range(2):
                part = slice(k * half, (k + 1) * half)
                g1[part, :] += mm_t(sc[part, :], gpre[...])
            prod[...] = mm(w1[...], gpre[...])

        def in_rows(r, carry):
            rows = place_of(r)
            row_in = tab[0, rows, :]
            v0 = vec[0, rows, :]
            for j in range(tiles):
                cols = slice(j * LANES, (j + 1) * LANES)
                gs = prod[rows, cols]
                v0 = v0 + gs * xb[rows, lanes_of(j)].astype(F32)
                go = cb[rows, lanes_of(j)].astype(F32) * masks[j]
                igb[rows, lanes_of(j)] = (gs * row_in + go).astype(BF16)
            vec[0, rows, :] = v0
            return carry

        with jax.named_scope("in"):
            lax.fori_loop(0, blocks, in_rows, 0)
        return carry

    lax.fori_loop(0, C, work, 0)

    items = [(kind, i) for i in range(C) for kind in range(2)]
    already = 2 * min(C, 2)
    state = {"sent": already, "done": 0}

    def pump(count=1):
        with jax.named_scope("pump"):
            for _ in range(count):
                if state["sent"] < len(items):
                    wait_out(*items[state["done"]])
                    state["done"] += 1
                    send_out(*items[state["sent"]])
                    state["sent"] += 1

    with jax.named_scope("pack"):

        def pack_g(i, carry):
            rows = pl.ds(multiple(i * dr, dr), dr)
            for j in range(M):
                cols = slice(j * F, (j + 1) * F)
                gb[i % 2, i // 2, j, 0:dr, :] = g1[rows, cols]
                gb[i % 2, i // 2, j, dr : 2 * dr, :] = g2t[rows, cols]
            return carry

        lax.fori_loop(0, N, pack_g, 0)

        def fold(t, carry):
            for j in range(D // LANES):
                cols = slice(j * LANES, (j + 1) * LANES)
                turned = vec[t, cols, :].T
                vt[t, :, cols] = sum(turned[k * K : (k + 1) * K, :] for k in range(per_mask))
            return carry

        lax.fori_loop(0, 6, fold, 0)
        for t in range(6):
            for i in range(N):
                for j in range(M):
                    row = 2 * dr + t * kb
                    gb[i % 2, i // 2, j, row : row + kb, :] = vt[t, i * kb : (i + 1) * kb, j * F : (j + 1) * F]
        totals = [stat[0:8, :], stat[8:16, :], jnp.pad(mk[...], ((0, -groups % 8), (0, 0)))]
        rows8 = [jnp.sum(v, keepdims=True).reshape(1, 1) for v in totals]
        row_id = lax.broadcasted_iota(jnp.int32, (8, F), 0)
        lines = sum(jnp.where(row_id == k, v, 0.0) for k, v in enumerate(rows8))

        def put(i, carry):
            for j in range(M):
                gb[i % 2, i // 2, j, 2 * dr + tr : pr, :] = lines
            return carry

        lax.fori_loop(0, N, put, 0)

    pump()
    with jax.named_scope("sum_core"):
        for o in xy_order + [0]:
            k = flip(q, o)
            remote(gb.at[1 - c, k], rcore.at[k], gc_send.at[o], gc_recv.at[o], core_peer).start()

        def add_core(k):
            def step(j, carry):
                gb[c, k, j] += rcore[k, j]
                return carry

            lax.fori_loop(0, M, step, 0)

        for o in xy_order + [0]:
            k = flip(q, o)
            remote(gb.at[1 - c, k], rcore.at[k], gc_send.at[o], gc_recv.at[o], core_peer).wait()
            add_core(k)
            if o:
                remote(gb.at[c, k], rxy.at[o], gx_send.at[o], gx_recv.at[o], xy_peer(o)).start()
    pump(2)
    with jax.named_scope("sum_xy"):
        for o in xy_order:
            k = flip(q, o)
            remote(gb.at[c, k], rxy.at[o], gx_send.at[o], gx_recv.at[o], xy_peer(o)).wait()

            def step(j, carry):
                gb[c, q, j] += rxy[o, j]
                return carry

            lax.fori_loop(0, M, step, 0)
    with jax.named_scope("sum_z"):
        slot = 0
        for bit in bits:
            moves = []
            for h in range(0, M, 2 * bit):
                away = flip(m, h + bit)
                zs[slot] = gb[c, q, away, 0 : 2 * dr, :].astype(BF16)
                sems = [(gz_send.at[k, slot], gz_recv.at[k, slot], z_peer(bit)) for k in range(2)]
                tail = gb.at[c, q, away, pl.ds(2 * dr, pr - 2 * dr), :]
                moves.append((slot, h, remote(zs.at[slot], rzg.at[slot], *sems[0]), remote(tail, rzv.at[slot], *sems[1])))
                slot += 1
            for _, _, one, two in moves:
                one.start()
                two.start()
            pump()
            for k, h, one, two in moves:
                keep = flip(m, h)
                one.wait()
                two.wait()
                gb[c, q, keep, 0 : 2 * dr, :] += rzg[k].astype(F32)
                gb[c, q, keep, 2 * dr : pr, :] += rzv[k]

    total = gb[c, q, m]
    ga[c, q, m] = total[0 : 2 * dr, :].astype(BF16)
    with jax.named_scope("spread_z"):
        first = list(spread_z(bits[-1], (ga,), az_send, az_recv))
        for go, _ in first:
            go.start()
        for load in loads[4:]:
            load.wait()
        g1_out[...] = total[0:dr, :]
        g2_out[...] = total[dr : 2 * dr, :]
        corr_one = 1.0 - beta_first**STEP
        corr_two = 1.0 - beta_second**STEP
        for t in range(6):
            row = 2 * dr + t * kb
            grad = total[row : row + kb, :]
            one = beta_first * m1_v[t] + (1.0 - beta_first) * grad
            two = beta_second * m2_v[t] + (1.0 - beta_second) * grad * grad
            m1_out[t] = one
            m2_out[t] = two
            mem_out[t] = mem_v[t] - adam_rate * (one / corr_one) / (jnp.sqrt(two / corr_two) + adam_eps)
        sums_out[...] = total[2 * dr + tr : pr, 0:LANES if F >= LANES else F]
        for bit in bits[::-1]:
            if bit != bits[-1]:
                first = list(spread_z(bit, (ga,), az_send, az_recv))
                for go, _ in first:
                    go.start()
            pump()
            for _, come in first:
                come.wait()
    with jax.named_scope("spread_xy"):
        for o in xy_order:
            remote(ga.at[c, q], ga.at[c, q], ax_send.at[o], ax_recv.at[o], xy_peer(o)).start()
        pump(1)
        for o in xy_order:
            remote(ga.at[c, q], ga.at[c, flip(q, o)], ax_send.at[o], ax_recv.at[o], xy_peer(o)).wait()
    with jax.named_scope("spread_core"):
        remote(ga.at[c], ga.at[c], ac_send, ac_recv, core_peer).start()
        remote(ga.at[c], ga.at[1 - c], ac_send, ac_recv, core_peer).wait()
    pump(1)

    with jax.named_scope("shampoo"):

        def place_g(i, carry):
            rows = pl.ds(multiple(i * dr, dr), dr)
            for j in range(M):
                cols = slice(j * F, (j + 1) * F)
                g1f[rows, cols] = ga[i % 2, i // 2, j, 0:dr, :]
                g2ft[rows, cols] = ga[i % 2, i // 2, j, dr : 2 * dr, :]
            return carry

        lax.fori_loop(0, N, place_g, 0)

        def turn_g(i, carry):
            here = pl.ds(multiple(i * LANES, LANES), LANES)
            for j in range(D // LANES):
                there = slice(j * LANES, (j + 1) * LANES)
                g1ft[there, here] = g1f[here, there].astype(F32).T.astype(BF16)
                g2f[there, here] = g2ft[here, there].astype(F32).T.astype(BF16)
            return carry

        lax.fori_loop(0, D // LANES, turn_g, 0)
        by_d = pl.ds(multiple(d * dr, dr), dr)
        by_m = pl.ds(multiple(m * F, F), F)

        def renewed(old, fresh):
            return stat_decay * old + (1.0 - stat_decay) * fresh

        l1_out[...] = renewed(l1_v[...], mm_t(g1f[by_d, :], g1f[by_m, :]))
        r1_out[...] = renewed(r1_v[...], mm_t(g1ft[by_d, :], g1ft[by_m, :]))
        l2_out[...] = renewed(l2_v[...], mm_t(g2f[by_d, :], g2f[by_m, :]))
        r2_out[...] = renewed(r2_v[...], mm_t(g2ft[by_d, :], g2ft[by_m, :]))

        def stepped(weight, left, grad, right):
            inner = jnp.dot(left[...], grad[...].astype(F32), precision=high, preferred_element_type=F32)
            return weight[...] - shampoo_rate * mm_t(inner, right[...], high)

        w1_out[...] = stepped(w1_v, p1_v, g1f, q1_v)
        pump(1)
        w2_out[...] = stepped(w2_v, q2_v, g2ft, p2_v)

    with jax.named_scope("drain"):
        pump(len(items))
        while state["done"] < len(items):
            wait_out(*items[state["done"]])
            state["done"] += 1
        for kind, (buf, hbm) in enumerate(((lgb, lg_out), (igb, ig_out))):
            part = hbm.at[:, pl.ds(0, (M - 1) * mine)]
            remote(part, part, in_send, out_recv.at[kind], z_peer(1)).wait_recv()
        for buf in (xb, cb):
            part = buf.at[pl.ds(0, others), pl.ds(0, mine)]
            remote(part, part, in_send, out_recv.at[0], z_peer(1)).wait_send()


def finish(n_out, D, sums_ref, *refs):
    outs, rms_ref, sems = refs[n_out : 2 * n_out], refs[2 * n_out], refs[2 * n_out + 1]
    copies = [pltpu.make_async_copy(refs[i], outs[i], sems.at[i]) for i in range(n_out)]
    for copy in copies:
        copy.start()
    sums = sums_ref[...]
    ratio = jnp.sqrt(sums / (sums[2:3, :] * D))
    rms_ref[0] = ratio[0, 0]
    rms_ref[1] = ratio[1, 0]
    for copy in copies:
        copy.wait()


def solution(mesh):
    N, M = mesh.shape["dp"], mesh.shape["mp"]
    Q = N // 2

    def on_device(*args):
        x, cot, mask, members, m1, m2, w1, w2, l1, r1, l2, r2, p1, q1, p2, q2 = args
        mask, w2, l2, r2 = mask.T, w2.T, l2.T, r2.T
        args = (x, cot, mask, members, m1, m2, w1, w2, l1, r1, l2, r2, p1, q1, p2, q2)
        F, R = x.shape
        D = F * M
        mine = R // M
        w = min(CHUNK, mine)
        C = mine // w
        kb = members.shape[1]
        dr = w1.shape[0]
        tr = -(-6 * kb // 8) * 8
        pr = 2 * dr + tr + 8
        S = jax.ShapeDtypeStruct
        V = pltpu.VMEM
        dma = pltpu.SemaphoreType.DMA
        outs = [S(x.shape, BF16), S(x.shape, BF16), S((8, min(F, LANES)), F32)]
        outs += [S(a.shape, F32) for a in (w1, w1, l1, r1, w2, w2, l2, r2, m1, m2, members)]
        scratch = [V(a.shape, a.dtype) for a in (mask, members, m1, m2, w1, w2, l1, r1, l2, r2, p1, q1, p2, q2)]
        scratch += [V((D, mine), BF16)] * 4
        scratch += [V((2, Q, M, 2 * dr, F), BF16), V((2, Q, M, tr, F), F32)]
        scratch += [V((D, D), BF16)] * 4
        scratch += [V((6, D, LANES), F32), V((6, K, D), F32), V(mask.shape[::-1], F32), V((mine // LANES, LANES), F32)]
        scratch += [V((D, w), F32)] * 4
        scratch += [V((D, w), BF16)] * 4
        scratch += [V((D, D), F32)] * 2
        scratch += [V((6, D, LANES), F32), V((6, K, D), F32), V((16, LANES), F32)]
        scratch += [V((2, Q, M, pr, F), F32), V((Q, M, pr, F), F32), V((Q, M, pr, F), F32)]
        scratch += [V((M - 1, 2 * dr, F), BF16), V((M - 1, pr - 2 * dr, F), F32), V((M - 1, 2 * dr, F), BF16)]
        scratch += [V((2, Q, M, 2 * dr, F), BF16)]
        scratch += [V((D, D), BF16)] * 4
        scratch += [dma((14,)), dma, dma((C,)), dma((C,)), dma((2, C)), dma((2, C)), dma((2, C)), dma((2,))]
        scratch += [dma((2, M)), dma((2, M)), dma((2, Q)), dma((2, Q)), dma((2,)), dma((2,))]
        scratch += [dma((Q,)), dma((Q,)), dma((Q,)), dma((Q,)), dma((2, M)), dma((2, M))]
        scratch += [dma((1, M)), dma((1, M)), dma((Q,)), dma((Q,)), dma, dma]
        hbm = pl.BlockSpec(memory_space=pl.ANY)
        vmem = pl.BlockSpec(memory_space=pltpu.VMEM)
        res = pl.pallas_call(
            functools.partial(kernel, N, M),
            out_shape=[V(a.shape, a.dtype) for a in outs],
            in_specs=[pl.BlockSpec(memory_space=pl.ANY)] * 16,
            out_specs=[pl.BlockSpec(memory_space=pl.ANY)] * 2 + [vmem] * 12,
            scratch_shapes=scratch,
            compiler_params=pltpu.CompilerParams(
                collective_id=0, has_side_effects=True, vmem_limit_bytes=42 << 20
            ),
            name="block",
        )(*[pltpu.with_memory_space_constraint(a, pltpu.HBM) for a in args])
        kept = [*res[:2], *res[3:]]
        done = pl.pallas_call(
            functools.partial(finish, len(kept), D),
            out_shape=[S(a.shape, a.dtype) for a in kept] + [S((2,), F32)],
            in_specs=[vmem] + [pl.BlockSpec(memory_space=pl.ANY)] * len(kept),
            out_specs=[hbm] * len(kept) + [pl.BlockSpec(memory_space=pltpu.SMEM)],
            scratch_shapes=[dma((len(kept),))],
            compiler_params=pltpu.CompilerParams(vmem_limit_bytes=16 << 20),
            name="finish",
        )(res[2], *kept)
        logits, igrad, g1, n1, l1, r1, g2, n2, l2, r2, m1, m2, new, rms = done
        return (logits, igrad, rms, g1, n1, l1, r1, g2.T, n2.T, l2.T, r2.T, m1, m2, new)

    placed = (
        P("mp", "dp"),
        P("mp", "dp"),
        P("dp", None),
        P(None, "dp", "mp"),
        P(None, "dp", "mp"),
        P(None, "dp", "mp"),
        P("dp", "mp"),
        P("mp", "dp"),
        P("dp", "mp"),
        P("dp", "mp"),
        P("mp", "dp"),
        P("mp", "dp"),
        P("dp", None),
        P("mp", None),
        P("mp", None),
        P("dp", None),
    )
    return jax.shard_map(
        on_device,
        mesh=mesh,
        in_specs=placed,
        out_specs=(
            P("mp", "dp"),
            P("mp", "dp"),
            P(),
            P("dp", "mp"),
            P("dp", "mp"),
            P("dp", "mp"),
            P("dp", "mp"),
            P("mp", "dp"),
            P("mp", "dp"),
            P("mp", "dp"),
            P("mp", "dp"),
            P(None, "dp", "mp"),
            P(None, "dp", "mp"),
            P(None, "dp", "mp"),
        ),
        check_vma=False,
    )
```

```python
import functools

import jax
import jax.numpy as jnp
from jax import lax
from jax.experimental import pallas as pl
from jax.experimental.pallas import tpu as pltpu
from jax.sharding import PartitionSpec as P

K = 32
STEP = 10
LANES = 128
CHUNK = 256
ROWS = 32
AHEAD = 2
FIRST = 4
OUT = 4
LEAST = 8

beta_first = 0.9
beta_second = 0.999
adam_eps = 1e-08
adam_rate = 0.2
stat_decay = 0.95
shampoo_rate = 1.0
curve_a = 0.7978845608028654
curve_b = 0.044715

MESH = pl.DeviceIdType.MESH
F32 = jnp.float32
BF16 = jnp.bfloat16
over_lanes = (((1,), (1,)), ((), ()))


def flip(index, mask):
    bit = 1
    while bit <= mask:
        if mask & bit:
            index = index + bit - 2 * bit * ((index // bit) % 2)
        bit *= 2
    return index


def mm(a, b):
    return jnp.dot(a, b, preferred_element_type=F32)


def mm_t(a, b, precision=None):
    return lax.dot_general(a, b, over_lanes, precision=precision, preferred_element_type=F32)


def multiple(value, by):
    return pl.multiple_of(value, by)


def kernel(
    N,
    M,
    cap,
    x_hbm,
    cot_hbm,
    mask_hbm,
    mem_hbm,
    m1_hbm,
    m2_hbm,
    w1_hbm,
    w2_hbm,
    l1_hbm,
    r1_hbm,
    l2_hbm,
    r2_hbm,
    p1_hbm,
    q1_hbm,
    p2_hbm,
    q2_hbm,
    lg_out,
    ig_out,
    sums_out,
    g1_out,
    w1_out,
    l1_out,
    r1_out,
    g2_out,
    w2_out,
    l2_out,
    r2_out,
    m1_out,
    m2_out,
    mem_out,
    mask_v,
    mem_v,
    m1_v,
    m2_v,
    w1_v,
    w2_v,
    l1_v,
    r1_v,
    l2_v,
    r2_v,
    p1_v,
    q1_v,
    p2_v,
    q2_v,
    cv,
    cp,
    st,
    igr,
    xb,
    cb,
    lgb,
    igb,
    wb,
    tb,
    w1,
    w1t,
    w2,
    w2t,
    tab,
    stage,
    mt,
    mk,
    rk,
    hp,
    hid,
    dgm,
    prod,
    sc,
    hi,
    gp,
    gpre,
    cx,
    ig,
    g1,
    g2t,
    vec,
    vt,
    stat,
    gb,
    rcore,
    xs,
    rxg,
    rxv,
    rzg,
    rzv,
    zs,
    ga,
    g1f,
    g1ft,
    g2f,
    g2ft,
    local_sem,
    in_send,
    x_recv,
    c_recv,
    own_sem,
    out_send,
    out_own,
    out_recv,
    wz_send,
    wz_recv,
    wx_send,
    wx_recv,
    wc_send,
    wc_recv,
    gc_send,
    gc_recv,
    gx_send,
    gx_recv,
    gz_send,
    gz_recv,
    az_send,
    az_recv,
    ax_send,
    ax_recv,
    ac_send,
    ac_recv,
):
    F, R = x_hbm.shape
    D = F * M
    Q = N // 2
    mine = R // M
    w = min(CHUNK, mine)
    C = mine // w
    tiles = w // LANES
    packed = cap < mine
    KC = cap // w
    groups = mine // LANES
    kb = K // N
    dr = D // N
    tr = tb.shape[3]
    pr = gb.shape[3]
    blocks = D // ROWS
    high = lax.Precision.HIGHEST

    d, m = lax.axis_index("dp"), lax.axis_index("mp")
    c, q = d % 2, d // 2

    def z_peer(o):
        return (d, flip(m, o))

    def xy_peer(o):
        return (flip(q, o) * 2 + c, m)

    core_peer = (flip(d, 1), m)
    z_order = sorted(range(1, M), reverse=True)
    bits = [1 << k for k in range(M.bit_length() - 1)]
    xy_order = sorted(range(1, Q), reverse=True)

    def remote(src, dst, send, recv, peer):
        return pltpu.make_async_remote_copy(
            src_ref=src, dst_ref=dst, send_sem=send, recv_sem=recv, device_id=peer, device_id_type=MESH
        )

    pairs = (
        (mask_hbm, mask_v),
        (mem_hbm, mem_v),
        (w1_hbm, w1_v),
        (w2_hbm, w2_v),
        (m1_hbm, m1_v),
        (m2_hbm, m2_v),
        (l1_hbm, l1_v),
        (r1_hbm, r1_v),
        (l2_hbm, l2_v),
        (r2_hbm, r2_v),
        (p1_hbm, p1_v),
        (q1_hbm, q1_v),
        (p2_hbm, p2_v),
        (q2_hbm, q2_v),
    )
    if packed:
        pairs = (*pairs, (cot_hbm, cv))
    loads = [pltpu.make_async_copy(a, b, local_sem.at[i]) for i, (a, b) in enumerate(pairs)]
    for load in loads:
        load.start()

    with jax.named_scope("barrier"):
        entry = pltpu.get_barrier_semaphore()
        peers = [z_peer(o) for o in z_order] + [xy_peer(o) for o in xy_order] + [core_peer]
        for peer in peers:
            pl.semaphore_signal(entry, inc=1, device_id=peer, device_id_type=MESH)
        pl.semaphore_wait(entry, len(peers))

    kinds_in = ((xb, x_recv, 0), (cb, c_recv, 1))

    def send_in(i, kinds=(0, 1)):
        here = pl.ds(multiple(m * F, F), F)
        col = pl.ds(multiple(i * w, w), w)

        def source(kind, to):
            if kind and packed:
                return cp.at[to, :, col]
            return (x_hbm, cot_hbm)[kind].at[:, pl.ds(multiple(to * mine + i * w, w), w)]

        def start(kind):
            buf, sem, _ = kinds_in[kind]
            for o in z_order:
                to = flip(m, o)
                remote(source(kind, to), buf.at[here, col], in_send.at[kind], sem.at[i], (d, to)).start()
            pltpu.make_async_copy(source(kind, m), buf.at[here, col], own_sem.at[kind, i]).start()

        for kind in kinds:
            if kind and packed and not isinstance(i, int):
                pl.when(i < KC)(lambda: start(1))
            elif not (kind and packed) or i < KC:
                start(kind)

    others = (M - 1) * F

    def wait_in(i):
        def arrive(kind):
            buf, sem, _ = kinds_in[kind]
            part = buf.at[pl.ds(0, others), pl.ds(0, w)]
            remote(part, part, in_send.at[kind], sem.at[i], z_peer(1)).wait_recv()
            block = buf.at[pl.ds(0, F), pl.ds(0, w)]
            pltpu.make_async_copy(block, block, own_sem.at[kind, i]).wait()

        arrive(0)
        if packed:
            pl.when(i < KC)(lambda: arrive(1))
        else:
            arrive(1)

    def send_out(kind, i):
        col = pl.ds(multiple(i * w, w), w)
        if kind and packed:
            there = igr.at[m, :, col]
        else:
            there = (lg_out, ig_out)[kind].at[:, pl.ds(multiple(m * mine + i * w, w), w)]
        buf = (lgb, igb)[kind]
        for o in z_order:
            to = flip(m, o)
            recv = out_recv.at[kind, o] if kind and packed else out_recv.at[kind, 0]
            remote(
                buf.at[pl.ds(multiple(to * F, F), F), col], there, out_send.at[kind, i], recv, (d, to)
            ).start()
        if not (kind and packed):
            pltpu.make_async_copy(buf.at[pl.ds(multiple(m * F, F), F), col], there, out_own.at[kind, i]).start()

    def wait_out(kind, i):
        buf = (lgb, igb)[kind]
        part = buf.at[pl.ds(0, others), pl.ds(0, w)]
        remote(part, part, out_send.at[kind, i], out_recv.at[kind, 0], z_peer(1)).wait_send()
        if not (kind and packed):
            own = buf.at[pl.ds(0, F), pl.ds(0, w)]
            pltpu.make_async_copy(own, own, out_own.at[kind, i]).wait()

    line = lax.broadcasted_iota(jnp.int32, (w, LANES), 0).astype(F32)

    def matches(p, k, i):
        base = (k * w) * jnp.float32(1) if isinstance(k, int) else (k * w).astype(F32)
        parts = []
        for j in range(tiles):
            row = rk[pl.ds(p * groups + i * tiles + j, 1), :] - base
            parts.append(jnp.where(line == row, 1.0, 0.0).astype(BF16))
        return jnp.concatenate(parts, axis=1)

    spread_by = K // LEAST

    def pack_block(k, p):
        def step(i, acc):
            cols = pl.ds(multiple(p * mine + i * w, w), w)
            return acc + mm_t(cv[:, cols], matches(p, k, i))

        acc = lax.fori_loop(k, min(C, spread_by * k + spread_by), step, jnp.zeros((F, w), F32))
        cp[p, :, k * w : (k + 1) * w] = acc.astype(BF16)

    def pack_chunk(k):
        with jax.named_scope("pack_cot"):

            def step(p, carry):
                pack_block(k, p)
                return carry

            lax.fori_loop(0, M, step, 0)

    def unpack_block(p):
        with jax.named_scope("unpack"):

            def chunk(i, carry):
                def step(k, acc):
                    return acc + mm(igr[p, :, pl.ds(multiple(k * w, w), w)], matches(p, k, i))

                acc = lax.fori_loop(i // spread_by, jnp.minimum(i, KC - 1) + 1, step, jnp.zeros((F, w), F32))
                ig_out[:, pl.ds(multiple(p * mine + i * w, w), w)] = acc.astype(BF16)
                return carry

            lax.fori_loop(0, C, chunk, 0)

    def unpack_from(o):
        part = igr.at[0]
        remote(part, part, in_send.at[0], out_recv.at[1, o], z_peer(o)).wait_recv()
        unpack_block(flip(m, o))

    for load in loads[:4]:
        load.wait()
    wb[c, q, m, 0:dr, :] = w1_v[...].astype(BF16)
    wb[c, q, m, dr : 2 * dr, :] = w2_v[...].astype(BF16)
    for t in range(6):
        tb[c, q, m, t * kb : (t + 1) * kb, :] = mem_v[t]

    def spread_z(bit, bufs, send, recv):
        for h in range(0, M, 2 * bit):
            slot, back = flip(m, h), flip(m, h + bit)
            for k, buf in enumerate(bufs):
                one, two = buf.at[c, q, slot], buf.at[c, q, back]
                sems = (send.at[k, h + bit], recv.at[k, h + bit], z_peer(bit))
                yield remote(one, one, *sems), remote(one, two, *sems)

    bufs = (wb, tb)
    first = list(spread_z(bits[-1], bufs, wz_send, wz_recv))
    for go, _ in first:
        go.start()
    per_mask = LANES // K
    mt[...] = mask_v[...].astype(F32).T
    mk[...] = jnp.concatenate(
        [mt[pl.ds(j, M * groups, stride=per_mask), :] for j in range(per_mask)], axis=1
    )
    if packed:
        flags = mk[...]
        rows, cols = M * groups, LANES
        lower = lax.broadcasted_iota(jnp.int32, (cols, cols), 0) < lax.broadcasted_iota(jnp.int32, (cols, cols), 1)
        inside = mm(flags.astype(BF16), jnp.where(lower, 1.0, 0.0).astype(BF16))
        sums = jnp.broadcast_to(jnp.sum(flags, axis=1, keepdims=True), (rows, cols)).astype(BF16)
        one = lax.broadcasted_iota(jnp.int32, (rows, rows), 0)
        two = lax.broadcasted_iota(jnp.int32, (rows, rows), 1)
        ahead = (two < one) & (two >= one - one % groups)
        place_in = inside + mm(jnp.where(ahead, 1.0, 0.0).astype(BF16), sums)
        rk[...] = jnp.where(flags > 0.0, place_in, -1.0)
    send_in(0, (0,) if packed else (0, 1))

    def clear(i, carry):
        rows = pl.ds(multiple(i * ROWS, ROWS), ROWS)
        g1[rows, :] = jnp.zeros((ROWS, D), F32)
        g2t[rows, :] = jnp.zeros((ROWS, D), F32)
        for t in range(6):
            vec[t, rows, :] = jnp.zeros((ROWS, LANES), F32)
        return carry

    lax.fori_loop(0, blocks, clear, 0)
    stat[...] = jnp.zeros_like(stat)
    if packed:

        def clear_packed(i, carry):
            igb[pl.ds(multiple(i * ROWS, ROWS), ROWS), :] = jnp.zeros((ROWS, cap), BF16)
            return carry

        lax.fori_loop(0, blocks, clear_packed, 0)

    ahead_of = min(FIRST, C)
    if packed:
        loads[-1].wait()
        pack_chunk(0)

    def step_in(k):
        if packed:
            if k < KC:
                send_in(k, (1,))
            if k + 1 < ahead_of:
                send_in(k + 1, (0,))
            if k + 1 < KC:
                pack_chunk(k + 1)
        elif k + 1 < ahead_of:
            send_in(k + 1)

    with jax.named_scope("weights_z"):
        for bit in bits[::-1]:
            if bit != bits[-1]:
                first = list(spread_z(bit, bufs, wz_send, wz_recv))
                for go, _ in first:
                    go.start()
            if bit == bits[0]:
                step_in(0)
            for _, come in first:
                come.wait()
    with jax.named_scope("weights_xy"):
        for o in xy_order:
            for k, buf in enumerate(bufs):
                remote(buf.at[c, q], buf.at[c, q], wx_send.at[k, o], wx_recv.at[k, o], xy_peer(o)).start()
        step_in(1)
        step_in(2)
        for o in xy_order:
            for k, buf in enumerate(bufs):
                remote(buf.at[c, q], buf.at[c, flip(q, o)], wx_send.at[k, o], wx_recv.at[k, o], xy_peer(o)).wait()
    with jax.named_scope("weights_core"):
        for k, buf in enumerate(bufs):
            remote(buf.at[c], buf.at[c], wc_send.at[k], wc_recv.at[k], core_peer).start()
        for k in range(3, max(ahead_of, KC if packed else 0)):
            if k < ahead_of:
                step_in(k)
            elif k + 1 < KC:
                pack_chunk(k + 1)
        for k, buf in enumerate(bufs):
            remote(buf.at[c], buf.at[1 - c], wc_send.at[k], wc_recv.at[k], core_peer).wait()

    with jax.named_scope("weights_spread"):

        def place(i, carry):
            rows = pl.ds(multiple(i * dr, dr), dr)
            for j in range(M):
                cols = slice(j * F, (j + 1) * F)
                w1[rows, cols] = wb[i % 2, i // 2, j, 0:dr, :]
                w2t[rows, cols] = wb[i % 2, i // 2, j, dr : 2 * dr, :]
            return carry

        lax.fori_loop(0, N, place, 0)

        def turn(i, carry):
            here = pl.ds(multiple(i * LANES, LANES), LANES)
            for j in range(D // LANES):
                there = slice(j * LANES, (j + 1) * LANES)
                w1t[there, here] = w1[here, there].astype(F32).T.astype(BF16)
                w2[there, here] = w2t[here, there].astype(F32).T.astype(BF16)
            return carry

        lax.fori_loop(0, D // LANES, turn, 0)
        for t in range(6):
            for i in range(N):
                for j in range(M):
                    stage[t, i * kb : (i + 1) * kb, j * F : (j + 1) * F] = tb[
                        i % 2, i // 2, j, t * kb : (t + 1) * kb, :
                    ]

        def table(t, carry):
            for j in range(D // LANES):
                cols = slice(j * LANES, (j + 1) * LANES)
                piece = stage[t, :, cols]
                tab[t, cols, :] = jnp.concatenate([piece] * per_mask, axis=0).T
            return carry

        lax.fori_loop(0, 6, table, 0)

    def eight(value):
        return value.reshape(ROWS // 8, 8, LANES).sum(0)

    if packed:
        early = [(C - 3, [(0, 0)]), (C - 2, [(0, 1)]), (C - 1, [(0, 2)])]
    else:
        early = [(C - 2, [(0, 0), (1, 0)]), (C - 1, [(0, 1), (1, 1)])]

    def work(i, carry):
        col = multiple(i * w, w)
        with jax.named_scope("wait_in"):
            wait_in(i)

        @pl.when((i + AHEAD >= FIRST) & (i + AHEAD < C))
        def _():
            send_in(i + AHEAD)

        for late, parts in early:
            for kind, k in parts:
                pl.when(i == late)(functools.partial(send_out, kind, k))

        masks = [mk[pl.ds(m * groups + i * tiles + j, 1), :] for j in range(tiles)]

        def place_of(r):
            return pl.ds(multiple(r * ROWS, ROWS), ROWS)

        def lanes_of(j):
            return pl.ds(multiple(col + j * LANES, LANES), LANES)

        def scale_rows(r, sums):
            rows = place_of(r)
            row_in = tab[0, rows, :]
            new = []
            for j in range(tiles):
                x = xb[rows, lanes_of(j)].astype(F32)
                sc[rows, j * LANES : (j + 1) * LANES] = (x * row_in).astype(BF16)
                new.append(sums[j] + eight(x * x))
            return tuple(new)

        zero = tuple(jnp.zeros((8, LANES), F32) for _ in range(tiles))
        with jax.named_scope("scale"):
            x_sums = lax.fori_loop(0, blocks, scale_rows, zero)
        with jax.named_scope("mm_one"):
            hp[...] = mm(w1t[...], sc[...])

        def curve_rows(r, carry):
            rows = place_of(r)
            gain, bias, row_mid = tab[1, rows, :], tab[2, rows, :], tab[3, rows, :]
            for j in range(tiles):
                cols = slice(j * LANES, (j + 1) * LANES)
                s = hp[rows, cols] * gain + bias
                s2 = s * s
                th = jnp.tanh(curve_a * (s + curve_b * (s2 * s)))
                cdf = 0.5 * (1.0 + th)
                h = s * cdf
                slope = cdf + (0.5 * s) * (1.0 - th * th) * (curve_a + (3.0 * curve_a * curve_b) * s2)
                hid[rows, cols] = h
                dgm[rows, cols] = slope * row_mid
                hi[rows, cols] = (h * row_mid).astype(BF16)
            return carry

        with jax.named_scope("curve"):
            lax.fori_loop(0, blocks, curve_rows, 0)
        with jax.named_scope("mm_two"):
            prod[...] = mm(w2t[...], hi[...])
        low, high_k = i // spread_by, jnp.minimum(i, KC - 1)
        if packed:
            with jax.named_scope("expand"):

                def grow(k, carry):
                    st[k] = matches(m, k, i)
                    cx[...] += mm(cb[:, pl.ds(multiple(k * w, w), w)], st[k])
                    return carry

                cx[...] = jnp.zeros_like(cx)
                lax.fori_loop(low, high_k + 1, grow, 0)

        def grad_of(rows, j):
            if packed:
                return cx[rows, j * LANES : (j + 1) * LANES]
            return cb[rows, lanes_of(j)].astype(F32) * masks[j]


        def out_rows(r, sums):
            rows = place_of(r)
            gain, bias = tab[4, rows, :], tab[5, rows, :]
            v4, v5 = vec[4, rows, :], vec[5, rows, :]
            new = []
            for j in range(tiles):
                cols = slice(j * LANES, (j + 1) * LANES)
                x = xb[rows, lanes_of(j)].astype(F32)
                projected = prod[rows, cols]
                branch = projected * gain + bias
                lgb[rows, lanes_of(j)] = (x + branch).astype(BF16)
                new.append(sums[j] + eight(branch * branch))
                go = grad_of(rows, j)
                v5 = v5 + go
                v4 = v4 + go * projected
                gp[rows, cols] = (go * gain).astype(BF16)
            vec[4, rows, :] = v4
            vec[5, rows, :] = v5
            return tuple(new)

        with jax.named_scope("out"):
            b_sums = lax.fori_loop(0, blocks, out_rows, zero)
        for j in range(tiles):
            stat[0:8, :] += x_sums[j] * masks[j]
            stat[8:16, :] += b_sums[j] * masks[j]

        with jax.named_scope("mm_three"):
            half = D // 2
            for k in range(2):
                part = slice(k * half, (k + 1) * half)
                g2t[part, :] += mm_t(gp[part, :], hi[...])
            prod[...] = mm(w2[...], gp[...])

        def back_rows(r, carry):
            rows = place_of(r)
            gain = tab[1, rows, :]
            v1, v2, v3 = vec[1, rows, :], vec[2, rows, :], vec[3, rows, :]
            for j in range(tiles):
                cols = slice(j * LANES, (j + 1) * LANES)
                gh = prod[rows, cols]
                v3 = v3 + gh * hid[rows, cols]
                gs = gh * dgm[rows, cols]
                v2 = v2 + gs
                v1 = v1 + gs * hp[rows, cols]
                gpre[rows, cols] = (gs * gain).astype(BF16)
            vec[1, rows, :] = v1
            vec[2, rows, :] = v2
            vec[3, rows, :] = v3
            return carry

        with jax.named_scope("back"):
            lax.fori_loop(0, blocks, back_rows, 0)
        with jax.named_scope("mm_four"):
            for k in range(2):
                part = slice(k * half, (k + 1) * half)
                g1[part, :] += mm_t(sc[part, :], gpre[...])
            prod[...] = mm(w1[...], gpre[...])

        def in_rows(r, carry):
            rows = place_of(r)
            row_in = tab[0, rows, :]
            v0 = vec[0, rows, :]
            for j in range(tiles):
                cols = slice(j * LANES, (j + 1) * LANES)
                gs = prod[rows, cols]
                v0 = v0 + gs * xb[rows, lanes_of(j)].astype(F32)
                go = grad_of(rows, j)
                done = (gs * row_in + go).astype(BF16)
                if packed:
                    ig[rows, cols] = done
                else:
                    igb[rows, lanes_of(j)] = done
            vec[0, rows, :] = v0
            return carry

        with jax.named_scope("in"):
            lax.fori_loop(0, blocks, in_rows, 0)
        if packed:
            ig_out[:, pl.ds(multiple(m * mine + col, w), w)] = ig[pl.ds(multiple(m * F, F), F), :]
            with jax.named_scope("shrink"):

                def shrink(k, carry):
                    cols = pl.ds(multiple(k * w, w), w)
                    igb[:, cols] = (igb[:, cols].astype(F32) + mm_t(ig[...], st[k])).astype(BF16)
                    return carry

                lax.fori_loop(low, high_k + 1, shrink, 0)
        return carry

    lax.fori_loop(0, C, work, 0)

    items = [item for _, parts in early for item in parts]
    already = len(items)
    if packed:
        items += [(1, k) for k in range(KC)] + [(0, i) for i in range(3, C)]
    else:
        items += [(kind, i) for i in range(2, C) for kind in range(2)]
    state = {"sent": already, "done": 0}

    def pump(count, most=OUT):
        with jax.named_scope("pump"):
            for _ in range(count):
                if state["sent"] < len(items):
                    while state["sent"] - state["done"] >= most:
                        wait_out(*items[state["done"]])
                        state["done"] += 1
                    send_out(*items[state["sent"]])
                    state["sent"] += 1

    pump(2)

    with jax.named_scope("pack"):

        def pack_g(i, carry):
            rows = pl.ds(multiple(i * dr, dr), dr)
            for j in range(M):
                cols = slice(j * F, (j + 1) * F)
                gb[i % 2, i // 2, j, 0:dr, :] = g1[rows, cols]
                gb[i % 2, i // 2, j, dr : 2 * dr, :] = g2t[rows, cols]
            return carry

        lax.fori_loop(0, N, pack_g, 0)

        def fold(t, carry):
            for j in range(D // LANES):
                cols = slice(j * LANES, (j + 1) * LANES)
                turned = vec[t, cols, :].T
                vt[t, :, cols] = sum(turned[k * K : (k + 1) * K, :] for k in range(per_mask))
            return carry

        lax.fori_loop(0, 6, fold, 0)
        for t in range(6):
            for i in range(N):
                for j in range(M):
                    row = 2 * dr + t * kb
                    gb[i % 2, i // 2, j, row : row + kb, :] = vt[t, i * kb : (i + 1) * kb, j * F : (j + 1) * F]
        own = mk[pl.ds(multiple(m * groups, groups), groups), :]
        totals = [stat[0:8, :], stat[8:16, :], own]
        rows8 = [jnp.sum(v, keepdims=True).reshape(1, 1) for v in totals]
        rows8.append(jnp.where(rows8[2] > cap, 1.0, 0.0))
        row_id = lax.broadcasted_iota(jnp.int32, (8, F), 0)
        lines = sum(jnp.where(row_id == k, v, 0.0) for k, v in enumerate(rows8))

        def put(i, carry):
            for j in range(M):
                gb[i % 2, i // 2, j, 2 * dr + tr : pr, :] = lines
            return carry

        lax.fori_loop(0, N, put, 0)

    with jax.named_scope("sum_core"):
        for o in xy_order + [0]:
            k = flip(q, o)
            remote(gb.at[1 - c, k], rcore.at[k], gc_send.at[o], gc_recv.at[o], core_peer).start()

        def add_core(k):
            def step(j, carry):
                gb[c, k, j] += rcore[k, j]
                return carry

            lax.fori_loop(0, M, step, 0)

        def over_xy(o):
            k = flip(q, o)
            sems = [(gx_send.at[n, o], gx_recv.at[n, o], xy_peer(o)) for n in range(2)]
            tail = gb.at[c, k, :, pl.ds(2 * dr, pr - 2 * dr), :]
            return remote(xs.at[o], rxg.at[o], *sems[0]), remote(tail, rxv.at[o], *sems[1])

        for o in xy_order + [0]:
            k = flip(q, o)
            remote(gb.at[1 - c, k], rcore.at[k], gc_send.at[o], gc_recv.at[o], core_peer).wait()
            add_core(k)
            if o:

                def round_piece(j, carry):
                    xs[o, j] = gb[c, k, j, 0 : 2 * dr, :].astype(BF16)
                    return carry

                lax.fori_loop(0, M, round_piece, 0)
                for copy in over_xy(o):
                    copy.start()
    with jax.named_scope("sum_xy"):
        for o in xy_order:
            for copy in over_xy(o):
                copy.wait()

            def step(j, carry):
                gb[c, q, j, 0 : 2 * dr, :] += rxg[o, j].astype(F32)
                gb[c, q, j, 2 * dr : pr, :] += rxv[o, j]
                return carry

            lax.fori_loop(0, M, step, 0)
    with jax.named_scope("sum_z"):
        slot = 0
        for bit in bits:
            moves = []
            for h in range(0, M, 2 * bit):
                away = flip(m, h + bit)
                zs[slot] = gb[c, q, away, 0 : 2 * dr, :].astype(BF16)
                sems = [(gz_send.at[k, slot], gz_recv.at[k, slot], z_peer(bit)) for k in range(2)]
                tail = gb.at[c, q, away, pl.ds(2 * dr, pr - 2 * dr), :]
                moves.append((slot, h, remote(zs.at[slot], rzg.at[slot], *sems[0]), remote(tail, rzv.at[slot], *sems[1])))
                slot += 1
            for _, _, one, two in moves:
                one.start()
                two.start()
            pump(3 if bit == bits[0] else 2)
            for k, h, one, two in moves:
                keep = flip(m, h)
                one.wait()
                two.wait()
                gb[c, q, keep, 0 : 2 * dr, :] += rzg[k].astype(F32)
                gb[c, q, keep, 2 * dr : pr, :] += rzv[k]

    total = gb[c, q, m]
    ga[c, q, m] = total[0 : 2 * dr, :].astype(BF16)
    with jax.named_scope("spread_z"):

        def over_z(o, slot):
            return remote(ga.at[c, q, m], ga.at[c, q, slot], az_send.at[o], az_recv.at[o], z_peer(o))

        for o in z_order:
            over_z(o, m).start()
        for load in loads[4:14]:
            load.wait()
        g1_out[...] = total[0:dr, :]
        g2_out[...] = total[dr : 2 * dr, :]
        corr_one = 1.0 - beta_first**STEP
        corr_two = 1.0 - beta_second**STEP
        for t in range(6):
            row = 2 * dr + t * kb
            grad = total[row : row + kb, :]
            one = beta_first * m1_v[t] + (1.0 - beta_first) * grad
            two = beta_second * m2_v[t] + (1.0 - beta_second) * grad * grad
            m1_out[t] = one
            m2_out[t] = two
            mem_out[t] = mem_v[t] - adam_rate * (one / corr_one) / (jnp.sqrt(two / corr_two) + adam_eps)
        sums_out[...] = total[2 * dr + tr : pr, 0:LANES if F >= LANES else F]
        pump(len(items), len(items))
        if packed:
            for o in z_order[:-1]:
                unpack_from(o)
        for o in z_order:
            over_z(o, flip(m, o)).wait()
    with jax.named_scope("spread_xy"):
        for o in xy_order:
            remote(ga.at[c, q], ga.at[c, q], ax_send.at[o], ax_recv.at[o], xy_peer(o)).start()
        if packed:
            for o in z_order[-1:]:
                unpack_from(o)
        for o in xy_order:
            remote(ga.at[c, q], ga.at[c, flip(q, o)], ax_send.at[o], ax_recv.at[o], xy_peer(o)).wait()
    with jax.named_scope("spread_core"):
        remote(ga.at[c], ga.at[c], ac_send, ac_recv, core_peer).start()
        remote(ga.at[c], ga.at[1 - c], ac_send, ac_recv, core_peer).wait()
    with jax.named_scope("shampoo"):

        def place_g(i, carry):
            rows = pl.ds(multiple(i * dr, dr), dr)
            for j in range(M):
                cols = slice(j * F, (j + 1) * F)
                g1f[rows, cols] = ga[i % 2, i // 2, j, 0:dr, :]
                g2ft[rows, cols] = ga[i % 2, i // 2, j, dr : 2 * dr, :]
            return carry

        lax.fori_loop(0, N, place_g, 0)

        def turn_g(i, carry):
            here = pl.ds(multiple(i * LANES, LANES), LANES)
            for j in range(D // LANES):
                there = slice(j * LANES, (j + 1) * LANES)
                g1ft[there, here] = g1f[here, there].astype(F32).T.astype(BF16)
                g2f[there, here] = g2ft[here, there].astype(F32).T.astype(BF16)
            return carry

        lax.fori_loop(0, D // LANES, turn_g, 0)
        by_d = pl.ds(multiple(d * dr, dr), dr)
        by_m = pl.ds(multiple(m * F, F), F)

        def renewed(old, fresh):
            return stat_decay * old + (1.0 - stat_decay) * fresh

        l1_out[...] = renewed(l1_v[...], mm_t(g1f[by_d, :], g1f[by_m, :]))
        r1_out[...] = renewed(r1_v[...], mm_t(g1ft[by_d, :], g1ft[by_m, :]))
        l2_out[...] = renewed(l2_v[...], mm_t(g2f[by_d, :], g2f[by_m, :]))
        r2_out[...] = renewed(r2_v[...], mm_t(g2ft[by_d, :], g2ft[by_m, :]))

        def stepped(weight, left, grad, right):
            inner = jnp.dot(left[...], grad[...].astype(F32), precision=high, preferred_element_type=F32)
            return weight[...] - shampoo_rate * mm_t(inner, right[...], high)

        w1_out[...] = stepped(w1_v, p1_v, g1f, q1_v)
        w2_out[...] = stepped(w2_v, q2_v, g2ft, p2_v)

    with jax.named_scope("drain"):
        while state["done"] < len(items):
            wait_out(*items[state["done"]])
            state["done"] += 1
        for kind, out in enumerate((lg_out,) if packed else (lg_out, ig_out)):
            part = out.at[:, pl.ds(0, (M - 1) * mine)]
            remote(part, part, in_send.at[kind], out_recv.at[kind, 0], z_peer(1)).wait_recv()
        for kind, buf in enumerate((xb, cb)):
            part = buf.at[pl.ds(0, others), :]
            remote(part, part, in_send.at[kind], out_recv.at[0, 0], z_peer(1)).wait_send()


def finish(n_out, D, sums_ref, *refs):
    outs = refs[n_out : 2 * n_out]
    rms_ref, flag_ref, sems = refs[2 * n_out :]
    copies = [pltpu.make_async_copy(refs[i], outs[i], sems.at[i]) for i in range(n_out)]
    for copy in copies:
        copy.start()
    sums = sums_ref[...]
    ratio = jnp.sqrt(sums / (sums[2:3, :] * D))
    rms_ref[0] = ratio[0, 0]
    rms_ref[1] = ratio[1, 0]
    flag_ref[0] = jnp.where(sums[3, 0] > 0.0, 1, 0)
    for copy in copies:
        copy.wait()


def solution(mesh):
    N, M = mesh.shape["dp"], mesh.shape["mp"]
    Q = N // 2

    def on_device(*args):
        x, cot, mask, members, m1, m2, w1, w2, l1, r1, l2, r2, p1, q1, p2, q2 = args
        mask, w2, l2, r2 = mask.T, w2.T, l2.T, r2.T
        args = (x, cot, mask, members, m1, m2, w1, w2, l1, r1, l2, r2, p1, q1, p2, q2)
        F, R = x.shape
        D = F * M
        mine = R // M
        w = min(CHUNK, mine)
        C = mine // w
        kb = members.shape[1]
        dr = w1.shape[0]
        tr = -(-6 * kb // 8) * 8
        pr = 2 * dr + tr + 8
        groups = mine // LANES
        S = jax.ShapeDtypeStruct
        V = pltpu.VMEM
        dma = pltpu.SemaphoreType.DMA
        outs = [S(x.shape, BF16), S(x.shape, BF16), S((8, min(F, LANES)), F32)]
        outs += [S(a.shape, F32) for a in (w1, w1, l1, r1, w2, w2, l2, r2, m1, m2, members)]
        anywhere = pl.BlockSpec(memory_space=pl.ANY)
        vmem = pl.BlockSpec(memory_space=pltpu.VMEM)
        smem = pl.BlockSpec(memory_space=pltpu.SMEM)

        def run(cap, number):
            packed = cap < mine
            KC = cap // w

            def only(shape, dtype):
                return V(shape if packed else (16, LANES), dtype)

            scratch = [V(a.shape, a.dtype) for a in (mask, members, m1, m2, w1, w2, l1, r1, l2, r2, p1, q1, p2, q2)]
            scratch += [only((F, R), BF16), only((M, F, cap), BF16), only((KC, w, w), BF16), only((M, F, cap), BF16)]
            scratch += [V((D, mine), BF16), V((D, cap), BF16), V((D, mine), BF16), V((D, cap), BF16)]
            scratch += [V((2, Q, M, 2 * dr, F), BF16), V((2, Q, M, tr, F), F32)]
            scratch += [V((D, D), BF16)] * 4
            scratch += [V((6, D, LANES), F32), V((6, K, D), F32), V(mask.shape[::-1], F32)]
            scratch += [V((M * groups, LANES), F32), V((M * groups, LANES), F32)]
            scratch += [V((D, w), F32)] * 4
            scratch += [V((D, w), BF16)] * 4
            scratch += [only((D, w), F32), only((D, w), BF16)]
            scratch += [V((D, D), F32)] * 2
            scratch += [V((6, D, LANES), F32), V((6, K, D), F32), V((16, LANES), F32)]
            scratch += [V((2, Q, M, pr, F), F32), V((Q, M, pr, F), F32)]
            scratch += [V((Q, M, 2 * dr, F), BF16), V((Q, M, 2 * dr, F), BF16), V((Q, M, pr - 2 * dr, F), F32)]
            scratch += [V((M - 1, 2 * dr, F), BF16), V((M - 1, pr - 2 * dr, F), F32), V((M - 1, 2 * dr, F), BF16)]
            scratch += [V((2, Q, M, 2 * dr, F), BF16)]
            scratch += [V((D, D), BF16)] * 4
            scratch += [dma((15,)), dma((2,)), dma((C,)), dma((C,)), dma((2, C)), dma((2, C)), dma((2, C)), dma((2, M))]
            scratch += [dma((2, M)), dma((2, M)), dma((2, Q)), dma((2, Q)), dma((2,)), dma((2,))]
            scratch += [dma((Q,)), dma((Q,)), dma((2, Q)), dma((2, Q)), dma((2, M)), dma((2, M))]
            scratch += [dma((M,)), dma((M,)), dma((Q,)), dma((Q,)), dma, dma]
            res = pl.pallas_call(
                functools.partial(kernel, N, M, cap),
                out_shape=[V(a.shape, a.dtype) for a in outs],
                in_specs=[anywhere] * 16,
                out_specs=[vmem] * 14,
                scratch_shapes=scratch,
                compiler_params=pltpu.CompilerParams(
                    collective_id=number, has_side_effects=True, vmem_limit_bytes=46 << 20
                ),
                name="packed" if packed else "whole",
            )(*[pltpu.with_memory_space_constraint(a, pltpu.HBM) for a in args])
            kept = [*res[:2], *res[3:]]
            *done, rms, flag = pl.pallas_call(
                functools.partial(finish, len(kept), D),
                out_shape=[S(a.shape, a.dtype) for a in kept] + [S((2,), F32), S((1,), jnp.int32)],
                in_specs=[vmem] + [anywhere] * len(kept),
                out_specs=[anywhere] * len(kept) + [smem] * 2,
                scratch_shapes=[dma((len(kept),))],
                compiler_params=pltpu.CompilerParams(vmem_limit_bytes=16 << 20),
                name="finish",
            )(res[2], *kept)
            return flag, (*done, rms)

        flag, fast = run(mine * 3 // 4, 0)
        done = lax.cond(flag[0] > 0, lambda: run(mine, 1)[1], lambda: fast)
        logits, igrad, g1, n1, l1, r1, g2, n2, l2, r2, m1, m2, new, rms = done
        return (logits, igrad, rms, g1, n1, l1, r1, g2.T, n2.T, l2.T, r2.T, m1, m2, new)

    placed = (
        P("mp", "dp"),
        P("mp", "dp"),
        P("dp", None),
        P(None, "dp", "mp"),
        P(None, "dp", "mp"),
        P(None, "dp", "mp"),
        P("dp", "mp"),
        P("mp", "dp"),
        P("dp", "mp"),
        P("dp", "mp"),
        P("mp", "dp"),
        P("mp", "dp"),
        P("dp", None),
        P("mp", None),
        P("mp", None),
        P("dp", None),
    )
    return jax.shard_map(
        on_device,
        mesh=mesh,
        in_specs=placed,
        out_specs=(
            P("mp", "dp"),
            P("mp", "dp"),
            P(),
            P("dp", "mp"),
            P("dp", "mp"),
            P("dp", "mp"),
            P("dp", "mp"),
            P("mp", "dp"),
            P("mp", "dp"),
            P("mp", "dp"),
            P("mp", "dp"),
            P(None, "dp", "mp"),
            P(None, "dp", "mp"),
            P(None, "dp", "mp"),
        ),
        check_vma=False,
    )
```

```python
import functools

import jax
import jax.numpy as jnp
from jax import lax
from jax.experimental import pallas as pl
from jax.experimental.pallas import tpu as pltpu
from jax.sharding import PartitionSpec as P

K = 32
STEP = 10
LANES = 128
CHUNK = 256
ROWS = 32
AHEAD = 2
FIRST = 4
OUT = 6
LEAST = 8

beta_first = 0.9
beta_second = 0.999
adam_eps = 1e-08
adam_rate = 0.2
stat_decay = 0.95
shampoo_rate = 1.0
curve_a = 0.7978845608028654
curve_b = 0.044715

MESH = pl.DeviceIdType.MESH
F32 = jnp.float32
BF16 = jnp.bfloat16
over_lanes = (((1,), (1,)), ((), ()))


def flip(index, mask):
    bit = 1
    while bit <= mask:
        if mask & bit:
            index = index + bit - 2 * bit * ((index // bit) % 2)
        bit *= 2
    return index


def mm(a, b):
    return jnp.dot(a, b, preferred_element_type=F32)


def mm_t(a, b, precision=None):
    return lax.dot_general(a, b, over_lanes, precision=precision, preferred_element_type=F32)


def multiple(value, by):
    return pl.multiple_of(value, by)


def kernel(
    N,
    M,
    cap,
    x_hbm,
    cot_hbm,
    mask_hbm,
    mem_hbm,
    m1_hbm,
    m2_hbm,
    w1_hbm,
    w2_hbm,
    l1_hbm,
    r1_hbm,
    l2_hbm,
    r2_hbm,
    p1_hbm,
    q1_hbm,
    p2_hbm,
    q2_hbm,
    lg_out,
    ig_out,
    sums_out,
    g1_out,
    w1_out,
    l1_out,
    r1_out,
    g2_out,
    w2_out,
    l2_out,
    r2_out,
    m1_out,
    m2_out,
    mem_out,
    mask_v,
    mem_v,
    m1_v,
    m2_v,
    w1_v,
    w2_v,
    l1_v,
    r1_v,
    l2_v,
    r2_v,
    p1_v,
    q1_v,
    p2_v,
    q2_v,
    cv,
    cp,
    st,
    igr,
    xb,
    cb,
    lgb,
    igb,
    wb,
    tb,
    w1,
    w1t,
    w2,
    w2t,
    tab,
    stage,
    mt,
    mk,
    rk,
    hp,
    hid,
    dgm,
    prod,
    sc,
    hi,
    gp,
    gpre,
    cx,
    ig,
    g1,
    g2t,
    vec,
    vt,
    stat,
    gb,
    rcore,
    xs,
    rxg,
    rxv,
    rzg,
    rzv,
    zs,
    ga,
    g1f,
    g1ft,
    g2f,
    g2ft,
    local_sem,
    in_send,
    x_recv,
    c_recv,
    own_sem,
    out_send,
    out_own,
    out_recv,
    wz_send,
    wz_recv,
    wx_send,
    wx_recv,
    wc_send,
    wc_recv,
    gc_send,
    gc_recv,
    gx_send,
    gx_recv,
    gz_send,
    gz_recv,
    az_send,
    az_recv,
    ax_send,
    ax_recv,
    ac_send,
    ac_recv,
):
    F, R = x_hbm.shape
    D = F * M
    Q = N // 2
    mine = R // M
    w = min(CHUNK, mine)
    C = mine // w
    tiles = w // LANES
    packed = cap < mine
    KC = cap // w
    groups = mine // LANES
    kb = K // N
    dr = D // N
    tr = tb.shape[3]
    pr = gb.shape[3]
    blocks = D // ROWS
    high = lax.Precision.HIGHEST

    d, m = lax.axis_index("dp"), lax.axis_index("mp")
    c, q = d % 2, d // 2

    def z_peer(o):
        return (d, flip(m, o))

    def xy_peer(o):
        return (flip(q, o) * 2 + c, m)

    core_peer = (flip(d, 1), m)
    z_order = sorted(range(1, M), reverse=True)
    bits = [1 << k for k in range(M.bit_length() - 1)]
    xy_order = sorted(range(1, Q), reverse=True)

    def remote(src, dst, send, recv, peer):
        return pltpu.make_async_remote_copy(
            src_ref=src, dst_ref=dst, send_sem=send, recv_sem=recv, device_id=peer, device_id_type=MESH
        )

    pairs = (
        (mask_hbm, mask_v),
        (mem_hbm, mem_v),
        (w1_hbm, w1_v),
        (w2_hbm, w2_v),
        (m1_hbm, m1_v),
        (m2_hbm, m2_v),
        (l1_hbm, l1_v),
        (r1_hbm, r1_v),
        (l2_hbm, l2_v),
        (r2_hbm, r2_v),
        (p1_hbm, p1_v),
        (q1_hbm, q1_v),
        (p2_hbm, p2_v),
        (q2_hbm, q2_v),
    )
    if packed:
        pairs = (*pairs, (cot_hbm, cv))
    loads = [pltpu.make_async_copy(a, b, local_sem.at[i]) for i, (a, b) in enumerate(pairs)]
    for load in loads:
        load.start()

    with jax.named_scope("barrier"):
        entry = pltpu.get_barrier_semaphore()
        peers = [z_peer(o) for o in z_order] + [xy_peer(o) for o in xy_order] + [core_peer]
        for peer in peers:
            pl.semaphore_signal(entry, inc=1, device_id=peer, device_id_type=MESH)
        pl.semaphore_wait(entry, len(peers))

    kinds_in = ((xb, x_recv, 0), (cb, c_recv, 1))

    def send_in(i, kinds=(0, 1)):
        here = pl.ds(multiple(m * F, F), F)
        col = pl.ds(multiple(i * w, w), w)

        def source(kind, to):
            if kind and packed:
                return cp.at[to, :, col]
            return (x_hbm, cot_hbm)[kind].at[:, pl.ds(multiple(to * mine + i * w, w), w)]

        def start(kind):
            buf, sem, _ = kinds_in[kind]
            for o in z_order:
                to = flip(m, o)
                remote(source(kind, to), buf.at[here, col], in_send.at[kind], sem.at[i], (d, to)).start()
            pltpu.make_async_copy(source(kind, m), buf.at[here, col], own_sem.at[kind, i]).start()

        for kind in kinds:
            if kind and packed and not isinstance(i, int):
                pl.when(i < KC)(lambda: start(1))
            elif not (kind and packed) or i < KC:
                start(kind)

    others = (M - 1) * F

    def wait_in(i):
        def arrive(kind):
            buf, sem, _ = kinds_in[kind]
            part = buf.at[pl.ds(0, others), pl.ds(0, w)]
            remote(part, part, in_send.at[kind], sem.at[i], z_peer(1)).wait_recv()
            block = buf.at[pl.ds(0, F), pl.ds(0, w)]
            pltpu.make_async_copy(block, block, own_sem.at[kind, i]).wait()

        arrive(0)
        if packed:
            pl.when(i < KC)(lambda: arrive(1))
        else:
            arrive(1)

    def send_out(kind, i):
        col = pl.ds(multiple(i * w, w), w)
        if kind and packed:
            there = igr.at[m, :, col]
        else:
            there = (lg_out, ig_out)[kind].at[:, pl.ds(multiple(m * mine + i * w, w), w)]
        buf = (lgb, igb)[kind]
        for o in z_order:
            to = flip(m, o)
            recv = out_recv.at[kind, o] if kind and packed else out_recv.at[kind, 0]
            remote(
                buf.at[pl.ds(multiple(to * F, F), F), col], there, out_send.at[kind, i], recv, (d, to)
            ).start()
        if not (kind and packed):
            pltpu.make_async_copy(buf.at[pl.ds(multiple(m * F, F), F), col], there, out_own.at[kind, i]).start()

    def wait_out(kind, i):
        buf = (lgb, igb)[kind]
        part = buf.at[pl.ds(0, others), pl.ds(0, w)]
        remote(part, part, out_send.at[kind, i], out_recv.at[kind, 0], z_peer(1)).wait_send()
        if not (kind and packed):
            own = buf.at[pl.ds(0, F), pl.ds(0, w)]
            pltpu.make_async_copy(own, own, out_own.at[kind, i]).wait()

    line = lax.broadcasted_iota(jnp.int32, (w, LANES), 0).astype(F32)

    def matches(p, k, i):
        base = (k * w) * jnp.float32(1) if isinstance(k, int) else (k * w).astype(F32)
        parts = []
        for j in range(tiles):
            row = rk[pl.ds(p * groups + i * tiles + j, 1), :] - base
            parts.append(jnp.where(line == row, 1.0, 0.0).astype(BF16))
        return jnp.concatenate(parts, axis=1)

    spread_by = K // LEAST

    def pack_block(k, p):
        def step(i, acc):
            cols = pl.ds(multiple(p * mine + i * w, w), w)
            return acc + mm_t(cv[:, cols], matches(p, k, i))

        acc = lax.fori_loop(k, min(C, spread_by * k + spread_by), step, jnp.zeros((F, w), F32))
        cp[p, :, k * w : (k + 1) * w] = acc.astype(BF16)

    def shrink(k):
        with jax.named_scope("shrink"):
            end = min(C, spread_by * k + spread_by)

            def step(i, carry):
                st[:, pl.ds(multiple(i * w, w), w)] = matches(m, k, i)
                return carry

            lax.fori_loop(k, end, step, 0)
            part = slice(k * w, end * w)
            igb[:, k * w : (k + 1) * w] = mm_t(ig[:, part], st[:, part]).astype(BF16)

    def pack_chunk(k):
        with jax.named_scope("pack_cot"):

            def step(p, carry):
                pack_block(k, p)
                return carry

            lax.fori_loop(0, M, step, 0)

    def unpack_block(p):
        with jax.named_scope("unpack"):

            def chunk(i, carry):
                def step(k, acc):
                    return acc + mm(igr[p, :, pl.ds(multiple(k * w, w), w)], matches(p, k, i))

                acc = lax.fori_loop(i // spread_by, jnp.minimum(i, KC - 1) + 1, step, jnp.zeros((F, w), F32))
                ig_out[:, pl.ds(multiple(p * mine + i * w, w), w)] = acc.astype(BF16)
                return carry

            lax.fori_loop(0, C, chunk, 0)

    def unpack_from(o):
        part = igr.at[0]
        remote(part, part, in_send.at[0], out_recv.at[1, o], z_peer(o)).wait_recv()
        unpack_block(flip(m, o))

    for load in loads[:4]:
        load.wait()
    wb[c, q, m, 0:dr, :] = w1_v[...].astype(BF16)
    wb[c, q, m, dr : 2 * dr, :] = w2_v[...].astype(BF16)
    for t in range(6):
        tb[c, q, m, t * kb : (t + 1) * kb, :] = mem_v[t]

    def spread_z(bit, bufs, send, recv):
        for h in range(0, M, 2 * bit):
            slot, back = flip(m, h), flip(m, h + bit)
            for k, buf in enumerate(bufs):
                one, two = buf.at[c, q, slot], buf.at[c, q, back]
                sems = (send.at[k, h + bit], recv.at[k, h + bit], z_peer(bit))
                yield remote(one, one, *sems), remote(one, two, *sems)

    bufs = (wb, tb)
    first = list(spread_z(bits[-1], bufs, wz_send, wz_recv))
    for go, _ in first:
        go.start()
    per_mask = LANES // K
    mt[...] = mask_v[...].astype(F32).T
    mk[...] = jnp.concatenate(
        [mt[pl.ds(j, M * groups, stride=per_mask), :] for j in range(per_mask)], axis=1
    )
    if packed:
        flags = mk[...]
        rows, cols = M * groups, LANES
        lower = lax.broadcasted_iota(jnp.int32, (cols, cols), 0) < lax.broadcasted_iota(jnp.int32, (cols, cols), 1)
        inside = mm(flags.astype(BF16), jnp.where(lower, 1.0, 0.0).astype(BF16))
        sums = jnp.broadcast_to(jnp.sum(flags, axis=1, keepdims=True), (rows, cols)).astype(BF16)
        one = lax.broadcasted_iota(jnp.int32, (rows, rows), 0)
        two = lax.broadcasted_iota(jnp.int32, (rows, rows), 1)
        ahead = (two < one) & (two >= one - one % groups)
        place_in = inside + mm(jnp.where(ahead, 1.0, 0.0).astype(BF16), sums)
        rk[...] = jnp.where(flags > 0.0, place_in, -1.0)
    send_in(0, (0,) if packed else (0, 1))

    def clear(i, carry):
        rows = pl.ds(multiple(i * ROWS, ROWS), ROWS)
        g1[rows, :] = jnp.zeros((ROWS, D), F32)
        g2t[rows, :] = jnp.zeros((ROWS, D), F32)
        for t in range(6):
            vec[t, rows, :] = jnp.zeros((ROWS, LANES), F32)
        return carry

    lax.fori_loop(0, blocks, clear, 0)
    stat[...] = jnp.zeros_like(stat)

    ahead_of = min(FIRST, C)
    if packed:
        loads[-1].wait()
        pack_chunk(0)

    def step_in(k):
        if packed:
            if k < KC:
                send_in(k, (1,))
            if k + 1 < ahead_of:
                send_in(k + 1, (0,))
            if k + 1 < KC:
                pack_chunk(k + 1)
        elif k + 1 < ahead_of:
            send_in(k + 1)

    with jax.named_scope("weights_z"):
        for bit in bits[::-1]:
            if bit != bits[-1]:
                first = list(spread_z(bit, bufs, wz_send, wz_recv))
                for go, _ in first:
                    go.start()
            if bit == bits[0]:
                step_in(0)
            for _, come in first:
                come.wait()
    with jax.named_scope("weights_xy"):
        for o in xy_order:
            for k, buf in enumerate(bufs):
                remote(buf.at[c, q], buf.at[c, q], wx_send.at[k, o], wx_recv.at[k, o], xy_peer(o)).start()
        step_in(1)
        step_in(2)
        for o in xy_order:
            for k, buf in enumerate(bufs):
                remote(buf.at[c, q], buf.at[c, flip(q, o)], wx_send.at[k, o], wx_recv.at[k, o], xy_peer(o)).wait()
    with jax.named_scope("weights_core"):
        for k, buf in enumerate(bufs):
            remote(buf.at[c], buf.at[c], wc_send.at[k], wc_recv.at[k], core_peer).start()
        for k in range(3, max(ahead_of, KC if packed else 0)):
            if k < ahead_of:
                step_in(k)
            elif k + 1 < KC:
                pack_chunk(k + 1)
        for k, buf in enumerate(bufs):
            remote(buf.at[c], buf.at[1 - c], wc_send.at[k], wc_recv.at[k], core_peer).wait()

    with jax.named_scope("weights_spread"):

        def place(i, carry):
            rows = pl.ds(multiple(i * dr, dr), dr)
            for j in range(M):
                cols = slice(j * F, (j + 1) * F)
                w1[rows, cols] = wb[i % 2, i // 2, j, 0:dr, :]
                w2t[rows, cols] = wb[i % 2, i // 2, j, dr : 2 * dr, :]
            return carry

        lax.fori_loop(0, N, place, 0)

        def turn(i, carry):
            here = pl.ds(multiple(i * LANES, LANES), LANES)
            for j in range(D // LANES):
                there = slice(j * LANES, (j + 1) * LANES)
                w1t[there, here] = w1[here, there].astype(F32).T.astype(BF16)
                w2[there, here] = w2t[here, there].astype(F32).T.astype(BF16)
            return carry

        lax.fori_loop(0, D // LANES, turn, 0)
        for t in range(6):
            for i in range(N):
                for j in range(M):
                    stage[t, i * kb : (i + 1) * kb, j * F : (j + 1) * F] = tb[
                        i % 2, i // 2, j, t * kb : (t + 1) * kb, :
                    ]

        def table(t, carry):
            for j in range(D // LANES):
                cols = slice(j * LANES, (j + 1) * LANES)
                piece = stage[t, :, cols]
                tab[t, cols, :] = jnp.concatenate([piece] * per_mask, axis=0).T
            return carry

        lax.fori_loop(0, 6, table, 0)

    def eight(value):
        return value.reshape(ROWS // 8, 8, LANES).sum(0)

    if packed:
        early = [(C - 3, [(0, 0)]), (C - 2, [(0, 1)]), (C - 1, [(0, 2)])]
    else:
        early = [(C - 2, [(0, 0), (1, 0)]), (C - 1, [(0, 1), (1, 1)])]

    def work(i, carry):
        col = multiple(i * w, w)
        with jax.named_scope("wait_in"):
            wait_in(i)

        @pl.when((i + AHEAD >= FIRST) & (i + AHEAD < C - 1))
        def _():
            send_in(i + AHEAD)

        if C > FIRST:

            @pl.when(i + AHEAD == C - 2)
            def _():
                send_in(C - 1)

        for late, parts in early:
            for kind, k in parts:
                pl.when(i == late)(functools.partial(send_out, kind, k))

        masks = [mk[pl.ds(m * groups + i * tiles + j, 1), :] for j in range(tiles)]

        def place_of(r):
            return pl.ds(multiple(r * ROWS, ROWS), ROWS)

        def lanes_of(j):
            return pl.ds(multiple(col + j * LANES, LANES), LANES)

        def scale_rows(r, sums):
            rows = place_of(r)
            row_in = tab[0, rows, :]
            new = []
            for j in range(tiles):
                x = xb[rows, lanes_of(j)].astype(F32)
                sc[rows, j * LANES : (j + 1) * LANES] = (x * row_in).astype(BF16)
                new.append(sums[j] + eight(x * x))
            return tuple(new)

        zero = tuple(jnp.zeros((8, LANES), F32) for _ in range(tiles))
        with jax.named_scope("scale"):
            x_sums = lax.fori_loop(0, blocks, scale_rows, zero)
        with jax.named_scope("mm_one"):
            hp[...] = mm(w1t[...], sc[...])

        def curve_rows(r, carry):
            rows = place_of(r)
            gain, bias, row_mid = tab[1, rows, :], tab[2, rows, :], tab[3, rows, :]
            for j in range(tiles):
                cols = slice(j * LANES, (j + 1) * LANES)
                s = hp[rows, cols] * gain + bias
                s2 = s * s
                th = jnp.tanh(curve_a * (s + curve_b * (s2 * s)))
                cdf = 0.5 * (1.0 + th)
                h = s * cdf
                slope = cdf + (0.5 * s) * (1.0 - th * th) * (curve_a + (3.0 * curve_a * curve_b) * s2)
                hid[rows, cols] = h
                dgm[rows, cols] = slope * row_mid
                hi[rows, cols] = (h * row_mid).astype(BF16)
            return carry

        with jax.named_scope("curve"):
            lax.fori_loop(0, blocks, curve_rows, 0)
        with jax.named_scope("mm_two"):
            prod[...] = mm(w2t[...], hi[...])
        low, high_k = i // spread_by, jnp.minimum(i, KC - 1)
        if packed:
            with jax.named_scope("expand"):

                def grow(k, carry):
                    cx[...] += mm(cb[:, pl.ds(multiple(k * w, w), w)], matches(m, k, i))
                    return carry

                cx[...] = jnp.zeros_like(cx)
                lax.fori_loop(low, high_k + 1, grow, 0)

        def grad_of(rows, j):
            if packed:
                return cx[rows, j * LANES : (j + 1) * LANES]
            return cb[rows, lanes_of(j)].astype(F32) * masks[j]


        def out_rows(r, sums):
            rows = place_of(r)
            gain, bias = tab[4, rows, :], tab[5, rows, :]
            v4, v5 = vec[4, rows, :], vec[5, rows, :]
            new = []
            for j in range(tiles):
                cols = slice(j * LANES, (j + 1) * LANES)
                x = xb[rows, lanes_of(j)].astype(F32)
                projected = prod[rows, cols]
                branch = projected * gain + bias
                lgb[rows, lanes_of(j)] = (x + branch).astype(BF16)
                new.append(sums[j] + eight(branch * branch))
                go = grad_of(rows, j)
                v5 = v5 + go
                v4 = v4 + go * projected
                gp[rows, cols] = (go * gain).astype(BF16)
            vec[4, rows, :] = v4
            vec[5, rows, :] = v5
            return tuple(new)

        with jax.named_scope("out"):
            b_sums = lax.fori_loop(0, blocks, out_rows, zero)
        for j in range(tiles):
            stat[0:8, :] += x_sums[j] * masks[j]
            stat[8:16, :] += b_sums[j] * masks[j]

        with jax.named_scope("mm_three"):
            half = D // 2
            for k in range(2):
                part = slice(k * half, (k + 1) * half)
                g2t[part, :] += mm_t(gp[part, :], hi[...])
            prod[...] = mm(w2[...], gp[...])

        def back_rows(r, carry):
            rows = place_of(r)
            gain = tab[1, rows, :]
            v1, v2, v3 = vec[1, rows, :], vec[2, rows, :], vec[3, rows, :]
            for j in range(tiles):
                cols = slice(j * LANES, (j + 1) * LANES)
                gh = prod[rows, cols]
                v3 = v3 + gh * hid[rows, cols]
                gs = gh * dgm[rows, cols]
                v2 = v2 + gs
                v1 = v1 + gs * hp[rows, cols]
                gpre[rows, cols] = (gs * gain).astype(BF16)
            vec[1, rows, :] = v1
            vec[2, rows, :] = v2
            vec[3, rows, :] = v3
            return carry

        with jax.named_scope("back"):
            lax.fori_loop(0, blocks, back_rows, 0)
        with jax.named_scope("mm_four"):
            for k in range(2):
                part = slice(k * half, (k + 1) * half)
                g1[part, :] += mm_t(sc[part, :], gpre[...])
            prod[...] = mm(w1[...], gpre[...])

        def in_rows(r, carry):
            rows = place_of(r)
            row_in = tab[0, rows, :]
            v0 = vec[0, rows, :]
            for j in range(tiles):
                cols = slice(j * LANES, (j + 1) * LANES)
                gs = prod[rows, cols]
                v0 = v0 + gs * xb[rows, lanes_of(j)].astype(F32)
                go = grad_of(rows, j)
                done = (gs * row_in + go).astype(BF16)
                if packed:
                    ig[rows, lanes_of(j)] = done
                else:
                    igb[rows, lanes_of(j)] = done
            vec[0, rows, :] = v0
            return carry

        with jax.named_scope("in"):
            lax.fori_loop(0, blocks, in_rows, 0)
        if packed:
            ig_out[:, pl.ds(multiple(m * mine + col, w), w)] = ig[pl.ds(multiple(m * F, F), F), pl.ds(col, w)]
        return carry

    lax.fori_loop(0, C, work, 0)

    items = [item for _, parts in early for item in parts]
    already = len(items)
    if packed:
        items += [(1, k) for k in range(KC)] + [(0, i) for i in range(3, C)]
    else:
        items += [(kind, i) for i in range(2, C) for kind in range(2)]
    state = {"sent": already, "done": 0}

    def pump(count, most=OUT):
        with jax.named_scope("pump"):
            for _ in range(count):
                if state["sent"] < len(items):
                    while state["sent"] - state["done"] >= most:
                        wait_out(*items[state["done"]])
                        state["done"] += 1
                    kind, k = items[state["sent"]]
                    if kind and packed:
                        shrink(k)
                    send_out(kind, k)
                    state["sent"] += 1


    with jax.named_scope("pack"):

        def pack_g(i, carry):
            rows = pl.ds(multiple(i * dr, dr), dr)
            for j in range(M):
                cols = slice(j * F, (j + 1) * F)
                gb[i % 2, i // 2, j, 0:dr, :] = g1[rows, cols]
                gb[i % 2, i // 2, j, dr : 2 * dr, :] = g2t[rows, cols]
            return carry

        lax.fori_loop(0, N, pack_g, 0)

        def fold(t, carry):
            for j in range(D // LANES):
                cols = slice(j * LANES, (j + 1) * LANES)
                turned = vec[t, cols, :].T
                vt[t, :, cols] = sum(turned[k * K : (k + 1) * K, :] for k in range(per_mask))
            return carry

        lax.fori_loop(0, 6, fold, 0)
        for t in range(6):
            for i in range(N):
                for j in range(M):
                    row = 2 * dr + t * kb
                    gb[i % 2, i // 2, j, row : row + kb, :] = vt[t, i * kb : (i + 1) * kb, j * F : (j + 1) * F]
        own = mk[pl.ds(multiple(m * groups, groups), groups), :]
        totals = [stat[0:8, :], stat[8:16, :], own]
        rows8 = [jnp.sum(v, keepdims=True).reshape(1, 1) for v in totals]
        rows8.append(jnp.where(rows8[2] > cap, 1.0, 0.0))
        row_id = lax.broadcasted_iota(jnp.int32, (8, F), 0)
        lines = sum(jnp.where(row_id == k, v, 0.0) for k, v in enumerate(rows8))

        def put(i, carry):
            for j in range(M):
                gb[i % 2, i // 2, j, 2 * dr + tr : pr, :] = lines
            return carry

        lax.fori_loop(0, N, put, 0)

    with jax.named_scope("sum_core"):
        for o in xy_order + [0]:
            k = flip(q, o)
            remote(gb.at[1 - c, k], rcore.at[k], gc_send.at[o], gc_recv.at[o], core_peer).start()

        def add_core(k):
            def step(j, carry):
                gb[c, k, j] += rcore[k, j]
                return carry

            lax.fori_loop(0, M, step, 0)

        def over_xy(o):
            k = flip(q, o)
            sems = [(gx_send.at[n, o], gx_recv.at[n, o], xy_peer(o)) for n in range(2)]
            tail = gb.at[c, k, :, pl.ds(2 * dr, pr - 2 * dr), :]
            return remote(xs.at[o], rxg.at[o], *sems[0]), remote(tail, rxv.at[o], *sems[1])

        for o in xy_order + [0]:
            k = flip(q, o)
            remote(gb.at[1 - c, k], rcore.at[k], gc_send.at[o], gc_recv.at[o], core_peer).wait()
            add_core(k)
            if o:

                def round_piece(j, carry):
                    xs[o, j] = gb[c, k, j, 0 : 2 * dr, :].astype(BF16)
                    return carry

                lax.fori_loop(0, M, round_piece, 0)
                for copy in over_xy(o):
                    copy.start()
    pump(2)
    with jax.named_scope("sum_xy"):
        for o in xy_order:
            for copy in over_xy(o):
                copy.wait()

            def step(j, carry):
                gb[c, q, j, 0 : 2 * dr, :] += rxg[o, j].astype(F32)
                gb[c, q, j, 2 * dr : pr, :] += rxv[o, j]
                return carry

            lax.fori_loop(0, M, step, 0)
    with jax.named_scope("sum_z"):
        slot = 0
        for bit in bits:
            moves = []
            for h in range(0, M, 2 * bit):
                away = flip(m, h + bit)
                zs[slot] = gb[c, q, away, 0 : 2 * dr, :].astype(BF16)
                sems = [(gz_send.at[k, slot], gz_recv.at[k, slot], z_peer(bit)) for k in range(2)]
                tail = gb.at[c, q, away, pl.ds(2 * dr, pr - 2 * dr), :]
                moves.append((slot, h, remote(zs.at[slot], rzg.at[slot], *sems[0]), remote(tail, rzv.at[slot], *sems[1])))
                slot += 1
            for _, _, one, two in moves:
                one.start()
                two.start()
            pump(1)
            for k, h, one, two in moves:
                keep = flip(m, h)
                one.wait()
                two.wait()
                gb[c, q, keep, 0 : 2 * dr, :] += rzg[k].astype(F32)
                gb[c, q, keep, 2 * dr : pr, :] += rzv[k]
            pump(1)

    total = gb[c, q, m]
    ga[c, q, m] = total[0 : 2 * dr, :].astype(BF16)
    with jax.named_scope("spread_z"):
        first = list(spread_z(bits[-1], (ga,), az_send, az_recv))
        for go, _ in first:
            go.start()
        pump(1)
        for load in loads[4:14]:
            load.wait()
        g1_out[...] = total[0:dr, :]
        g2_out[...] = total[dr : 2 * dr, :]
        corr_one = 1.0 - beta_first**STEP
        corr_two = 1.0 - beta_second**STEP
        for t in range(6):
            row = 2 * dr + t * kb
            grad = total[row : row + kb, :]
            one = beta_first * m1_v[t] + (1.0 - beta_first) * grad
            two = beta_second * m2_v[t] + (1.0 - beta_second) * grad * grad
            m1_out[t] = one
            m2_out[t] = two
            mem_out[t] = mem_v[t] - adam_rate * (one / corr_one) / (jnp.sqrt(two / corr_two) + adam_eps)
        sums_out[...] = total[2 * dr + tr : pr, 0:LANES if F >= LANES else F]
        for bit in bits[::-1]:
            if bit != bits[-1]:
                pump(1)
                first = list(spread_z(bit, (ga,), az_send, az_recv))
                for go, _ in first:
                    go.start()
            if bit == bits[0]:
                pump(len(items), len(items))
            if packed and bit == bits[0]:
                for o in z_order[:-1]:
                    unpack_from(o)
            for _, come in first:
                come.wait()
    with jax.named_scope("spread_xy"):
        for o in xy_order:
            remote(ga.at[c, q], ga.at[c, q], ax_send.at[o], ax_recv.at[o], xy_peer(o)).start()
        if packed:
            for o in z_order[-1:]:
                unpack_from(o)
        for o in xy_order:
            remote(ga.at[c, q], ga.at[c, flip(q, o)], ax_send.at[o], ax_recv.at[o], xy_peer(o)).wait()
    with jax.named_scope("spread_core"):
        remote(ga.at[c], ga.at[c], ac_send, ac_recv, core_peer).start()
        remote(ga.at[c], ga.at[1 - c], ac_send, ac_recv, core_peer).wait()
    with jax.named_scope("shampoo"):

        def place_g(i, carry):
            rows = pl.ds(multiple(i * dr, dr), dr)
            for j in range(M):
                cols = slice(j * F, (j + 1) * F)
                g1f[rows, cols] = ga[i % 2, i // 2, j, 0:dr, :]
                g2ft[rows, cols] = ga[i % 2, i // 2, j, dr : 2 * dr, :]
            return carry

        lax.fori_loop(0, N, place_g, 0)

        def turn_g(i, carry):
            here = pl.ds(multiple(i * LANES, LANES), LANES)
            for j in range(D // LANES):
                there = slice(j * LANES, (j + 1) * LANES)
                g1ft[there, here] = g1f[here, there].astype(F32).T.astype(BF16)
                g2f[there, here] = g2ft[here, there].astype(F32).T.astype(BF16)
            return carry

        lax.fori_loop(0, D // LANES, turn_g, 0)
        by_d = pl.ds(multiple(d * dr, dr), dr)
        by_m = pl.ds(multiple(m * F, F), F)

        def renewed(old, fresh):
            return stat_decay * old + (1.0 - stat_decay) * fresh

        l1_out[...] = renewed(l1_v[...], mm_t(g1f[by_d, :], g1f[by_m, :]))
        r1_out[...] = renewed(r1_v[...], mm_t(g1ft[by_d, :], g1ft[by_m, :]))
        l2_out[...] = renewed(l2_v[...], mm_t(g2f[by_d, :], g2f[by_m, :]))
        r2_out[...] = renewed(r2_v[...], mm_t(g2ft[by_d, :], g2ft[by_m, :]))

        def stepped(weight, left, grad, right):
            inner = jnp.dot(left[...], grad[...].astype(F32), precision=high, preferred_element_type=F32)
            return weight[...] - shampoo_rate * mm_t(inner, right[...], high)

        w1_out[...] = stepped(w1_v, p1_v, g1f, q1_v)
        w2_out[...] = stepped(w2_v, q2_v, g2ft, p2_v)

    with jax.named_scope("drain"):
        while state["done"] < len(items):
            wait_out(*items[state["done"]])
            state["done"] += 1
        for kind, out in enumerate((lg_out,) if packed else (lg_out, ig_out)):
            part = out.at[:, pl.ds(0, (M - 1) * mine)]
            remote(part, part, in_send.at[kind], out_recv.at[kind, 0], z_peer(1)).wait_recv()
        for kind, buf in enumerate((xb, cb)):
            part = buf.at[pl.ds(0, others), :]
            remote(part, part, in_send.at[kind], out_recv.at[0, 0], z_peer(1)).wait_send()


def finish(n_out, D, sums_ref, *refs):
    outs = refs[n_out : 2 * n_out]
    rms_ref, flag_ref, sems = refs[2 * n_out :]
    copies = [pltpu.make_async_copy(refs[i], outs[i], sems.at[i]) for i in range(n_out)]
    for copy in copies:
        copy.start()
    sums = sums_ref[...]
    ratio = jnp.sqrt(sums / (sums[2:3, :] * D))
    rms_ref[0] = ratio[0, 0]
    rms_ref[1] = ratio[1, 0]
    flag_ref[0] = jnp.where(sums[3, 0] > 0.0, 1, 0)
    for copy in copies:
        copy.wait()


def solution(mesh):
    N, M = mesh.shape["dp"], mesh.shape["mp"]
    Q = N // 2

    def on_device(*args):
        x, cot, mask, members, m1, m2, w1, w2, l1, r1, l2, r2, p1, q1, p2, q2 = args
        mask, w2, l2, r2 = mask.T, w2.T, l2.T, r2.T
        args = (x, cot, mask, members, m1, m2, w1, w2, l1, r1, l2, r2, p1, q1, p2, q2)
        F, R = x.shape
        D = F * M
        mine = R // M
        w = min(CHUNK, mine)
        C = mine // w
        kb = members.shape[1]
        dr = w1.shape[0]
        tr = -(-6 * kb // 8) * 8
        pr = 2 * dr + tr + 8
        groups = mine // LANES
        S = jax.ShapeDtypeStruct
        V = pltpu.VMEM
        dma = pltpu.SemaphoreType.DMA
        outs = [S(x.shape, BF16), S(x.shape, BF16), S((8, min(F, LANES)), F32)]
        outs += [S(a.shape, F32) for a in (w1, w1, l1, r1, w2, w2, l2, r2, m1, m2, members)]
        anywhere = pl.BlockSpec(memory_space=pl.ANY)
        vmem = pl.BlockSpec(memory_space=pltpu.VMEM)
        smem = pl.BlockSpec(memory_space=pltpu.SMEM)

        def run(cap, number):
            packed = cap < mine
            KC = cap // w

            def only(shape, dtype):
                return V(shape if packed else (16, LANES), dtype)

            scratch = [V(a.shape, a.dtype) for a in (mask, members, m1, m2, w1, w2, l1, r1, l2, r2, p1, q1, p2, q2)]
            scratch += [only((F, R), BF16), only((M, F, cap), BF16), only((w, mine), BF16), only((M, F, cap), BF16)]
            scratch += [V((D, mine), BF16), V((D, cap), BF16), V((D, mine), BF16), V((D, cap), BF16)]
            scratch += [V((2, Q, M, 2 * dr, F), BF16), V((2, Q, M, tr, F), F32)]
            scratch += [V((D, D), BF16)] * 4
            scratch += [V((6, D, LANES), F32), V((6, K, D), F32), V(mask.shape[::-1], F32)]
            scratch += [V((M * groups, LANES), F32), V((M * groups, LANES), F32)]
            scratch += [V((D, w), F32)] * 4
            scratch += [V((D, w), BF16)] * 4
            scratch += [only((D, w), F32), only((D, mine), BF16)]
            scratch += [V((D, D), F32)] * 2
            scratch += [V((6, D, LANES), F32), V((6, K, D), F32), V((16, LANES), F32)]
            scratch += [V((2, Q, M, pr, F), F32), V((Q, M, pr, F), F32)]
            scratch += [V((Q, M, 2 * dr, F), BF16), V((Q, M, 2 * dr, F), BF16), V((Q, M, pr - 2 * dr, F), F32)]
            scratch += [V((M - 1, 2 * dr, F), BF16), V((M - 1, pr - 2 * dr, F), F32), V((M - 1, 2 * dr, F), BF16)]
            scratch += [V((2, Q, M, 2 * dr, F), BF16)]
            scratch += [V((D, D), BF16)] * 4
            scratch += [dma((15,)), dma((2,)), dma((C,)), dma((C,)), dma((2, C)), dma((2, C)), dma((2, C)), dma((2, M))]
            scratch += [dma((2, M)), dma((2, M)), dma((2, Q)), dma((2, Q)), dma((2,)), dma((2,))]
            scratch += [dma((Q,)), dma((Q,)), dma((2, Q)), dma((2, Q)), dma((2, M)), dma((2, M))]
            scratch += [dma((1, M)), dma((1, M)), dma((Q,)), dma((Q,)), dma, dma]
            res = pl.pallas_call(
                functools.partial(kernel, N, M, cap),
                out_shape=[V(a.shape, a.dtype) for a in outs],
                in_specs=[anywhere] * 16,
                out_specs=[vmem] * 14,
                scratch_shapes=scratch,
                compiler_params=pltpu.CompilerParams(
                    collective_id=number, has_side_effects=True, vmem_limit_bytes=46 << 20
                ),
                name="packed" if packed else "whole",
            )(*[pltpu.with_memory_space_constraint(a, pltpu.HBM) for a in args])
            kept = [*res[:2], *res[3:]]
            *done, rms, flag = pl.pallas_call(
                functools.partial(finish, len(kept), D),
                out_shape=[S(a.shape, a.dtype) for a in kept] + [S((2,), F32), S((1,), jnp.int32)],
                in_specs=[vmem] + [anywhere] * len(kept),
                out_specs=[anywhere] * len(kept) + [smem] * 2,
                scratch_shapes=[dma((len(kept),))],
                compiler_params=pltpu.CompilerParams(vmem_limit_bytes=16 << 20),
                name="finish",
            )(res[2], *kept)
            return flag, (*done, rms)

        flag, fast = run(mine * 3 // 4, 0)
        done = lax.cond(flag[0] > 0, lambda: run(mine, 1)[1], lambda: fast)
        logits, igrad, g1, n1, l1, r1, g2, n2, l2, r2, m1, m2, new, rms = done
        return (logits, igrad, rms, g1, n1, l1, r1, g2.T, n2.T, l2.T, r2.T, m1, m2, new)

    placed = (
        P("mp", "dp"),
        P("mp", "dp"),
        P("dp", None),
        P(None, "dp", "mp"),
        P(None, "dp", "mp"),
        P(None, "dp", "mp"),
        P("dp", "mp"),
        P("mp", "dp"),
        P("dp", "mp"),
        P("dp", "mp"),
        P("mp", "dp"),
        P("mp", "dp"),
        P("dp", None),
        P("mp", None),
        P("mp", None),
        P("dp", None),
    )
    return jax.shard_map(
        on_device,
        mesh=mesh,
        in_specs=placed,
        out_specs=(
            P("mp", "dp"),
            P("mp", "dp"),
            P(),
            P("dp", "mp"),
            P("dp", "mp"),
            P("dp", "mp"),
            P("dp", "mp"),
            P("mp", "dp"),
            P("mp", "dp"),
            P("mp", "dp"),
            P("mp", "dp"),
            P(None, "dp", "mp"),
            P(None, "dp", "mp"),
            P(None, "dp", "mp"),
        ),
        check_vma=False,
    )
```

```python
import functools

import jax
import jax.numpy as jnp
from jax import lax
from jax.experimental import pallas as pl
from jax.experimental.pallas import tpu as pltpu
from jax.sharding import PartitionSpec as P

K = 32
STEP = 10
LANES = 128
CHUNK = 256
ROWS = 32
AHEAD = 2
FIRST = 4
OUT = 6
LEAST = 8

beta_first = 0.9
beta_second = 0.999
adam_eps = 1e-08
adam_rate = 0.2
stat_decay = 0.95
shampoo_rate = 1.0
curve_a = 0.7978845608028654
curve_b = 0.044715

MESH = pl.DeviceIdType.MESH
F32 = jnp.float32
BF16 = jnp.bfloat16
over_lanes = (((1,), (1,)), ((), ()))


def flip(index, mask):
    bit = 1
    while bit <= mask:
        if mask & bit:
            index = index + bit - 2 * bit * ((index // bit) % 2)
        bit *= 2
    return index


def mm(a, b):
    return jnp.dot(a, b, preferred_element_type=F32)


def mm_t(a, b, precision=None):
    return lax.dot_general(a, b, over_lanes, precision=precision, preferred_element_type=F32)


def multiple(value, by):
    return pl.multiple_of(value, by)


def kernel(
    N,
    M,
    cap,
    x_hbm,
    cot_hbm,
    mask_hbm,
    mem_hbm,
    m1_hbm,
    m2_hbm,
    w1_hbm,
    w2_hbm,
    l1_hbm,
    r1_hbm,
    l2_hbm,
    r2_hbm,
    p1_hbm,
    q1_hbm,
    p2_hbm,
    q2_hbm,
    lg_out,
    ig_out,
    sums_out,
    order_out,
    g1_out,
    w1_out,
    l1_out,
    r1_out,
    g2_out,
    w2_out,
    l2_out,
    r2_out,
    m1_out,
    m2_out,
    mem_out,
    mask_v,
    mem_v,
    m1_v,
    m2_v,
    w1_v,
    w2_v,
    l1_v,
    r1_v,
    l2_v,
    r2_v,
    p1_v,
    q1_v,
    p2_v,
    q2_v,
    xv,
    xp,
    cv,
    cq,
    order_v,
    order_s,
    seats_v,
    seats_s,
    cp,
    st,
    igr,
    xb,
    cb,
    lgb,
    igb,
    wb,
    tb,
    w1,
    w1t,
    w2,
    w2t,
    tab,
    stage,
    mt,
    mp,
    mk,
    rk,
    hp,
    hid,
    dgm,
    prod,
    sc,
    hi,
    gp,
    gpre,
    cx,
    ig,
    g1,
    g2t,
    vec,
    vt,
    stat,
    gb,
    rcore,
    xs,
    rxg,
    rxv,
    rzg,
    rzv,
    zs,
    ga,
    g1f,
    g1ft,
    g2f,
    g2ft,
    local_sem,
    in_send,
    x_recv,
    c_recv,
    own_sem,
    out_send,
    out_own,
    out_recv,
    wz_send,
    wz_recv,
    wx_send,
    wx_recv,
    wc_send,
    wc_recv,
    gc_send,
    gc_recv,
    gx_send,
    gx_recv,
    gz_send,
    gz_recv,
    az_send,
    az_recv,
    ax_send,
    ax_recv,
    ac_send,
    ac_recv,
):
    F, R = x_hbm.shape
    D = F * M
    Q = N // 2
    mine = R // M
    w = min(CHUNK, mine)
    C = mine // w
    tiles = w // LANES
    packed = cap < mine
    KC = -(-cap // w)
    groups = mine // LANES
    kb = K // N
    dr = D // N
    tr = tb.shape[3]
    pr = gb.shape[3]
    blocks = D // ROWS
    high = lax.Precision.HIGHEST

    d, m = lax.axis_index("dp"), lax.axis_index("mp")
    c, q = d % 2, d // 2

    def z_peer(o):
        return (d, flip(m, o))

    def xy_peer(o):
        return (flip(q, o) * 2 + c, m)

    core_peer = (flip(d, 1), m)
    z_order = sorted(range(1, M), reverse=True)
    bits = [1 << k for k in range(M.bit_length() - 1)]
    xy_order = sorted(range(1, Q), reverse=True)

    def remote(src, dst, send, recv, peer):
        return pltpu.make_async_remote_copy(
            src_ref=src, dst_ref=dst, send_sem=send, recv_sem=recv, device_id=peer, device_id_type=MESH
        )

    pairs = (
        (mask_hbm, mask_v),
        (mem_hbm, mem_v),
        (w1_hbm, w1_v),
        (w2_hbm, w2_v),
        (m1_hbm, m1_v),
        (m2_hbm, m2_v),
        (l1_hbm, l1_v),
        (r1_hbm, r1_v),
        (l2_hbm, l2_v),
        (r2_hbm, r2_v),
        (p1_hbm, p1_v),
        (q1_hbm, q1_v),
        (p2_hbm, p2_v),
        (q2_hbm, q2_v),
    )
    if packed:
        pairs = (*pairs, (cot_hbm, cv), (x_hbm, xv))
    loads = [pltpu.make_async_copy(a, b, local_sem.at[i]) for i, (a, b) in enumerate(pairs)]
    for load in loads:
        load.start()

    per_mask = LANES // K
    total_tiles = M * groups

    I32 = jnp.int32

    def masks_to(ref):
        loads[0].wait()
        mt[...] = mask_v[...].T
        ref[...] = jnp.concatenate(
            [mt[pl.ds(j, total_tiles, stride=per_mask), :] for j in range(per_mask)], axis=1
        )

    def across(row):
        return jnp.broadcast_to(row, (LANES, LANES)).T

    def order_tiles():
        masks_to(mp)
        tall = jnp.concatenate([mp[...], jnp.zeros((LANES - total_tiles, LANES), I32)], axis=0)
        count = jnp.sum(tall.T, axis=0, keepdims=True)
        line_id = lax.broadcasted_iota(I32, (LANES, LANES), 0)
        lane_id = lax.broadcasted_iota(I32, (LANES, LANES), 1)
        mine_here, other = jnp.broadcast_to(count, (LANES, LANES)), across(count)
        before = (other > mine_here) | ((other == mine_here) & (line_id < lane_id))
        rank = jnp.sum(jnp.where(before & (line_id < total_tiles), 1, 0), axis=0, keepdims=True)
        turn, seat = rank // M, rank % M
        block = jnp.where(turn % 2 == 0, seat, M - 1 - seat)
        lane = lax.broadcasted_iota(I32, (1, LANES), 1)
        seats = jnp.where(lane < total_tiles, block * groups + turn, LANES)
        seats_v[...] = seats
        order_v[...] = jnp.sum(jnp.where(across(seats) == lane_id, line_id, 0), axis=0, keepdims=True)
        order_out[...] = order_v[...]
        to_scalars = pltpu.make_async_copy(order_v, order_s, local_sem.at[16])
        to_scalars.start()
        loads[15].wait()
        to_scalars.wait()
        deal(xv, xp, 0, 1)

    def deal(src, dst, start, end, order=None):
        order = order_s if order is None else order


        def step(i, carry):
            for p in range(M):
                for j in range(tiles):
                    t = p * groups + i * tiles + j
                    dst[:, pl.ds(multiple(t * LANES, LANES), LANES)] = src[
                        :, pl.ds(order[0, t] * LANES, LANES)
                    ]
            return carry

        lax.fori_loop(start, end, step, 0)

    with jax.named_scope("barrier"):
        entry = pltpu.get_barrier_semaphore()
        peers = [z_peer(o) for o in z_order] + [xy_peer(o) for o in xy_order] + [core_peer]
        for peer in peers:
            pl.semaphore_signal(entry, inc=1, device_id=peer, device_id_type=MESH)
        if packed:
            order_tiles()
        for load in loads[1:4]:
            load.wait()
        wb[c, q, m, 0:dr, :] = w1_v[...].astype(BF16)
        wb[c, q, m, dr : 2 * dr, :] = w2_v[...].astype(BF16)
        for t in range(6):
            tb[c, q, m, t * kb : (t + 1) * kb, :] = mem_v[t]
        pl.semaphore_wait(entry, len(peers))

    kinds_in = ((xb, x_recv, 0), (cb, c_recv, 1))

    def at_width(i, act):
        if not packed:
            act(w)
        elif isinstance(i, int):
            if i < KC:
                act(min(w, cap - i * w))
        elif cap % w == 0:
            pl.when(i < KC)(lambda: act(w))
        else:
            pl.when(i < KC - 1)(lambda: act(w))
            pl.when(i == KC - 1)(lambda: act(cap % w))

    def send_in(i, kinds=(0, 1)):
        here = pl.ds(multiple(m * F, F), F)

        def source(kind, to, width):
            if kind and packed:
                return cp.at[to, :, pl.ds(multiple(i * w, w), width)]
            hbm = xp if packed else (x_hbm, cot_hbm)[kind]
            return hbm.at[:, pl.ds(multiple(to * mine + i * w, w), width)]

        def start(kind, width):
            buf, sem, _ = kinds_in[kind]
            there = buf.at[here, pl.ds(multiple(i * w, w), width)]
            for o in z_order:
                to = flip(m, o)
                remote(source(kind, to, width), there, in_send.at[kind], sem.at[i], (d, to)).start()
            pltpu.make_async_copy(source(kind, m, width), there, own_sem.at[kind, i]).start()

        for kind in kinds:
            if kind:
                at_width(i, functools.partial(start, 1))
            else:
                start(0, w)

    others = (M - 1) * F

    def wait_in(i):
        def arrive(kind, width):
            buf, sem, _ = kinds_in[kind]
            part = buf.at[pl.ds(0, others), pl.ds(0, width)]
            remote(part, part, in_send.at[kind], sem.at[i], z_peer(1)).wait_recv()
            block = buf.at[pl.ds(0, F), pl.ds(0, width)]
            pltpu.make_async_copy(block, block, own_sem.at[kind, i]).wait()

        arrive(0, w)
        at_width(i, functools.partial(arrive, 1))

    def width_of(kind, i):
        return min(w, cap - i * w) if kind and packed else w

    def send_out(kind, i):
        col = pl.ds(multiple(i * w, w), width_of(kind, i))
        if kind and packed:
            there = igr.at[m, :, col]
        else:
            there = (lg_out, ig_out)[kind].at[:, pl.ds(multiple(m * mine + i * w, w), w)]
        buf = (lgb, igb)[kind]
        for o in z_order:
            to = flip(m, o)
            recv = out_recv.at[kind, o] if kind and packed else out_recv.at[kind, 0]
            remote(
                buf.at[pl.ds(multiple(to * F, F), F), col], there, out_send.at[kind, i], recv, (d, to)
            ).start()
        if not (kind and packed):
            pltpu.make_async_copy(buf.at[pl.ds(multiple(m * F, F), F), col], there, out_own.at[kind, i]).start()

    def wait_out(kind, i):
        buf = (lgb, igb)[kind]
        part = buf.at[pl.ds(0, others), pl.ds(0, width_of(kind, i))]
        remote(part, part, out_send.at[kind, i], out_recv.at[kind, 0], z_peer(1)).wait_send()
        if not (kind and packed):
            own = buf.at[pl.ds(0, F), pl.ds(0, w)]
            pltpu.make_async_copy(own, own, out_own.at[kind, i]).wait()

    line = lax.broadcasted_iota(jnp.int32, (w, LANES), 0).astype(F32)

    def matches(p, k, i):
        base = (k * w) * jnp.float32(1) if isinstance(k, int) else (k * w).astype(F32)
        parts = []
        for j in range(tiles):
            row = rk[pl.ds(p * groups + i * tiles + j, 1), :] - base
            parts.append(jnp.where(line == row, 1.0, 0.0).astype(BF16))
        return jnp.concatenate(parts, axis=1)

    spread_by = K // LEAST

    def pack_block(k, p):
        def step(i, acc):
            cols = pl.ds(multiple(p * mine + i * w, w), w)
            return acc + mm_t(cq[:, cols], matches(p, k, i))

        acc = lax.fori_loop(k, min(C, spread_by * k + spread_by), step, jnp.zeros((F, w), F32))
        cp[p, :, k * w : (k + 1) * w] = acc.astype(BF16)

    def shrink(k):
        with jax.named_scope("shrink"):
            end = min(C, spread_by * k + spread_by)

            def step(i, carry):
                st[:, pl.ds(multiple(i * w, w), w)] = matches(m, k, i)
                return carry

            lax.fori_loop(k, end, step, 0)
            part = slice(k * w, end * w)
            igb[:, k * w : (k + 1) * w] = mm_t(ig[:, part], st[:, part]).astype(BF16)

    def pack_chunk(k):
        with jax.named_scope("pack_cot"):

            def step(p, carry):
                pack_block(k, p)
                return carry

            lax.fori_loop(0, M, step, 0)

    def unpack_block(p):
        with jax.named_scope("unpack"):

            def chunk(i, carry):
                def step(k, acc):
                    return acc + mm(igr[p, :, pl.ds(multiple(k * w, w), w)], matches(p, k, i))

                acc = lax.fori_loop(i // spread_by, jnp.minimum(i, KC - 1) + 1, step, jnp.zeros((F, w), F32))
                xv[:, pl.ds(multiple(p * mine + i * w, w), w)] = acc.astype(BF16)
                return carry

            lax.fori_loop(0, C, chunk, 0)

    def unpack_from(o):
        part = igr.at[0, :, pl.ds(0, cap)]
        remote(part, part, in_send.at[0], out_recv.at[1, o], z_peer(o)).wait_recv()
        unpack_block(flip(m, o))

    if not packed:
        order_out[...] = jnp.zeros_like(order_out)
    def spread_z(bit, bufs, send, recv):
        for h in range(0, M, 2 * bit):
            slot, back = flip(m, h), flip(m, h + bit)
            for k, buf in enumerate(bufs):
                one, two = buf.at[c, q, slot], buf.at[c, q, back]
                sems = (send.at[k, h + bit], recv.at[k, h + bit], z_peer(bit))
                yield remote(one, one, *sems), remote(one, two, *sems)

    bufs = (wb, tb)
    first = list(spread_z(bits[-1], bufs, wz_send, wz_recv))
    for go, _ in first:
        go.start()
    send_in(0, (0,) if packed else (0, 1))
    if not packed:
        masks_to(mp)
        mk[...] = mp[...].astype(F32)
    else:
        deal(xv, xp, 1, C)
        to_seats = pltpu.make_async_copy(seats_v, seats_s, local_sem.at[17])
        to_seats.start()

        def deal_masks(t, carry):
            for j in range(8):
                mk[pl.ds(t * 8 + j, 1), :] = mp[pl.ds(order_s[0, t * 8 + j], 1), :].astype(F32)
            return carry

        lax.fori_loop(0, total_tiles // 8, deal_masks, 0)
        to_seats.wait()
        flags = mk[...]
        rows, cols = M * groups, LANES
        lower = lax.broadcasted_iota(jnp.int32, (cols, cols), 0) < lax.broadcasted_iota(jnp.int32, (cols, cols), 1)
        inside = mm(flags.astype(BF16), jnp.where(lower, 1.0, 0.0).astype(BF16))
        sums = jnp.broadcast_to(jnp.sum(flags, axis=1, keepdims=True), (rows, cols)).astype(BF16)
        one = lax.broadcasted_iota(jnp.int32, (rows, rows), 0)
        two = lax.broadcasted_iota(jnp.int32, (rows, rows), 1)
        ahead = (two < one) & (two >= one - one % groups)
        place_in = inside + mm(jnp.where(ahead, 1.0, 0.0).astype(BF16), sums)
        rk[...] = jnp.where(flags > 0.0, place_in, -1.0)
    def clear(i, carry):
        rows = pl.ds(multiple(i * ROWS, ROWS), ROWS)
        g1[rows, :] = jnp.zeros((ROWS, D), F32)
        g2t[rows, :] = jnp.zeros((ROWS, D), F32)
        for t in range(6):
            vec[t, rows, :] = jnp.zeros((ROWS, LANES), F32)
        return carry

    lax.fori_loop(0, blocks, clear, 0)
    stat[...] = jnp.zeros_like(stat)

    ahead_of = min(FIRST, C)
    if packed:
        loads[14].wait()
        deal(cv, cq, 0, C)
        if cap % w:
            cb[:, cap : KC * w] = jnp.zeros((D, KC * w - cap), BF16)
            for p in range(M):
                igr[p, :, cap : KC * w] = jnp.zeros((F, KC * w - cap), BF16)
        pack_chunk(0)

    def step_in(k):
        if packed:
            if k < KC:
                send_in(k, (1,))
            if k + 1 < ahead_of:
                send_in(k + 1, (0,))
            if k + 1 < KC:
                pack_chunk(k + 1)
        elif k + 1 < ahead_of:
            send_in(k + 1)

    with jax.named_scope("weights_z"):
        for bit in bits[::-1]:
            if bit != bits[-1]:
                first = list(spread_z(bit, bufs, wz_send, wz_recv))
                for go, _ in first:
                    go.start()
            if bit == bits[0]:
                step_in(0)
            for _, come in first:
                come.wait()
    with jax.named_scope("weights_xy"):
        for o in xy_order:
            for k, buf in enumerate(bufs):
                remote(buf.at[c, q], buf.at[c, q], wx_send.at[k, o], wx_recv.at[k, o], xy_peer(o)).start()
        step_in(1)
        step_in(2)
        for o in xy_order:
            for k, buf in enumerate(bufs):
                remote(buf.at[c, q], buf.at[c, flip(q, o)], wx_send.at[k, o], wx_recv.at[k, o], xy_peer(o)).wait()
    with jax.named_scope("weights_core"):
        for k, buf in enumerate(bufs):
            remote(buf.at[c], buf.at[c], wc_send.at[k], wc_recv.at[k], core_peer).start()
        for k in range(3, max(ahead_of, KC if packed else 0)):
            if k < ahead_of:
                step_in(k)
            elif k + 1 < KC:
                pack_chunk(k + 1)
        for k, buf in enumerate(bufs):
            remote(buf.at[c], buf.at[1 - c], wc_send.at[k], wc_recv.at[k], core_peer).wait()

    with jax.named_scope("weights_spread"):

        def place(i, carry):
            rows = pl.ds(multiple(i * dr, dr), dr)
            for j in range(M):
                cols = slice(j * F, (j + 1) * F)
                w1[rows, cols] = wb[i % 2, i // 2, j, 0:dr, :]
                w2t[rows, cols] = wb[i % 2, i // 2, j, dr : 2 * dr, :]
            return carry

        lax.fori_loop(0, N, place, 0)

        def turn(i, carry):
            here = pl.ds(multiple(i * LANES, LANES), LANES)
            for j in range(D // LANES):
                there = slice(j * LANES, (j + 1) * LANES)
                w1t[there, here] = w1[here, there].astype(F32).T.astype(BF16)
                w2[there, here] = w2t[here, there].astype(F32).T.astype(BF16)
            return carry

        lax.fori_loop(0, D // LANES, turn, 0)
        for t in range(6):
            for i in range(N):
                for j in range(M):
                    stage[t, i * kb : (i + 1) * kb, j * F : (j + 1) * F] = tb[
                        i % 2, i // 2, j, t * kb : (t + 1) * kb, :
                    ]

        def table(t, carry):
            for j in range(D // LANES):
                cols = slice(j * LANES, (j + 1) * LANES)
                piece = stage[t, :, cols]
                tab[t, cols, :] = jnp.concatenate([piece] * per_mask, axis=0).T
            return carry

        lax.fori_loop(0, 6, table, 0)

    def eight(value):
        return value.reshape(ROWS // 8, 8, LANES).sum(0)

    if packed:
        early = [(C - 3, [(0, 0)]), (C - 2, [(0, 1)]), (C - 1, [(0, 2)])]
    else:
        early = [(C - 2, [(0, 0), (1, 0)]), (C - 1, [(0, 1), (1, 1)])]

    def work(i, carry):
        col = multiple(i * w, w)
        with jax.named_scope("wait_in"):
            wait_in(i)

        @pl.when((i + AHEAD >= FIRST) & (i + AHEAD < C - 1))
        def _():
            send_in(i + AHEAD)

        if C > FIRST:

            @pl.when(i + AHEAD == C - 2)
            def _():
                send_in(C - 1)

        for late, parts in early:
            for kind, k in parts:
                pl.when(i == late)(functools.partial(send_out, kind, k))

        masks = [mk[pl.ds(m * groups + i * tiles + j, 1), :] for j in range(tiles)]

        def place_of(r):
            return pl.ds(multiple(r * ROWS, ROWS), ROWS)

        def lanes_of(j):
            return pl.ds(multiple(col + j * LANES, LANES), LANES)

        def scale_rows(r, sums):
            rows = place_of(r)
            row_in = tab[0, rows, :]
            new = []
            for j in range(tiles):
                x = xb[rows, lanes_of(j)].astype(F32)
                sc[rows, j * LANES : (j + 1) * LANES] = (x * row_in).astype(BF16)
                new.append(sums[j] + eight(x * x))
            return tuple(new)

        zero = tuple(jnp.zeros((8, LANES), F32) for _ in range(tiles))
        with jax.named_scope("scale"):
            x_sums = lax.fori_loop(0, blocks, scale_rows, zero)
        with jax.named_scope("mm_one"):
            hp[...] = mm(w1t[...], sc[...])

        def curve_rows(r, carry):
            rows = place_of(r)
            gain, bias, row_mid = tab[1, rows, :], tab[2, rows, :], tab[3, rows, :]
            for j in range(tiles):
                cols = slice(j * LANES, (j + 1) * LANES)
                s = hp[rows, cols] * gain + bias
                s2 = s * s
                th = jnp.tanh(curve_a * (s + curve_b * (s2 * s)))
                cdf = 0.5 * (1.0 + th)
                h = s * cdf
                slope = cdf + (0.5 * s) * (1.0 - th * th) * (curve_a + (3.0 * curve_a * curve_b) * s2)
                hid[rows, cols] = h
                dgm[rows, cols] = slope * row_mid
                hi[rows, cols] = (h * row_mid).astype(BF16)
            return carry

        with jax.named_scope("curve"):
            lax.fori_loop(0, blocks, curve_rows, 0)
        with jax.named_scope("mm_two"):
            prod[...] = mm(w2t[...], hi[...])
        low, high_k = i // spread_by, jnp.minimum(i, KC - 1)
        if packed:
            with jax.named_scope("expand"):

                def grow(k, carry):
                    cx[...] += mm(cb[:, pl.ds(multiple(k * w, w), w)], matches(m, k, i))
                    return carry

                cx[...] = jnp.zeros_like(cx)
                lax.fori_loop(low, high_k + 1, grow, 0)

        def grad_of(rows, j):
            if packed:
                return cx[rows, j * LANES : (j + 1) * LANES]
            return cb[rows, lanes_of(j)].astype(F32) * masks[j]


        def out_rows(r, sums):
            rows = place_of(r)
            gain, bias = tab[4, rows, :], tab[5, rows, :]
            v4, v5 = vec[4, rows, :], vec[5, rows, :]
            new = []
            for j in range(tiles):
                cols = slice(j * LANES, (j + 1) * LANES)
                x = xb[rows, lanes_of(j)].astype(F32)
                projected = prod[rows, cols]
                branch = projected * gain + bias
                lgb[rows, lanes_of(j)] = (x + branch).astype(BF16)
                new.append(sums[j] + eight(branch * branch))
                go = grad_of(rows, j)
                v5 = v5 + go
                v4 = v4 + go * projected
                gp[rows, cols] = (go * gain).astype(BF16)
            vec[4, rows, :] = v4
            vec[5, rows, :] = v5
            return tuple(new)

        with jax.named_scope("out"):
            b_sums = lax.fori_loop(0, blocks, out_rows, zero)
        for j in range(tiles):
            stat[0:8, :] += x_sums[j] * masks[j]
            stat[8:16, :] += b_sums[j] * masks[j]

        with jax.named_scope("mm_three"):
            half = D // 2
            for k in range(2):
                part = slice(k * half, (k + 1) * half)
                g2t[part, :] += mm_t(gp[part, :], hi[...])
            prod[...] = mm(w2[...], gp[...])

        def back_rows(r, carry):
            rows = place_of(r)
            gain = tab[1, rows, :]
            v1, v2, v3 = vec[1, rows, :], vec[2, rows, :], vec[3, rows, :]
            for j in range(tiles):
                cols = slice(j * LANES, (j + 1) * LANES)
                gh = prod[rows, cols]
                v3 = v3 + gh * hid[rows, cols]
                gs = gh * dgm[rows, cols]
                v2 = v2 + gs
                v1 = v1 + gs * hp[rows, cols]
                gpre[rows, cols] = (gs * gain).astype(BF16)
            vec[1, rows, :] = v1
            vec[2, rows, :] = v2
            vec[3, rows, :] = v3
            return carry

        with jax.named_scope("back"):
            lax.fori_loop(0, blocks, back_rows, 0)
        with jax.named_scope("mm_four"):
            for k in range(2):
                part = slice(k * half, (k + 1) * half)
                g1[part, :] += mm_t(sc[part, :], gpre[...])
            prod[...] = mm(w1[...], gpre[...])

        def in_rows(r, carry):
            rows = place_of(r)
            row_in = tab[0, rows, :]
            v0 = vec[0, rows, :]
            for j in range(tiles):
                cols = slice(j * LANES, (j + 1) * LANES)
                gs = prod[rows, cols]
                v0 = v0 + gs * xb[rows, lanes_of(j)].astype(F32)
                go = grad_of(rows, j)
                done = (gs * row_in + go).astype(BF16)
                if packed:
                    ig[rows, lanes_of(j)] = done
                else:
                    igb[rows, lanes_of(j)] = done
            vec[0, rows, :] = v0
            return carry

        with jax.named_scope("in"):
            lax.fori_loop(0, blocks, in_rows, 0)
        if packed:
            xv[:, pl.ds(multiple(m * mine + col, w), w)] = ig[pl.ds(multiple(m * F, F), F), pl.ds(col, w)]
        return carry

    lax.fori_loop(0, C, work, 0)

    items = [item for _, parts in early for item in parts]
    already = len(items)
    if packed:
        items += [(1, k) for k in range(KC)] + [(0, i) for i in range(3, C)]
    else:
        items += [(kind, i) for i in range(2, C) for kind in range(2)]
    state = {"sent": already, "done": 0}

    def pump(count, most=OUT):
        with jax.named_scope("pump"):
            for _ in range(count):
                if state["sent"] < len(items):
                    while state["sent"] - state["done"] >= most:
                        wait_out(*items[state["done"]])
                        state["done"] += 1
                    kind, k = items[state["sent"]]
                    if kind and packed:
                        shrink(k)
                    send_out(kind, k)
                    state["sent"] += 1


    with jax.named_scope("pack"):

        def pack_g(i, carry):
            rows = pl.ds(multiple(i * dr, dr), dr)
            for j in range(M):
                cols = slice(j * F, (j + 1) * F)
                gb[i % 2, i // 2, j, 0:dr, :] = g1[rows, cols]
                gb[i % 2, i // 2, j, dr : 2 * dr, :] = g2t[rows, cols]
            return carry

        lax.fori_loop(0, N, pack_g, 0)

        def fold(t, carry):
            for j in range(D // LANES):
                cols = slice(j * LANES, (j + 1) * LANES)
                turned = vec[t, cols, :].T
                vt[t, :, cols] = sum(turned[k * K : (k + 1) * K, :] for k in range(per_mask))
            return carry

        lax.fori_loop(0, 6, fold, 0)
        for t in range(6):
            for i in range(N):
                for j in range(M):
                    row = 2 * dr + t * kb
                    gb[i % 2, i // 2, j, row : row + kb, :] = vt[t, i * kb : (i + 1) * kb, j * F : (j + 1) * F]
        own = mk[pl.ds(multiple(m * groups, groups), groups), :]
        totals = [stat[0:8, :], stat[8:16, :], own]
        rows8 = [jnp.sum(v, keepdims=True).reshape(1, 1) for v in totals]
        rows8.append(jnp.where(rows8[2] > cap, 1.0, 0.0))
        row_id = lax.broadcasted_iota(jnp.int32, (8, F), 0)
        lines = sum(jnp.where(row_id == k, v, 0.0) for k, v in enumerate(rows8))

        def put(i, carry):
            for j in range(M):
                gb[i % 2, i // 2, j, 2 * dr + tr : pr, :] = lines
            return carry

        lax.fori_loop(0, N, put, 0)

    with jax.named_scope("sum_core"):
        for o in xy_order + [0]:
            k = flip(q, o)
            remote(gb.at[1 - c, k], rcore.at[k], gc_send.at[o], gc_recv.at[o], core_peer).start()

        def add_core(k):
            def step(j, carry):
                gb[c, k, j] += rcore[k, j]
                return carry

            lax.fori_loop(0, M, step, 0)

        def over_xy(o):
            k = flip(q, o)
            sems = [(gx_send.at[n, o], gx_recv.at[n, o], xy_peer(o)) for n in range(2)]
            tail = gb.at[c, k, :, pl.ds(2 * dr, pr - 2 * dr), :]
            return remote(xs.at[o], rxg.at[o], *sems[0]), remote(tail, rxv.at[o], *sems[1])

        for o in xy_order + [0]:
            k = flip(q, o)
            remote(gb.at[1 - c, k], rcore.at[k], gc_send.at[o], gc_recv.at[o], core_peer).wait()
            add_core(k)
            if o:

                def round_piece(j, carry):
                    xs[o, j] = gb[c, k, j, 0 : 2 * dr, :].astype(BF16)
                    return carry

                lax.fori_loop(0, M, round_piece, 0)
                for copy in over_xy(o):
                    copy.start()
    pump(2)
    with jax.named_scope("sum_xy"):
        for o in xy_order:
            for copy in over_xy(o):
                copy.wait()

            def step(j, carry):
                gb[c, q, j, 0 : 2 * dr, :] += rxg[o, j].astype(F32)
                gb[c, q, j, 2 * dr : pr, :] += rxv[o, j]
                return carry

            lax.fori_loop(0, M, step, 0)
    with jax.named_scope("sum_z"):
        slot = 0
        for bit in bits:
            moves = []
            for h in range(0, M, 2 * bit):
                away = flip(m, h + bit)
                zs[slot] = gb[c, q, away, 0 : 2 * dr, :].astype(BF16)
                sems = [(gz_send.at[k, slot], gz_recv.at[k, slot], z_peer(bit)) for k in range(2)]
                tail = gb.at[c, q, away, pl.ds(2 * dr, pr - 2 * dr), :]
                moves.append((slot, h, remote(zs.at[slot], rzg.at[slot], *sems[0]), remote(tail, rzv.at[slot], *sems[1])))
                slot += 1
            for _, _, one, two in moves:
                one.start()
                two.start()
            pump(1)
            for k, h, one, two in moves:
                keep = flip(m, h)
                one.wait()
                two.wait()
                gb[c, q, keep, 0 : 2 * dr, :] += rzg[k].astype(F32)
                gb[c, q, keep, 2 * dr : pr, :] += rzv[k]
            pump(1)

    total = gb[c, q, m]
    ga[c, q, m] = total[0 : 2 * dr, :].astype(BF16)
    with jax.named_scope("spread_z"):
        first = list(spread_z(bits[-1], (ga,), az_send, az_recv))
        for go, _ in first:
            go.start()
        pump(1)
        for load in loads[4:14]:
            load.wait()
        g1_out[...] = total[0:dr, :]
        g2_out[...] = total[dr : 2 * dr, :]
        corr_one = 1.0 - beta_first**STEP
        corr_two = 1.0 - beta_second**STEP
        for t in range(6):
            row = 2 * dr + t * kb
            grad = total[row : row + kb, :]
            one = beta_first * m1_v[t] + (1.0 - beta_first) * grad
            two = beta_second * m2_v[t] + (1.0 - beta_second) * grad * grad
            m1_out[t] = one
            m2_out[t] = two
            mem_out[t] = mem_v[t] - adam_rate * (one / corr_one) / (jnp.sqrt(two / corr_two) + adam_eps)
        sums_out[...] = total[2 * dr + tr : pr, 0:LANES if F >= LANES else F]
        for bit in bits[::-1]:
            if bit != bits[-1]:
                pump(1)
                first = list(spread_z(bit, (ga,), az_send, az_recv))
                for go, _ in first:
                    go.start()
            if bit == bits[0]:
                pump(len(items), len(items))
            if packed and bit == bits[0]:
                for o in z_order[:-1]:
                    unpack_from(o)
            for _, come in first:
                come.wait()
    with jax.named_scope("spread_xy"):
        for o in xy_order:
            remote(ga.at[c, q], ga.at[c, q], ax_send.at[o], ax_recv.at[o], xy_peer(o)).start()
        if packed:
            for o in z_order[-1:]:
                unpack_from(o)
            with jax.named_scope("settle"):
                deal(xv, ig_out, 0, C, seats_s)
        for o in xy_order:
            remote(ga.at[c, q], ga.at[c, flip(q, o)], ax_send.at[o], ax_recv.at[o], xy_peer(o)).wait()
    with jax.named_scope("spread_core"):
        remote(ga.at[c], ga.at[c], ac_send, ac_recv, core_peer).start()
        remote(ga.at[c], ga.at[1 - c], ac_send, ac_recv, core_peer).wait()
    with jax.named_scope("shampoo"):

        def place_g(i, carry):
            rows = pl.ds(multiple(i * dr, dr), dr)
            for j in range(M):
                cols = slice(j * F, (j + 1) * F)
                g1f[rows, cols] = ga[i % 2, i // 2, j, 0:dr, :]
                g2ft[rows, cols] = ga[i % 2, i // 2, j, dr : 2 * dr, :]
            return carry

        lax.fori_loop(0, N, place_g, 0)

        def turn_g(i, carry):
            here = pl.ds(multiple(i * LANES, LANES), LANES)
            for j in range(D // LANES):
                there = slice(j * LANES, (j + 1) * LANES)
                g1ft[there, here] = g1f[here, there].astype(F32).T.astype(BF16)
                g2f[there, here] = g2ft[here, there].astype(F32).T.astype(BF16)
            return carry

        lax.fori_loop(0, D // LANES, turn_g, 0)
        by_d = pl.ds(multiple(d * dr, dr), dr)
        by_m = pl.ds(multiple(m * F, F), F)

        def renewed(old, fresh):
            return stat_decay * old + (1.0 - stat_decay) * fresh

        l1_out[...] = renewed(l1_v[...], mm_t(g1f[by_d, :], g1f[by_m, :]))
        r1_out[...] = renewed(r1_v[...], mm_t(g1ft[by_d, :], g1ft[by_m, :]))
        l2_out[...] = renewed(l2_v[...], mm_t(g2f[by_d, :], g2f[by_m, :]))
        r2_out[...] = renewed(r2_v[...], mm_t(g2ft[by_d, :], g2ft[by_m, :]))

        def stepped(weight, left, grad, right):
            inner = jnp.dot(left[...], grad[...].astype(F32), precision=high, preferred_element_type=F32)
            return weight[...] - shampoo_rate * mm_t(inner, right[...], high)

        w1_out[...] = stepped(w1_v, p1_v, g1f, q1_v)
        w2_out[...] = stepped(w2_v, q2_v, g2ft, p2_v)

    with jax.named_scope("drain"):
        while state["done"] < len(items):
            wait_out(*items[state["done"]])
            state["done"] += 1
        for kind, out in enumerate((lg_out,) if packed else (lg_out, ig_out)):
            part = out.at[:, pl.ds(0, (M - 1) * mine)]
            remote(part, part, in_send.at[kind], out_recv.at[kind, 0], z_peer(1)).wait_recv()
        for kind, buf in enumerate((xb, cb)):
            part = buf.at[pl.ds(0, others), pl.ds(0, (mine, cap)[kind])]
            remote(part, part, in_send.at[kind], out_recv.at[0, 0], z_peer(1)).wait_send()


def finish(n_out, D, tiles, sums_ref, order_ref, *refs):
    outs = refs[n_out : 2 * n_out]
    rms_out, flag_out, order_s, rms_s, flag_s, sems = refs[2 * n_out :]
    copies = [pltpu.make_async_copy(refs[i], outs[i], sems.at[i]) for i in range(n_out)]
    if tiles:
        order = pltpu.make_async_copy(order_ref, order_s, sems.at[n_out])
        order.start()
    for copy in copies[1 if tiles else 0 :]:
        copy.start()
    sums = sums_ref[...]
    ratio = jnp.sqrt(sums / (sums[2:3, :] * D))
    rms_s[0] = ratio[0, 0]
    rms_s[1] = ratio[1, 0]
    flag_s[0] = jnp.where(sums[3, 0] > 0.0, 1, 0)
    for k, (src, dst) in enumerate(((rms_s, rms_out), (flag_s, flag_out))):
        copies.append(pltpu.make_async_copy(src, dst, sems.at[n_out + 1 + k]))
        copies[-1].start()
    if tiles:
        order.wait()

        def step(g, carry):
            for j in range(8):
                t = g * 8 + j
                here = pl.ds(multiple(t * LANES, LANES), LANES)
                there = pl.ds(multiple(order_s[0, t] * LANES, LANES), LANES)
                pltpu.make_async_copy(refs[0].at[:, here], outs[0].at[:, there], sems.at[0]).start()
            return carry

        lax.fori_loop(0, tiles // 8, step, 0)
    for copy in copies:
        copy.wait()


def solution(mesh):
    N, M = mesh.shape["dp"], mesh.shape["mp"]
    Q = N // 2

    def on_device(*args):
        x, cot, mask, members, m1, m2, w1, w2, l1, r1, l2, r2, p1, q1, p2, q2 = args
        mask, w2, l2, r2 = mask.T, w2.T, l2.T, r2.T
        args = (x, cot, mask, members, m1, m2, w1, w2, l1, r1, l2, r2, p1, q1, p2, q2)
        F, R = x.shape
        D = F * M
        mine = R // M
        w = min(CHUNK, mine)
        C = mine // w
        kb = members.shape[1]
        dr = w1.shape[0]
        tr = -(-6 * kb // 8) * 8
        pr = 2 * dr + tr + 8
        groups = mine // LANES
        S = jax.ShapeDtypeStruct
        V = pltpu.VMEM
        dma = pltpu.SemaphoreType.DMA
        outs = [S(x.shape, BF16), S(x.shape, BF16), S((8, min(F, LANES)), F32), S((1, LANES), jnp.int32)]
        outs += [S(a.shape, F32) for a in (w1, w1, l1, r1, w2, w2, l2, r2, m1, m2, members)]
        anywhere = pl.BlockSpec(memory_space=pl.ANY)
        vmem = pl.BlockSpec(memory_space=pltpu.VMEM)

        def run(cap, number):
            packed = cap < mine
            KC = -(-cap // w)

            def only(shape, dtype):
                return V(shape if packed else (16, LANES), dtype)

            scratch = [V(a.shape, a.dtype) for a in (mask, members, m1, m2, w1, w2, l1, r1, l2, r2, p1, q1, p2, q2)]
            scratch += [only((F, R), BF16)] * 4
            scratch += [V((1, LANES), jnp.int32), pltpu.SMEM((1, LANES), jnp.int32)]
            scratch += [V((1, LANES), jnp.int32), pltpu.SMEM((1, LANES), jnp.int32)]
            scratch += [only((M, F, KC * w), BF16), only((w, mine), BF16), only((M, F, KC * w), BF16)]
            scratch += [V((D, mine), BF16), V((D, KC * w), BF16), V((D, mine), BF16), V((D, KC * w), BF16)]
            scratch += [V((2, Q, M, 2 * dr, F), BF16), V((2, Q, M, tr, F), F32)]
            scratch += [V((D, D), BF16)] * 4
            scratch += [V((6, D, LANES), F32), V((6, K, D), F32), V(mask.shape[::-1], jnp.int32)]
            scratch += [V((M * groups, LANES), jnp.int32)] + [V((M * groups, LANES), F32)] * 2
            scratch += [V((D, w), F32)] * 4
            scratch += [V((D, w), BF16)] * 4
            scratch += [only((D, w), F32), only((D, mine), BF16)]
            scratch += [V((D, D), F32)] * 2
            scratch += [V((6, D, LANES), F32), V((6, K, D), F32), V((16, LANES), F32)]
            scratch += [V((2, Q, M, pr, F), F32), V((Q, M, pr, F), F32)]
            scratch += [V((Q, M, 2 * dr, F), BF16), V((Q, M, 2 * dr, F), BF16), V((Q, M, pr - 2 * dr, F), F32)]
            scratch += [V((M - 1, 2 * dr, F), BF16), V((M - 1, pr - 2 * dr, F), F32), V((M - 1, 2 * dr, F), BF16)]
            scratch += [V((2, Q, M, 2 * dr, F), BF16)]
            scratch += [V((D, D), BF16)] * 4
            scratch += [dma((18,)), dma((2,)), dma((C,)), dma((C,)), dma((2, C)), dma((2, C)), dma((2, C)), dma((2, M))]
            scratch += [dma((2, M)), dma((2, M)), dma((2, Q)), dma((2, Q)), dma((2,)), dma((2,))]
            scratch += [dma((Q,)), dma((Q,)), dma((2, Q)), dma((2, Q)), dma((2, M)), dma((2, M))]
            scratch += [dma((1, M)), dma((1, M)), dma((Q,)), dma((Q,)), dma, dma]
            res = pl.pallas_call(
                functools.partial(kernel, N, M, cap),
                out_shape=[V(a.shape, a.dtype) for a in outs],
                in_specs=[anywhere] * 16,
                out_specs=[vmem] * 15,
                scratch_shapes=scratch,
                compiler_params=pltpu.CompilerParams(
                    collective_id=number, has_side_effects=True, vmem_limit_bytes=46 << 20
                ),
                name="packed" if packed else "whole",
            )(*[pltpu.with_memory_space_constraint(a, pltpu.HBM) for a in args])
            kept = [*res[:2], *res[4:]]
            *done, rms, flag = pl.pallas_call(
                functools.partial(finish, len(kept), D, M * groups if packed else 0),
                out_shape=[S(a.shape, a.dtype) for a in kept] + [S((2,), F32), S((1,), jnp.int32)],
                in_specs=[vmem, anywhere] + [anywhere] * len(kept),
                out_specs=[anywhere] * (len(kept) + 2),
                scratch_shapes=[
                    pltpu.SMEM((1, LANES), jnp.int32),
                    pltpu.SMEM((2,), F32),
                    pltpu.SMEM((1,), jnp.int32),
                    dma((len(kept) + 3,)),
                ],
                compiler_params=pltpu.CompilerParams(vmem_limit_bytes=16 << 20),
                name="finish",
            )(res[2], res[3], *kept)
            return flag, (*done, rms)

        flag, fast = run(-(-mine * 11 // (16 * LANES)) * LANES, 0)
        done = lax.cond(flag[0] > 0, lambda: run(mine, 1)[1], lambda: fast)
        logits, igrad, g1, n1, l1, r1, g2, n2, l2, r2, m1, m2, new, rms = done
        return (logits, igrad, rms, g1, n1, l1, r1, g2.T, n2.T, l2.T, r2.T, m1, m2, new)

    placed = (
        P("mp", "dp"),
        P("mp", "dp"),
        P("dp", None),
        P(None, "dp", "mp"),
        P(None, "dp", "mp"),
        P(None, "dp", "mp"),
        P("dp", "mp"),
        P("mp", "dp"),
        P("dp", "mp"),
        P("dp", "mp"),
        P("mp", "dp"),
        P("mp", "dp"),
        P("dp", None),
        P("mp", None),
        P("mp", None),
        P("dp", None),
    )
    return jax.shard_map(
        on_device,
        mesh=mesh,
        in_specs=placed,
        out_specs=(
            P("mp", "dp"),
            P("mp", "dp"),
            P(),
            P("dp", "mp"),
            P("dp", "mp"),
            P("dp", "mp"),
            P("dp", "mp"),
            P("mp", "dp"),
            P("mp", "dp"),
            P("mp", "dp"),
            P("mp", "dp"),
            P(None, "dp", "mp"),
            P(None, "dp", "mp"),
            P(None, "dp", "mp"),
        ),
        check_vma=False,
    )
```

```python
import functools

import jax
import jax.numpy as jnp
from jax import lax
from jax.experimental import pallas as pl
from jax.experimental.pallas import tpu as pltpu
from jax.sharding import PartitionSpec as P

K = 32
STEP = 10
LANES = 128
CHUNK = 256
ROWS = 32
AHEAD = 2
FIRST = 4
LEAST = 8

beta_first = 0.9
beta_second = 0.999
adam_eps = 1e-08
adam_rate = 0.2
stat_decay = 0.95
shampoo_rate = 1.0
curve_a = 0.7978845608028654
curve_b = 0.044715

MESH = pl.DeviceIdType.MESH
F32 = jnp.float32
BF16 = jnp.bfloat16
over_lanes = (((1,), (1,)), ((), ()))


def flip(index, mask):
    bit = 1
    while bit <= mask:
        if mask & bit:
            index = index + bit - 2 * bit * ((index // bit) % 2)
        bit *= 2
    return index


def mm(a, b):
    return jnp.dot(a, b, preferred_element_type=F32)


def mm_t(a, b, precision=None):
    return lax.dot_general(a, b, over_lanes, precision=precision, preferred_element_type=F32)


def multiple(value, by):
    return pl.multiple_of(value, by)


def kernel(
    N,
    M,
    cap,
    x_hbm,
    cot_hbm,
    mask_hbm,
    mem_hbm,
    m1_hbm,
    m2_hbm,
    w1_hbm,
    w2_hbm,
    l1_hbm,
    r1_hbm,
    l2_hbm,
    r2_hbm,
    p1_hbm,
    q1_hbm,
    p2_hbm,
    q2_hbm,
    lg_out,
    ig_out,
    sums_out,
    order_out,
    g1_out,
    w1_out,
    l1_out,
    r1_out,
    g2_out,
    w2_out,
    l2_out,
    r2_out,
    m1_out,
    m2_out,
    mem_out,
    mask_v,
    mem_v,
    m1_v,
    m2_v,
    w1_v,
    w2_v,
    l1_v,
    r1_v,
    l2_v,
    r2_v,
    p1_v,
    q1_v,
    p2_v,
    q2_v,
    xv,
    xp,
    cv,
    cq,
    order_v,
    order_s,
    seats_v,
    seats_s,
    cp,
    st,
    igr,
    xb,
    cb,
    lgb,
    igb,
    wb,
    tb,
    w1,
    w1t,
    w2,
    w2t,
    tab,
    stage,
    mt,
    mp,
    mk,
    rk,
    hp,
    hid,
    dgm,
    prod,
    sc,
    hi,
    gp,
    gpre,
    cx,
    ig,
    g1,
    g2t,
    vec,
    vt,
    stat,
    gb,
    rcore,
    xs,
    rxg,
    rxv,
    rzg,
    rzv,
    zs,
    ga,
    g1f,
    g1ft,
    g2f,
    g2ft,
    local_sem,
    in_send,
    in_recv,
    out_send,
    out_recv,
    wz_send,
    wz_recv,
    wx_send,
    wx_recv,
    wc_send,
    wc_recv,
    gc_send,
    gc_recv,
    gx_send,
    gx_recv,
    gz_send,
    gz_recv,
    az_send,
    az_recv,
    ax_send,
    ax_recv,
    ac_send,
    ac_recv,
):
    F, R = x_hbm.shape
    D = F * M
    Q = N // 2
    mine = R // M
    w = min(CHUNK, mine)
    C = mine // w
    tiles = w // LANES
    packed = cap < mine
    KC = -(-cap // w)
    groups = mine // LANES
    kb = K // N
    dr = D // N
    tr = tb.shape[3]
    pr = gb.shape[3]
    blocks = D // ROWS
    high = lax.Precision.HIGHEST

    d, m = lax.axis_index("dp"), lax.axis_index("mp")
    c, q = d % 2, d // 2

    def z_peer(o):
        return (d, flip(m, o))

    def xy_peer(o):
        return (flip(q, o) * 2 + c, m)

    core_peer = (flip(d, 1), m)
    z_order = sorted(range(1, M), reverse=True)
    bits = [1 << k for k in range(M.bit_length() - 1)]
    xy_order = sorted(range(1, Q), reverse=True)

    def remote(src, dst, send, recv, peer):
        return pltpu.make_async_remote_copy(
            src_ref=src, dst_ref=dst, send_sem=send, recv_sem=recv, device_id=peer, device_id_type=MESH
        )

    pairs = (
        (mask_hbm, mask_v),
        (mem_hbm, mem_v),
        (w1_hbm, w1_v),
        (w2_hbm, w2_v),
        (m1_hbm, m1_v),
        (m2_hbm, m2_v),
        (l1_hbm, l1_v),
        (r1_hbm, r1_v),
        (l2_hbm, l2_v),
        (r2_hbm, r2_v),
        (p1_hbm, p1_v),
        (q1_hbm, q1_v),
        (p2_hbm, p2_v),
        (q2_hbm, q2_v),
    )
    if packed:
        pairs = (*pairs, (cot_hbm, cv), (x_hbm, xv))
    loads = [pltpu.make_async_copy(a, b, local_sem.at[i]) for i, (a, b) in enumerate(pairs)]
    for load in loads:
        load.start()

    per_mask = LANES // K
    total_tiles = M * groups

    I32 = jnp.int32

    def masks_to(ref):
        loads[0].wait()
        mt[...] = mask_v[...].T
        ref[...] = jnp.concatenate(
            [mt[pl.ds(j, total_tiles, stride=per_mask), :] for j in range(per_mask)], axis=1
        )

    def across(row):
        return jnp.broadcast_to(row, (LANES, LANES)).T

    def order_tiles():
        masks_to(mp)
        tall = jnp.concatenate([mp[...], jnp.zeros((LANES - total_tiles, LANES), I32)], axis=0)
        count = jnp.sum(tall.T, axis=0, keepdims=True)
        line_id = lax.broadcasted_iota(I32, (LANES, LANES), 0)
        lane_id = lax.broadcasted_iota(I32, (LANES, LANES), 1)
        mine_here, other = jnp.broadcast_to(count, (LANES, LANES)), across(count)
        before = (other > mine_here) | ((other == mine_here) & (line_id < lane_id))
        dealt = (line_id < total_tiles) & (line_id % groups != 0)
        rank = jnp.sum(jnp.where(before & dealt, 1, 0), axis=0, keepdims=True)
        turn, seat = rank // M, rank % M
        block = jnp.where(turn % 2 == 0, seat, M - 1 - seat)
        lane = lax.broadcasted_iota(I32, (1, LANES), 1)
        seats = jnp.where(lane % groups == 0, lane, block * groups + 1 + turn)
        seats = jnp.where(lane < total_tiles, seats, LANES)
        seats_v[...] = seats
        order_v[...] = jnp.sum(jnp.where(across(seats) == lane_id, line_id, 0), axis=0, keepdims=True)
        order_out[...] = order_v[...]
        to_scalars = pltpu.make_async_copy(order_v, order_s, local_sem.at[16])
        to_scalars.start()
        loads[15].wait()
        to_scalars.wait()
        deal(xv, xp, 0, 1)

    def deal(src, dst, start, end, order=None):
        order = order_s if order is None else order


        def step(i, carry):
            for p in range(M):
                for j in range(tiles):
                    t = p * groups + i * tiles + j
                    dst[:, pl.ds(multiple(t * LANES, LANES), LANES)] = src[
                        :, pl.ds(order[0, t] * LANES, LANES)
                    ]
            return carry

        lax.fori_loop(start, end, step, 0)

    with jax.named_scope("barrier"):
        entry = pltpu.get_barrier_semaphore()
        peers = [z_peer(o) for o in z_order] + [xy_peer(o) for o in xy_order] + [core_peer]
        for peer in peers:
            pl.semaphore_signal(entry, inc=1, device_id=peer, device_id_type=MESH)
        for load in loads[1:4]:
            load.wait()
        wb[c, q, m, 0:dr, :] = w1_v[...].astype(BF16)
        wb[c, q, m, dr : 2 * dr, :] = w2_v[...].astype(BF16)
        for t in range(6):
            tb[c, q, m, t * kb : (t + 1) * kb, :] = mem_v[t]
        pl.semaphore_wait(entry, len(peers))

    kinds_in = (xb, cb)

    def at_width(i, act):
        if not packed:
            act(w)
        elif isinstance(i, int):
            if i < KC:
                act(min(w, cap - i * w))
        elif cap % w == 0:
            pl.when(i < KC)(lambda: act(w))
        else:
            pl.when(i < KC - 1)(lambda: act(w))
            pl.when(i == KC - 1)(lambda: act(cap % w))

    def send_tile(j, src):
        here = pl.ds(multiple(m * F, F), F)
        there = xb.at[here, j * LANES : (j + 1) * LANES]

        def tile(to):
            return src.at[:, pl.ds(multiple(to * mine + j * LANES, LANES), LANES)]

        for o in z_order:
            to = flip(m, o)
            remote(tile(to), there, in_send.at[0], in_recv.at[0], (d, to)).start()
        pltpu.make_async_copy(tile(m), there, in_recv.at[0]).start()

    def send_in(i, kinds=(0, 1)):
        here = pl.ds(multiple(m * F, F), F)

        def source(kind, to, width):
            if kind and packed:
                return cp.at[to, :, pl.ds(multiple(i * w, w), width)]
            hbm = xp if packed else (x_hbm, cot_hbm)[kind]
            return hbm.at[:, pl.ds(multiple(to * mine + i * w, w), width)]

        def start(kind, width):
            there = kinds_in[kind].at[here, pl.ds(multiple(i * w, w), width)]
            for o in z_order:
                to = flip(m, o)
                remote(source(kind, to, width), there, in_send.at[kind], in_recv.at[i], (d, to)).start()
            pltpu.make_async_copy(source(kind, m, width), there, in_recv.at[i]).start()

        for kind in kinds:
            if kind:
                at_width(i, functools.partial(start, 1))
            else:
                start(0, w)

    others = (M - 1) * F

    def wait_in(i):
        def arrive(width):
            part = xb.at[:, pl.ds(0, w + width)]
            remote(part, part, in_send.at[0], in_recv.at[i], z_peer(1)).wait_recv()

        at_width(i, arrive)
        if packed:
            pl.when(i >= KC)(lambda: arrive(0))

    def width_of(kind, i):
        return min(w, cap - i * w) if kind and packed else w

    def send_out(kind, i):
        col = pl.ds(multiple(i * w, w), width_of(kind, i))
        if kind and packed:
            there = igr.at[m, :, col]
        else:
            there = (lg_out, ig_out)[kind].at[:, pl.ds(multiple(m * mine + i * w, w), w)]
        buf = (lgb, igb)[kind]
        for o in z_order:
            to = flip(m, o)
            recv = out_recv.at[kind, o] if kind and packed else out_recv.at[kind, 0]
            remote(buf.at[pl.ds(multiple(to * F, F), F), col], there, out_send.at[kind], recv, (d, to)).start()
        if not (kind and packed):
            pltpu.make_async_copy(buf.at[pl.ds(multiple(m * F, F), F), col], there, out_recv.at[kind, 0]).start()

    line = lax.broadcasted_iota(jnp.int32, (w, LANES), 0).astype(F32)

    def matches(p, k, i):
        base = (k * w) * jnp.float32(1) if isinstance(k, int) else (k * w).astype(F32)
        parts = []
        for j in range(tiles):
            row = rk[pl.ds(p * groups + i * tiles + j, 1), :] - base
            parts.append(jnp.where(line == row, 1.0, 0.0).astype(BF16))
        return jnp.concatenate(parts, axis=1)

    spread_by = K // LEAST

    def pack_block(k, p):
        def step(i, acc):
            cols = pl.ds(multiple(p * mine + i * w, w), w)
            return acc + mm_t(cq[:, cols], matches(p, k, i))

        acc = lax.fori_loop(k, min(C, spread_by * k + spread_by), step, jnp.zeros((F, w), F32))
        cp[p, :, k * w : (k + 1) * w] = acc.astype(BF16)

    def shrink(k):
        with jax.named_scope("shrink"):
            end = min(C, spread_by * k + spread_by)

            def step(i, carry):
                st[:, pl.ds(multiple(i * w, w), w)] = matches(m, k, i)
                return carry

            lax.fori_loop(k, end, step, 0)
            part = slice(k * w, end * w)
            igb[:, k * w : (k + 1) * w] = mm_t(ig[:, part], st[:, part]).astype(BF16)

    def pack_chunk(k):
        with jax.named_scope("pack_cot"):

            def step(p, carry):
                pack_block(k, p)
                return carry

            lax.fori_loop(0, M, step, 0)

    def unpack_block(p):
        with jax.named_scope("unpack"):

            def chunk(i, carry):
                def step(k, acc):
                    return acc + mm(igr[p, :, pl.ds(multiple(k * w, w), w)], matches(p, k, i))

                acc = lax.fori_loop(i // spread_by, jnp.minimum(i, KC - 1) + 1, step, jnp.zeros((F, w), F32))
                xv[:, pl.ds(multiple(p * mine + i * w, w), w)] = acc.astype(BF16)
                return carry

            lax.fori_loop(0, C, chunk, 0)

    def unpack_from(o):
        part = igr.at[0, :, pl.ds(0, cap)]
        remote(part, part, in_send.at[0], out_recv.at[1, o], z_peer(o)).wait_recv()
        unpack_block(flip(m, o))

    if not packed:
        order_out[...] = jnp.zeros_like(order_out)
    class SpreadZ:
        def __init__(self, bit, bufs, send, recv):
            self.go, self.come = [], []
            offsets = list(range(0, M, 2 * bit))
            for k, buf in enumerate(bufs):
                sems = (send.at[k, bits.index(bit)], recv.at[k, bits.index(bit)], z_peer(bit))
                for h in offsets:
                    slot = buf.at[c, q, flip(m, h)]
                    self.go.append(remote(slot, slot, *sems))
                both = buf.at[c, q, pl.ds(0, len(offsets))]
                self.come.append(remote(both, both, *sems))

        def start(self):
            for copy in self.go:
                copy.start()

        def wait(self):
            for copy in self.come:
                copy.wait()

    bufs = (wb, tb)
    first = SpreadZ(bits[-1], bufs, wz_send, wz_recv)
    first.start()
    if packed:
        send_tile(0, x_hbm)
        order_tiles()
        for j in range(1, tiles):
            send_tile(j, xp)
    else:
        send_in(0)
    if not packed:
        masks_to(mp)
        mk[...] = mp[...].astype(F32)
    else:
        deal(xv, xp, 1, C)
        to_seats = pltpu.make_async_copy(seats_v, seats_s, local_sem.at[17])
        to_seats.start()

        def deal_masks(t, carry):
            for j in range(8):
                mk[pl.ds(t * 8 + j, 1), :] = mp[pl.ds(order_s[0, t * 8 + j], 1), :].astype(F32)
            return carry

        lax.fori_loop(0, total_tiles // 8, deal_masks, 0)
        to_seats.wait()
        flags = mk[...]
        rows, cols = M * groups, LANES
        lower = lax.broadcasted_iota(jnp.int32, (cols, cols), 0) < lax.broadcasted_iota(jnp.int32, (cols, cols), 1)
        inside = mm(flags.astype(BF16), jnp.where(lower, 1.0, 0.0).astype(BF16))
        sums = jnp.broadcast_to(jnp.sum(flags, axis=1, keepdims=True), (rows, cols)).astype(BF16)
        one = lax.broadcasted_iota(jnp.int32, (rows, rows), 0)
        two = lax.broadcasted_iota(jnp.int32, (rows, rows), 1)
        ahead = (two < one) & (two >= one - one % groups)
        place_in = inside + mm(jnp.where(ahead, 1.0, 0.0).astype(BF16), sums)
        rk[...] = jnp.where(flags > 0.0, place_in, -1.0)
    def clear(i, carry):
        rows = pl.ds(multiple(i * ROWS, ROWS), ROWS)
        g1[rows, :] = jnp.zeros((ROWS, D), F32)
        g2t[rows, :] = jnp.zeros((ROWS, D), F32)
        for t in range(6):
            vec[t, rows, :] = jnp.zeros((ROWS, LANES), F32)
        return carry

    lax.fori_loop(0, blocks, clear, 0)
    stat[...] = jnp.zeros_like(stat)

    ahead_of = min(FIRST, C)
    if packed:
        loads[14].wait()
        deal(cv, cq, 0, C)
        if cap % w:
            cb[:, cap : KC * w] = jnp.zeros((D, KC * w - cap), BF16)
            for p in range(M):
                igr[p, :, cap : KC * w] = jnp.zeros((F, KC * w - cap), BF16)
        pack_chunk(0)

    def step_in(k):
        if packed:
            if k < KC:
                send_in(k, (1,))
            if k + 1 < ahead_of:
                send_in(k + 1, (0,))
            if k + 1 < KC:
                pack_chunk(k + 1)
        elif k + 1 < ahead_of:
            send_in(k + 1)

    with jax.named_scope("weights_z"):
        for bit in bits[::-1]:
            if bit != bits[-1]:
                first = SpreadZ(bit, bufs, wz_send, wz_recv)
                first.start()
            if bit == bits[0]:
                step_in(0)
            first.wait()
    with jax.named_scope("weights_xy"):
        for o in xy_order:
            for k, buf in enumerate(bufs):
                remote(buf.at[c, q], buf.at[c, q], wx_send.at[k], wx_recv.at[k], xy_peer(o)).start()
        step_in(1)
        step_in(2)
        for k, buf in enumerate(bufs):
            rest = buf.at[c, pl.ds(0, Q - 1)]
            remote(rest, rest, wx_send.at[k], wx_recv.at[k], xy_peer(1)).wait()
    with jax.named_scope("weights_core"):
        for k, buf in enumerate(bufs):
            remote(buf.at[c], buf.at[c], wc_send.at[k], wc_recv.at[k], core_peer).start()
        for k in range(3, max(ahead_of, KC if packed else 0)):
            if k < ahead_of:
                step_in(k)
            elif k + 1 < KC:
                pack_chunk(k + 1)
        for k, buf in enumerate(bufs):
            remote(buf.at[c], buf.at[1 - c], wc_send.at[k], wc_recv.at[k], core_peer).wait()

    with jax.named_scope("weights_spread"):

        def place(i, carry):
            rows = pl.ds(multiple(i * dr, dr), dr)
            for j in range(M):
                cols = slice(j * F, (j + 1) * F)
                w1[rows, cols] = wb[i % 2, i // 2, j, 0:dr, :]
                w2t[rows, cols] = wb[i % 2, i // 2, j, dr : 2 * dr, :]
            return carry

        lax.fori_loop(0, N, place, 0)

        def turn(i, carry):
            here = pl.ds(multiple(i * LANES, LANES), LANES)
            for j in range(D // LANES):
                there = slice(j * LANES, (j + 1) * LANES)
                w1t[there, here] = w1[here, there].astype(F32).T.astype(BF16)
                w2[there, here] = w2t[here, there].astype(F32).T.astype(BF16)
            return carry

        lax.fori_loop(0, D // LANES, turn, 0)
        for t in range(6):
            for i in range(N):
                for j in range(M):
                    stage[t, i * kb : (i + 1) * kb, j * F : (j + 1) * F] = tb[
                        i % 2, i // 2, j, t * kb : (t + 1) * kb, :
                    ]

        def table(t, carry):
            for j in range(D // LANES):
                cols = slice(j * LANES, (j + 1) * LANES)
                piece = stage[t, :, cols]
                tab[t, cols, :] = jnp.concatenate([piece] * per_mask, axis=0).T
            return carry

        lax.fori_loop(0, 6, table, 0)

    def eight(value):
        return value.reshape(ROWS // 8, 8, LANES).sum(0)

    if packed:
        early = [(C - 3, [(0, 0)]), (C - 2, [(0, 1)]), (C - 1, [(0, 2)])]
    else:
        early = [(C - 2, [(0, 0), (1, 0)]), (C - 1, [(0, 1), (1, 1)])]

    def work(i, carry):
        col = multiple(i * w, w)
        with jax.named_scope("wait_in"):
            wait_in(i)

        @pl.when((i + AHEAD >= FIRST) & (i + AHEAD < C - 1))
        def _():
            send_in(i + AHEAD)

        if C > FIRST:

            @pl.when(i + AHEAD == C - 2)
            def _():
                send_in(C - 1)

        for late, parts in early:
            for kind, k in parts:
                pl.when(i == late)(functools.partial(send_out, kind, k))

        masks = [mk[pl.ds(m * groups + i * tiles + j, 1), :] for j in range(tiles)]

        def place_of(r):
            return pl.ds(multiple(r * ROWS, ROWS), ROWS)

        def lanes_of(j):
            return pl.ds(multiple(col + j * LANES, LANES), LANES)

        def scale_rows(r, sums):
            rows = place_of(r)
            row_in = tab[0, rows, :]
            new = []
            for j in range(tiles):
                x = xb[rows, lanes_of(j)].astype(F32)
                sc[rows, j * LANES : (j + 1) * LANES] = (x * row_in).astype(BF16)
                new.append(sums[j] + eight(x * x))
            return tuple(new)

        zero = tuple(jnp.zeros((8, LANES), F32) for _ in range(tiles))
        with jax.named_scope("scale"):
            x_sums = lax.fori_loop(0, blocks, scale_rows, zero)
        with jax.named_scope("mm_one"):
            hp[...] = mm(w1t[...], sc[...])

        def curve_rows(r, carry):
            rows = place_of(r)
            gain, bias, row_mid = tab[1, rows, :], tab[2, rows, :], tab[3, rows, :]
            for j in range(tiles):
                cols = slice(j * LANES, (j + 1) * LANES)
                s = hp[rows, cols] * gain + bias
                s2 = s * s
                th = jnp.tanh(curve_a * (s + curve_b * (s2 * s)))
                cdf = 0.5 * (1.0 + th)
                h = s * cdf
                slope = cdf + (0.5 * s) * (1.0 - th * th) * (curve_a + (3.0 * curve_a * curve_b) * s2)
                hid[rows, cols] = h
                dgm[rows, cols] = slope * row_mid
                hi[rows, cols] = (h * row_mid).astype(BF16)
            return carry

        with jax.named_scope("curve"):
            lax.fori_loop(0, blocks, curve_rows, 0)
        with jax.named_scope("mm_two"):
            prod[...] = mm(w2t[...], hi[...])
        low, high_k = i // spread_by, jnp.minimum(i, KC - 1)
        if packed:
            with jax.named_scope("expand"):

                def grow(k, carry):
                    cx[...] += mm(cb[:, pl.ds(multiple(k * w, w), w)], matches(m, k, i))
                    return carry

                cx[...] = jnp.zeros_like(cx)
                lax.fori_loop(low, high_k + 1, grow, 0)

        def grad_of(rows, j):
            if packed:
                return cx[rows, j * LANES : (j + 1) * LANES]
            return cb[rows, lanes_of(j)].astype(F32) * masks[j]


        def out_rows(r, sums):
            rows = place_of(r)
            gain, bias = tab[4, rows, :], tab[5, rows, :]
            v4, v5 = vec[4, rows, :], vec[5, rows, :]
            new = []
            for j in range(tiles):
                cols = slice(j * LANES, (j + 1) * LANES)
                x = xb[rows, lanes_of(j)].astype(F32)
                projected = prod[rows, cols]
                branch = projected * gain + bias
                lgb[rows, lanes_of(j)] = (x + branch).astype(BF16)
                new.append(sums[j] + eight(branch * branch))
                go = grad_of(rows, j)
                v5 = v5 + go
                v4 = v4 + go * projected
                gp[rows, cols] = (go * gain).astype(BF16)
            vec[4, rows, :] = v4
            vec[5, rows, :] = v5
            return tuple(new)

        with jax.named_scope("out"):
            b_sums = lax.fori_loop(0, blocks, out_rows, zero)
        for j in range(tiles):
            stat[0:8, :] += x_sums[j] * masks[j]
            stat[8:16, :] += b_sums[j] * masks[j]

        with jax.named_scope("mm_three"):
            half = D // 2
            for k in range(2):
                part = slice(k * half, (k + 1) * half)
                g2t[part, :] += mm_t(gp[part, :], hi[...])
            prod[...] = mm(w2[...], gp[...])

        def back_rows(r, carry):
            rows = place_of(r)
            gain = tab[1, rows, :]
            v1, v2, v3 = vec[1, rows, :], vec[2, rows, :], vec[3, rows, :]
            for j in range(tiles):
                cols = slice(j * LANES, (j + 1) * LANES)
                gh = prod[rows, cols]
                v3 = v3 + gh * hid[rows, cols]
                gs = gh * dgm[rows, cols]
                v2 = v2 + gs
                v1 = v1 + gs * hp[rows, cols]
                gpre[rows, cols] = (gs * gain).astype(BF16)
            vec[1, rows, :] = v1
            vec[2, rows, :] = v2
            vec[3, rows, :] = v3
            return carry

        with jax.named_scope("back"):
            lax.fori_loop(0, blocks, back_rows, 0)
        with jax.named_scope("mm_four"):
            for k in range(2):
                part = slice(k * half, (k + 1) * half)
                g1[part, :] += mm_t(sc[part, :], gpre[...])
            prod[...] = mm(w1[...], gpre[...])

        def in_rows(r, carry):
            rows = place_of(r)
            row_in = tab[0, rows, :]
            v0 = vec[0, rows, :]
            for j in range(tiles):
                cols = slice(j * LANES, (j + 1) * LANES)
                gs = prod[rows, cols]
                v0 = v0 + gs * xb[rows, lanes_of(j)].astype(F32)
                go = grad_of(rows, j)
                done = (gs * row_in + go).astype(BF16)
                if packed:
                    ig[rows, lanes_of(j)] = done
                else:
                    igb[rows, lanes_of(j)] = done
            vec[0, rows, :] = v0
            return carry

        with jax.named_scope("in"):
            lax.fori_loop(0, blocks, in_rows, 0)
        if packed:
            xv[:, pl.ds(multiple(m * mine + col, w), w)] = ig[pl.ds(multiple(m * F, F), F), pl.ds(col, w)]
        return carry

    lax.fori_loop(0, C, work, 0)

    items = [item for _, parts in early for item in parts]
    already = len(items)
    if packed:
        items += [(1, k) for k in range(KC)] + [(0, i) for i in range(3, C)]
    else:
        items += [(kind, i) for i in range(2, C) for kind in range(2)]
    state = {"sent": already}

    def pump(count):
        with jax.named_scope("pump"):
            for kind, k in items[state["sent"] : state["sent"] + count]:
                if kind and packed:
                    shrink(k)
                send_out(kind, k)
            state["sent"] += count

    with jax.named_scope("pack"):

        def pack_g(i, carry):
            rows = pl.ds(multiple(i * dr, dr), dr)
            for j in range(M):
                cols = slice(j * F, (j + 1) * F)
                gb[i % 2, i // 2, j, 0:dr, :] = g1[rows, cols]
                gb[i % 2, i // 2, j, dr : 2 * dr, :] = g2t[rows, cols]
            return carry

        lax.fori_loop(0, N, pack_g, 0)

        def fold(t, carry):
            for j in range(D // LANES):
                cols = slice(j * LANES, (j + 1) * LANES)
                turned = vec[t, cols, :].T
                vt[t, :, cols] = sum(turned[k * K : (k + 1) * K, :] for k in range(per_mask))
            return carry

        lax.fori_loop(0, 6, fold, 0)
        for t in range(6):
            for i in range(N):
                for j in range(M):
                    row = 2 * dr + t * kb
                    gb[i % 2, i // 2, j, row : row + kb, :] = vt[t, i * kb : (i + 1) * kb, j * F : (j + 1) * F]
        own = mk[pl.ds(multiple(m * groups, groups), groups), :]
        totals = [stat[0:8, :], stat[8:16, :], own]
        rows8 = [jnp.sum(v, keepdims=True).reshape(1, 1) for v in totals]
        rows8.append(jnp.where(rows8[2] > cap, 1.0, 0.0))
        row_id = lax.broadcasted_iota(jnp.int32, (8, F), 0)
        lines = sum(jnp.where(row_id == k, v, 0.0) for k, v in enumerate(rows8))

        def put(i, carry):
            for j in range(M):
                gb[i % 2, i // 2, j, 2 * dr + tr : pr, :] = lines
            return carry

        lax.fori_loop(0, N, put, 0)

    with jax.named_scope("sum_core"):
        for o in xy_order + [0]:
            k = flip(q, o)
            remote(gb.at[1 - c, k], rcore.at[k], gc_send.at[o], gc_recv.at[o], core_peer).start()

        def add_core(k):
            def step(j, carry):
                gb[c, k, j] += rcore[k, j]
                return carry

            lax.fori_loop(0, M, step, 0)

        def over_xy(o):
            k = flip(q, o)
            sems = [(gx_send.at[n], gx_recv.at[n], xy_peer(o)) for n in range(2)]
            tail = gb.at[c, k, :, pl.ds(2 * dr, pr - 2 * dr), :]
            return remote(xs.at[o], rxg.at[o], *sems[0]), remote(tail, rxv.at[o], *sems[1])

        for o in xy_order + [0]:
            k = flip(q, o)
            remote(gb.at[1 - c, k], rcore.at[k], gc_send.at[o], gc_recv.at[o], core_peer).wait()
            add_core(k)
            if o:

                def round_piece(j, carry):
                    xs[o, j] = gb[c, k, j, 0 : 2 * dr, :].astype(BF16)
                    return carry

                lax.fori_loop(0, M, round_piece, 0)
                for copy in over_xy(o):
                    copy.start()
    pump(2)
    with jax.named_scope("sum_xy"):
        for n, buf in enumerate((rxg, rxv)):
            rest = buf.at[pl.ds(1, Q - 1)]
            remote(rest, rest, gx_send.at[n], gx_recv.at[n], xy_peer(1)).wait()
        for o in xy_order:

            def step(j, carry):
                gb[c, q, j, 0 : 2 * dr, :] += rxg[o, j].astype(F32)
                gb[c, q, j, 2 * dr : pr, :] += rxv[o, j]
                return carry

            lax.fori_loop(0, M, step, 0)
    with jax.named_scope("sum_z"):
        slot = 0
        for stage, bit in enumerate(bits):
            moves = []
            at = slot
            for h in range(0, M, 2 * bit):
                away = flip(m, h + bit)
                zs[slot] = gb[c, q, away, 0 : 2 * dr, :].astype(BF16)
                sems = [(gz_send.at[k, stage], gz_recv.at[k, stage], z_peer(bit)) for k in range(2)]
                tail = gb.at[c, q, away, pl.ds(2 * dr, pr - 2 * dr), :]
                moves.append((slot, h, remote(zs.at[slot], rzg.at[slot], *sems[0]), remote(tail, rzv.at[slot], *sems[1])))
                slot += 1
            for _, _, one, two in moves:
                one.start()
                two.start()
            pump(1)
            for k, buf in enumerate((rzg, rzv)):
                rest = buf.at[pl.ds(at, len(moves))]
                remote(rest, rest, gz_send.at[k, stage], gz_recv.at[k, stage], z_peer(bit)).wait()
            for k, h, _, _ in moves:
                keep = flip(m, h)
                gb[c, q, keep, 0 : 2 * dr, :] += rzg[k].astype(F32)
                gb[c, q, keep, 2 * dr : pr, :] += rzv[k]
            pump(1)

    total = gb[c, q, m]
    ga[c, q, m] = total[0 : 2 * dr, :].astype(BF16)
    with jax.named_scope("spread_z"):
        first = SpreadZ(bits[-1], (ga,), az_send, az_recv)
        first.start()
        pump(1)
        for load in loads[4:14]:
            load.wait()
        g1_out[...] = total[0:dr, :]
        g2_out[...] = total[dr : 2 * dr, :]
        corr_one = 1.0 - beta_first**STEP
        corr_two = 1.0 - beta_second**STEP
        for t in range(6):
            row = 2 * dr + t * kb
            grad = total[row : row + kb, :]
            one = beta_first * m1_v[t] + (1.0 - beta_first) * grad
            two = beta_second * m2_v[t] + (1.0 - beta_second) * grad * grad
            m1_out[t] = one
            m2_out[t] = two
            mem_out[t] = mem_v[t] - adam_rate * (one / corr_one) / (jnp.sqrt(two / corr_two) + adam_eps)
        sums_out[...] = total[2 * dr + tr : pr, 0:LANES if F >= LANES else F]
        for bit in bits[::-1]:
            if bit != bits[-1]:
                pump(1)
                first = SpreadZ(bit, (ga,), az_send, az_recv)
                first.start()
            if bit == bits[0]:
                pump(len(items))
            if packed and bit == bits[0]:
                for o in z_order[:-1]:
                    unpack_from(o)
            first.wait()
    with jax.named_scope("spread_xy"):
        for o in xy_order:
            remote(ga.at[c, q], ga.at[c, q], ax_send, ax_recv, xy_peer(o)).start()
        if packed:
            for o in z_order[-1:]:
                unpack_from(o)
            with jax.named_scope("settle"):
                deal(xv, ig_out, 0, C, seats_s)
        rest = ga.at[c, pl.ds(0, Q - 1)]
        remote(rest, rest, ax_send, ax_recv, xy_peer(1)).wait()
    with jax.named_scope("spread_core"):
        remote(ga.at[c], ga.at[c], ac_send, ac_recv, core_peer).start()
        remote(ga.at[c], ga.at[1 - c], ac_send, ac_recv, core_peer).wait()
    with jax.named_scope("shampoo"):

        def place_g(i, carry):
            rows = pl.ds(multiple(i * dr, dr), dr)
            for j in range(M):
                cols = slice(j * F, (j + 1) * F)
                g1f[rows, cols] = ga[i % 2, i // 2, j, 0:dr, :]
                g2ft[rows, cols] = ga[i % 2, i // 2, j, dr : 2 * dr, :]
            return carry

        lax.fori_loop(0, N, place_g, 0)

        def turn_g(i, carry):
            here = pl.ds(multiple(i * LANES, LANES), LANES)
            for j in range(D // LANES):
                there = slice(j * LANES, (j + 1) * LANES)
                g1ft[there, here] = g1f[here, there].astype(F32).T.astype(BF16)
                g2f[there, here] = g2ft[here, there].astype(F32).T.astype(BF16)
            return carry

        lax.fori_loop(0, D // LANES, turn_g, 0)
        by_d = pl.ds(multiple(d * dr, dr), dr)
        by_m = pl.ds(multiple(m * F, F), F)

        def renewed(old, fresh):
            return stat_decay * old + (1.0 - stat_decay) * fresh

        l1_out[...] = renewed(l1_v[...], mm_t(g1f[by_d, :], g1f[by_m, :]))
        r1_out[...] = renewed(r1_v[...], mm_t(g1ft[by_d, :], g1ft[by_m, :]))
        l2_out[...] = renewed(l2_v[...], mm_t(g2f[by_d, :], g2f[by_m, :]))
        r2_out[...] = renewed(r2_v[...], mm_t(g2ft[by_d, :], g2ft[by_m, :]))

        def stepped(weight, left, grad, right):
            inner = jnp.dot(left[...], grad[...].astype(F32), precision=high, preferred_element_type=F32)
            return weight[...] - shampoo_rate * mm_t(inner, right[...], high)

        w1_out[...] = stepped(w1_v, p1_v, g1f, q1_v)
        w2_out[...] = stepped(w2_v, q2_v, g2ft, p2_v)

    with jax.named_scope("drain"):
        for kind, out in enumerate((lg_out,) if packed else (lg_out, ig_out)):
            remote(out, out, in_send.at[kind], out_recv.at[kind, 0], z_peer(1)).wait_recv()
        for kind, buf in enumerate((lgb, igb)):
            part = buf.at[pl.ds(0, others), pl.ds(0, (mine, cap)[kind])]
            remote(part, part, out_send.at[kind], out_recv.at[0, 0], z_peer(1)).wait_send()
        for kind, buf in enumerate((xb, cb)):
            part = buf.at[pl.ds(0, others), pl.ds(0, (mine, cap)[kind])]
            remote(part, part, in_send.at[kind], out_recv.at[0, 0], z_peer(1)).wait_send()


def finish(n_out, D, tiles, sums_ref, order_ref, *refs):
    outs = refs[n_out : 2 * n_out]
    rms_out, flag_out, order_s, rms_s, flag_s, sems = refs[2 * n_out :]
    copies = [pltpu.make_async_copy(refs[i], outs[i], sems.at[i]) for i in range(n_out)]
    if tiles:
        order = pltpu.make_async_copy(order_ref, order_s, sems.at[n_out])
        order.start()
    for copy in copies[1 if tiles else 0 :]:
        copy.start()
    sums = sums_ref[...]
    ratio = jnp.sqrt(sums / (sums[2:3, :] * D))
    rms_s[0] = ratio[0, 0]
    rms_s[1] = ratio[1, 0]
    flag_s[0] = jnp.where(sums[3, 0] > 0.0, 1, 0)
    for k, (src, dst) in enumerate(((rms_s, rms_out), (flag_s, flag_out))):
        copies.append(pltpu.make_async_copy(src, dst, sems.at[n_out + 1 + k]))
        copies[-1].start()
    if tiles:
        order.wait()

        def step(g, carry):
            for j in range(8):
                t = g * 8 + j
                here = pl.ds(multiple(t * LANES, LANES), LANES)
                there = pl.ds(multiple(order_s[0, t] * LANES, LANES), LANES)
                pltpu.make_async_copy(refs[0].at[:, here], outs[0].at[:, there], sems.at[0]).start()
            return carry

        lax.fori_loop(0, tiles // 8, step, 0)
    for copy in copies:
        copy.wait()


def solution(mesh):
    N, M = mesh.shape["dp"], mesh.shape["mp"]
    Q = N // 2

    def on_device(*args):
        x, cot, mask, members, m1, m2, w1, w2, l1, r1, l2, r2, p1, q1, p2, q2 = args
        mask, w2, l2, r2 = mask.T, w2.T, l2.T, r2.T
        args = (x, cot, mask, members, m1, m2, w1, w2, l1, r1, l2, r2, p1, q1, p2, q2)
        F, R = x.shape
        D = F * M
        mine = R // M
        w = min(CHUNK, mine)
        C = mine // w
        kb = members.shape[1]
        dr = w1.shape[0]
        tr = -(-6 * kb // 8) * 8
        pr = 2 * dr + tr + 8
        groups = mine // LANES
        S = jax.ShapeDtypeStruct
        V = pltpu.VMEM
        dma = pltpu.SemaphoreType.DMA
        outs = [S(x.shape, BF16), S(x.shape, BF16), S((8, min(F, LANES)), F32), S((1, LANES), jnp.int32)]
        outs += [S(a.shape, F32) for a in (w1, w1, l1, r1, w2, w2, l2, r2, m1, m2, members)]
        anywhere = pl.BlockSpec(memory_space=pl.ANY)
        vmem = pl.BlockSpec(memory_space=pltpu.VMEM)

        def run(cap, number):
            packed = cap < mine
            KC = -(-cap // w)

            def only(shape, dtype):
                return V(shape if packed else (16, LANES), dtype)

            scratch = [V(a.shape, a.dtype) for a in (mask, members, m1, m2, w1, w2, l1, r1, l2, r2, p1, q1, p2, q2)]
            scratch += [only((F, R), BF16)] * 4
            scratch += [V((1, LANES), jnp.int32), pltpu.SMEM((1, LANES), jnp.int32)]
            scratch += [V((1, LANES), jnp.int32), pltpu.SMEM((1, LANES), jnp.int32)]
            scratch += [only((M, F, KC * w), BF16), only((w, mine), BF16), only((M, F, KC * w), BF16)]
            scratch += [V((D, mine), BF16), V((D, KC * w), BF16), V((D, mine), BF16), V((D, KC * w), BF16)]
            scratch += [V((2, Q, M, 2 * dr, F), BF16), V((2, Q, M, tr, F), F32)]
            scratch += [V((D, D), BF16)] * 4
            scratch += [V((6, D, LANES), F32), V((6, K, D), F32), V(mask.shape[::-1], jnp.int32)]
            scratch += [V((M * groups, LANES), jnp.int32)] + [V((M * groups, LANES), F32)] * 2
            scratch += [V((D, w), F32)] * 4
            scratch += [V((D, w), BF16)] * 4
            scratch += [only((D, w), F32), only((D, mine), BF16)]
            scratch += [V((D, D), F32)] * 2
            scratch += [V((6, D, LANES), F32), V((6, K, D), F32), V((16, LANES), F32)]
            scratch += [V((2, Q, M, pr, F), F32), V((Q, M, pr, F), F32)]
            scratch += [V((Q, M, 2 * dr, F), BF16), V((Q, M, 2 * dr, F), BF16), V((Q, M, pr - 2 * dr, F), F32)]
            scratch += [V((M - 1, 2 * dr, F), BF16), V((M - 1, pr - 2 * dr, F), F32), V((M - 1, 2 * dr, F), BF16)]
            scratch += [V((2, Q, M, 2 * dr, F), BF16)]
            scratch += [V((D, D), BF16)] * 4
            Z = M.bit_length() - 1
            scratch += [dma((18,)), dma((2,)), dma((C,)), dma((2,)), dma((2, M))]
            scratch += [dma((2, Z)), dma((2, Z)), dma((2,)), dma((2,)), dma((2,)), dma((2,))]
            scratch += [dma((Q,)), dma((Q,)), dma((2,)), dma((2,)), dma((2, Z)), dma((2, Z))]
            scratch += [dma((1, Z)), dma((1, Z)), dma, dma, dma, dma]
            res = pl.pallas_call(
                functools.partial(kernel, N, M, cap),
                out_shape=[V(a.shape, a.dtype) for a in outs],
                in_specs=[anywhere] * 16,
                out_specs=[vmem] * 15,
                scratch_shapes=scratch,
                compiler_params=pltpu.CompilerParams(
                    collective_id=number, has_side_effects=True, vmem_limit_bytes=46 << 20
                ),
                name="packed" if packed else "whole",
            )(*[pltpu.with_memory_space_constraint(a, pltpu.HBM) for a in args])
            kept = [*res[:2], *res[4:]]
            *done, rms, flag = pl.pallas_call(
                functools.partial(finish, len(kept), D, M * groups if packed else 0),
                out_shape=[S(a.shape, a.dtype) for a in kept] + [S((2,), F32), S((1,), jnp.int32)],
                in_specs=[vmem, anywhere] + [anywhere] * len(kept),
                out_specs=[anywhere] * (len(kept) + 2),
                scratch_shapes=[
                    pltpu.SMEM((1, LANES), jnp.int32),
                    pltpu.SMEM((2,), F32),
                    pltpu.SMEM((1,), jnp.int32),
                    dma((len(kept) + 3,)),
                ],
                compiler_params=pltpu.CompilerParams(vmem_limit_bytes=16 << 20),
                name="finish",
            )(res[2], res[3], *kept)
            return flag, (*done, rms)

        flag, fast = run(-(-mine * 11 // (16 * LANES)) * LANES, 0)
        done = lax.cond(flag[0] > 0, lambda: run(mine, 1)[1], lambda: fast)
        logits, igrad, g1, n1, l1, r1, g2, n2, l2, r2, m1, m2, new, rms = done
        return (logits, igrad, rms, g1, n1, l1, r1, g2.T, n2.T, l2.T, r2.T, m1, m2, new)

    placed = (
        P("mp", "dp"),
        P("mp", "dp"),
        P("dp", None),
        P(None, "dp", "mp"),
        P(None, "dp", "mp"),
        P(None, "dp", "mp"),
        P("dp", "mp"),
        P("mp", "dp"),
        P("dp", "mp"),
        P("dp", "mp"),
        P("mp", "dp"),
        P("mp", "dp"),
        P("dp", None),
        P("mp", None),
        P("mp", None),
        P("dp", None),
    )
    return jax.shard_map(
        on_device,
        mesh=mesh,
        in_specs=placed,
        out_specs=(
            P("mp", "dp"),
            P("mp", "dp"),
            P(),
            P("dp", "mp"),
            P("dp", "mp"),
            P("dp", "mp"),
            P("dp", "mp"),
            P("mp", "dp"),
            P("mp", "dp"),
            P("mp", "dp"),
            P("mp", "dp"),
            P(None, "dp", "mp"),
            P(None, "dp", "mp"),
            P(None, "dp", "mp"),
        ),
        check_vma=False,
    )
```

```python
import functools

import jax
import jax.numpy as jnp
from jax import lax
from jax.experimental import pallas as pl
from jax.experimental.pallas import tpu as pltpu
from jax.sharding import PartitionSpec as P

K = 32
STEP = 10
LANES = 128
CHUNK = 256
ROWS = 32
AHEAD = 2
FIRST = 4
LEAST = 8

beta_first = 0.9
beta_second = 0.999
adam_eps = 1e-08
adam_rate = 0.2
stat_decay = 0.95
shampoo_rate = 1.0
curve_a = 0.7978845608028654
curve_b = 0.044715

MESH = pl.DeviceIdType.MESH
F32 = jnp.float32
BF16 = jnp.bfloat16
over_lanes = (((1,), (1,)), ((), ()))


def flip(index, mask):
    bit = 1
    while bit <= mask:
        if mask & bit:
            index = index + bit - 2 * bit * ((index // bit) % 2)
        bit *= 2
    return index


def mm(a, b):
    return jnp.dot(a, b, preferred_element_type=F32)


def mm_t(a, b, precision=None):
    return lax.dot_general(a, b, over_lanes, precision=precision, preferred_element_type=F32)


def multiple(value, by):
    return pl.multiple_of(value, by)


def kernel(
    N,
    M,
    cap,
    x_hbm,
    cot_hbm,
    mask_hbm,
    mem_hbm,
    m1_hbm,
    m2_hbm,
    w1_hbm,
    w2_hbm,
    l1_hbm,
    r1_hbm,
    l2_hbm,
    r2_hbm,
    p1_hbm,
    q1_hbm,
    p2_hbm,
    q2_hbm,
    lg_out,
    ig_out,
    sums_out,
    order_out,
    g1_out,
    w1_out,
    l1_out,
    r1_out,
    g2_out,
    w2_out,
    l2_out,
    r2_out,
    m1_out,
    m2_out,
    mem_out,
    mask_v,
    mem_v,
    m1_v,
    m2_v,
    w1_v,
    w2_v,
    l1_v,
    r1_v,
    l2_v,
    r2_v,
    p1_v,
    q1_v,
    p2_v,
    q2_v,
    xv,
    xp,
    cv,
    cq,
    order_v,
    order_s,
    seats_v,
    seats_s,
    cp,
    st,
    igr,
    xb,
    cb,
    lgb,
    igb,
    wb,
    tb,
    w1,
    w1t,
    w2,
    w2t,
    tab,
    stage,
    mt,
    mp,
    mk,
    rk,
    hp,
    hid,
    dgm,
    prod,
    sc,
    hi,
    gp,
    gpre,
    cx,
    ig,
    g1,
    g2t,
    vec,
    vt,
    stat,
    gb,
    rcore,
    xs,
    rxg,
    rxv,
    rzg,
    rzv,
    zs,
    ga,
    g1f,
    g1ft,
    g2f,
    g2ft,
    local_sem,
    in_send,
    in_recv,
    out_send,
    out_recv,
    wz_send,
    wz_recv,
    wx_send,
    wx_recv,
    wc_send,
    wc_recv,
    gc_send,
    gc_recv,
    gx_send,
    gx_recv,
    gz_send,
    gz_recv,
    az_send,
    az_recv,
    ax_send,
    ax_recv,
    ac_send,
    ac_recv,
):
    F, R = x_hbm.shape
    D = F * M
    Q = N // 2
    mine = R // M
    w = min(CHUNK, mine)
    C = mine // w
    tiles = w // LANES
    packed = cap < mine
    KC = -(-cap // w)
    groups = mine // LANES
    kb = K // N
    dr = D // N
    tr = tb.shape[3]
    pr = gb.shape[3]
    blocks = D // ROWS
    high = lax.Precision.HIGHEST

    d, m = lax.axis_index("dp"), lax.axis_index("mp")
    c, q = d % 2, d // 2

    def z_peer(o):
        return (d, flip(m, o))

    def xy_peer(o):
        return (flip(q, o) * 2 + c, m)

    core_peer = (flip(d, 1), m)
    z_order = sorted(range(1, M), reverse=True)
    bits = [1 << k for k in range(M.bit_length() - 1)]
    xy_order = sorted(range(1, Q), reverse=True)

    def remote(src, dst, send, recv, peer):
        return pltpu.make_async_remote_copy(
            src_ref=src, dst_ref=dst, send_sem=send, recv_sem=recv, device_id=peer, device_id_type=MESH
        )

    pairs = (
        (mask_hbm, mask_v),
        (mem_hbm, mem_v),
        (w1_hbm, w1_v),
        (w2_hbm, w2_v),
        (m1_hbm, m1_v),
        (m2_hbm, m2_v),
        (l1_hbm, l1_v),
        (r1_hbm, r1_v),
        (l2_hbm, l2_v),
        (r2_hbm, r2_v),
        (p1_hbm, p1_v),
        (q1_hbm, q1_v),
        (p2_hbm, p2_v),
        (q2_hbm, q2_v),
    )
    if packed:
        pairs = (*pairs, (cot_hbm, cv), (x_hbm, xv))
    loads = [pltpu.make_async_copy(a, b, local_sem.at[i]) for i, (a, b) in enumerate(pairs)]
    for load in loads:
        load.start()

    per_mask = LANES // K
    total_tiles = M * groups

    I32 = jnp.int32

    def masks_to(ref):
        loads[0].wait()
        mt[...] = mask_v[...].T
        ref[...] = jnp.concatenate(
            [mt[pl.ds(j, total_tiles, stride=per_mask), :] for j in range(per_mask)], axis=1
        )

    def across(row):
        return jnp.broadcast_to(row, (LANES, LANES)).T

    def order_tiles():
        masks_to(mp)
        tall = jnp.concatenate([mp[...], jnp.zeros((LANES - total_tiles, LANES), I32)], axis=0)
        count = jnp.sum(tall.T, axis=0, keepdims=True)
        line_id = lax.broadcasted_iota(I32, (LANES, LANES), 0)
        lane_id = lax.broadcasted_iota(I32, (LANES, LANES), 1)
        mine_here, other = jnp.broadcast_to(count, (LANES, LANES)), across(count)
        before = (other > mine_here) | ((other == mine_here) & (line_id < lane_id))
        dealt = (line_id < total_tiles) & (line_id % groups != 0)
        rank = jnp.sum(jnp.where(before & dealt, 1, 0), axis=0, keepdims=True)
        turn, seat = rank // M, rank % M
        block = jnp.where(turn % 2 == 0, seat, M - 1 - seat)
        lane = lax.broadcasted_iota(I32, (1, LANES), 1)
        seats = jnp.where(lane % groups == 0, lane, block * groups + 1 + turn)
        seats = jnp.where(lane < total_tiles, seats, LANES)
        seats_v[...] = seats
        order_v[...] = jnp.sum(jnp.where(across(seats) == lane_id, line_id, 0), axis=0, keepdims=True)
        order_out[...] = order_v[...]
        to_scalars = pltpu.make_async_copy(order_v, order_s, local_sem.at[16])
        to_scalars.start()
        loads[15].wait()
        to_scalars.wait()
        deal(xv, xp, 0, 1)

    def deal(src, dst, start, end, order=None):
        order = order_s if order is None else order


        def step(i, carry):
            for p in range(M):
                for j in range(tiles):
                    t = p * groups + i * tiles + j
                    dst[:, pl.ds(multiple(t * LANES, LANES), LANES)] = src[
                        :, pl.ds(order[0, t] * LANES, LANES)
                    ]
            return carry

        lax.fori_loop(start, end, step, 0)

    with jax.named_scope("barrier"):
        entry = pltpu.get_barrier_semaphore()
        peers = [z_peer(o) for o in z_order] + [xy_peer(o) for o in xy_order] + [core_peer]
        for peer in peers:
            pl.semaphore_signal(entry, inc=1, device_id=peer, device_id_type=MESH)
        for load in loads[1:4]:
            load.wait()
        wb[c, q, m, 0:dr, :] = w1_v[...].astype(BF16)
        wb[c, q, m, dr : 2 * dr, :] = w2_v[...].astype(BF16)
        for t in range(6):
            tb[c, q, m, t * kb : (t + 1) * kb, :] = mem_v[t]
        pl.semaphore_wait(entry, len(peers))

    kinds_in = (xb, cb)

    def at_width(i, act):
        if not packed:
            act(w)
        elif isinstance(i, int):
            if i < KC:
                act(min(w, cap - i * w))
        elif cap % w == 0:
            pl.when(i < KC)(lambda: act(w))
        else:
            pl.when(i < KC - 1)(lambda: act(w))
            pl.when(i == KC - 1)(lambda: act(cap % w))

    def send_tile(j, src):
        here = pl.ds(multiple(m * F, F), F)
        there = xb.at[here, j * LANES : (j + 1) * LANES]

        def tile(to):
            return src.at[:, pl.ds(multiple(to * mine + j * LANES, LANES), LANES)]

        for o in z_order:
            to = flip(m, o)
            remote(tile(to), there, in_send.at[0], in_recv.at[0], (d, to)).start()
        pltpu.make_async_copy(tile(m), there, in_recv.at[0]).start()

    def send_in(i, kinds=(0, 1)):
        here = pl.ds(multiple(m * F, F), F)

        def source(kind, to, width):
            if kind and packed:
                return cp.at[to, :, pl.ds(multiple(i * w, w), width)]
            hbm = xp if packed else (x_hbm, cot_hbm)[kind]
            return hbm.at[:, pl.ds(multiple(to * mine + i * w, w), width)]

        def start(kind, width):
            there = kinds_in[kind].at[here, pl.ds(multiple(i * w, w), width)]
            for o in z_order:
                to = flip(m, o)
                remote(source(kind, to, width), there, in_send.at[kind], in_recv.at[i], (d, to)).start()
            pltpu.make_async_copy(source(kind, m, width), there, in_recv.at[i]).start()

        for kind in kinds:
            if kind:
                at_width(i, functools.partial(start, 1))
            else:
                start(0, w)

    others = (M - 1) * F

    def wait_in(i):
        def arrive(width):
            part = xb.at[:, pl.ds(0, w + width)]
            remote(part, part, in_send.at[0], in_recv.at[i], z_peer(1)).wait_recv()

        at_width(i, arrive)
        if packed:
            pl.when(i >= KC)(lambda: arrive(0))

    def width_of(kind, i):
        return min(w, cap - i * w) if kind and packed else w

    def send_out(kind, i):
        col = pl.ds(multiple(i * w, w), width_of(kind, i))
        if kind and packed:
            there = igr.at[m, :, col]
        else:
            there = (lg_out, ig_out)[kind].at[:, pl.ds(multiple(m * mine + i * w, w), w)]
        buf = (lgb, igb)[kind]
        for o in z_order[::-1]:
            to = flip(m, o)
            recv = out_recv.at[kind, o] if kind and packed else out_recv.at[kind, 0]
            remote(buf.at[pl.ds(multiple(to * F, F), F), col], there, out_send.at[kind], recv, (d, to)).start()
        if not (kind and packed):
            pltpu.make_async_copy(buf.at[pl.ds(multiple(m * F, F), F), col], there, out_recv.at[kind, 0]).start()

    line = lax.broadcasted_iota(jnp.int32, (w, LANES), 0).astype(F32)

    def matches(p, k, i):
        base = (k * w) * jnp.float32(1) if isinstance(k, int) else (k * w).astype(F32)
        parts = []
        for j in range(tiles):
            row = rk[pl.ds(p * groups + i * tiles + j, 1), :] - base
            parts.append(jnp.where(line == row, 1.0, 0.0).astype(BF16))
        return jnp.concatenate(parts, axis=1)

    spread_by = K // LEAST

    def pack_block(k, p):
        def step(i, acc):
            cols = pl.ds(multiple(p * mine + i * w, w), w)
            return acc + mm_t(cq[:, cols], matches(p, k, i))

        acc = lax.fori_loop(k, min(C, spread_by * k + spread_by), step, jnp.zeros((F, w), F32))
        cp[p, :, k * w : (k + 1) * w] = acc.astype(BF16)

    def shrink(k):
        with jax.named_scope("shrink"):
            end = min(C, spread_by * k + spread_by)

            def step(i, carry):
                st[:, pl.ds(multiple(i * w, w), w)] = matches(m, k, i)
                return carry

            lax.fori_loop(k, end, step, 0)
            part = slice(k * w, end * w)
            igb[:, k * w : (k + 1) * w] = mm_t(ig[:, part], st[:, part]).astype(BF16)

    def pack_chunk(k):
        with jax.named_scope("pack_cot"):

            def step(p, carry):
                pack_block(k, p)
                return carry

            lax.fori_loop(0, M, step, 0)

    def unpack_block(p):
        with jax.named_scope("unpack"):

            def chunk(i, carry):
                def step(k, acc):
                    return acc + mm(igr[p, :, pl.ds(multiple(k * w, w), w)], matches(p, k, i))

                acc = lax.fori_loop(i // spread_by, jnp.minimum(i, KC - 1) + 1, step, jnp.zeros((F, w), F32))
                xv[:, pl.ds(multiple(p * mine + i * w, w), w)] = acc.astype(BF16)
                return carry

            lax.fori_loop(0, C, chunk, 0)

    def unpack_from(o):
        part = igr.at[0, :, pl.ds(0, cap)]
        remote(part, part, in_send.at[0], out_recv.at[1, o], z_peer(o)).wait_recv()
        unpack_block(flip(m, o))

    if not packed:
        order_out[...] = jnp.zeros_like(order_out)
    class SpreadZ:
        def __init__(self, bit, bufs, send, recv):
            self.go, self.come = [], []
            offsets = list(range(0, M, 2 * bit))
            for k, buf in enumerate(bufs):
                sems = (send.at[k, bits.index(bit)], recv.at[k, bits.index(bit)], z_peer(bit))
                for h in offsets:
                    slot = buf.at[c, q, flip(m, h)]
                    self.go.append(remote(slot, slot, *sems))
                both = buf.at[c, q, pl.ds(0, len(offsets))]
                self.come.append(remote(both, both, *sems))

        def start(self):
            for copy in self.go:
                copy.start()

        def wait(self):
            for copy in self.come:
                copy.wait()

    bufs = (wb, tb)
    first = SpreadZ(bits[-1], bufs, wz_send, wz_recv)
    first.start()
    if packed:
        send_tile(0, x_hbm)
        order_tiles()
        for j in range(1, tiles):
            send_tile(j, xp)
    else:
        send_in(0)
    if not packed:
        masks_to(mp)
        mk[...] = mp[...].astype(F32)
    else:
        deal(xv, xp, 1, C)
        to_seats = pltpu.make_async_copy(seats_v, seats_s, local_sem.at[17])
        to_seats.start()

        def deal_masks(t, carry):
            for j in range(8):
                mk[pl.ds(t * 8 + j, 1), :] = mp[pl.ds(order_s[0, t * 8 + j], 1), :].astype(F32)
            return carry

        lax.fori_loop(0, total_tiles // 8, deal_masks, 0)
        to_seats.wait()
        flags = mk[...]
        rows, cols = M * groups, LANES
        lower = lax.broadcasted_iota(jnp.int32, (cols, cols), 0) < lax.broadcasted_iota(jnp.int32, (cols, cols), 1)
        inside = mm(flags.astype(BF16), jnp.where(lower, 1.0, 0.0).astype(BF16))
        sums = jnp.broadcast_to(jnp.sum(flags, axis=1, keepdims=True), (rows, cols)).astype(BF16)
        one = lax.broadcasted_iota(jnp.int32, (rows, rows), 0)
        two = lax.broadcasted_iota(jnp.int32, (rows, rows), 1)
        ahead = (two < one) & (two >= one - one % groups)
        place_in = inside + mm(jnp.where(ahead, 1.0, 0.0).astype(BF16), sums)
        rk[...] = jnp.where(flags > 0.0, place_in, -1.0)
    def clear(i, carry):
        rows = pl.ds(multiple(i * ROWS, ROWS), ROWS)
        g1[rows, :] = jnp.zeros((ROWS, D), F32)
        g2t[rows, :] = jnp.zeros((ROWS, D), F32)
        for t in range(6):
            vec[t, rows, :] = jnp.zeros((ROWS, LANES), F32)
        return carry

    lax.fori_loop(0, blocks, clear, 0)
    stat[...] = jnp.zeros_like(stat)

    ahead_of = min(FIRST, C)
    if packed:
        loads[14].wait()
        deal(cv, cq, 0, C)
        if cap % w:
            cb[:, cap : KC * w] = jnp.zeros((D, KC * w - cap), BF16)
            for p in range(M):
                igr[p, :, cap : KC * w] = jnp.zeros((F, KC * w - cap), BF16)
        pack_chunk(0)

    def step_in(k):
        if packed:
            if k < KC:
                send_in(k, (1,))
            if k + 1 < ahead_of:
                send_in(k + 1, (0,))
            if k + 1 < KC:
                pack_chunk(k + 1)
        elif k + 1 < ahead_of:
            send_in(k + 1)

    with jax.named_scope("weights_z"):
        for bit in bits[::-1]:
            if bit != bits[-1]:
                first = SpreadZ(bit, bufs, wz_send, wz_recv)
                first.start()
            if bit == bits[0]:
                step_in(0)
            first.wait()
    with jax.named_scope("weights_xy"):
        for o in xy_order:
            for k, buf in enumerate(bufs):
                remote(buf.at[c, q], buf.at[c, q], wx_send.at[k], wx_recv.at[k], xy_peer(o)).start()
        step_in(1)
        step_in(2)
        for k, buf in enumerate(bufs):
            rest = buf.at[c, pl.ds(0, Q - 1)]
            remote(rest, rest, wx_send.at[k], wx_recv.at[k], xy_peer(1)).wait()
    with jax.named_scope("weights_core"):
        for k, buf in enumerate(bufs):
            remote(buf.at[c], buf.at[c], wc_send.at[k], wc_recv.at[k], core_peer).start()
        for k in range(3, max(ahead_of, KC if packed else 0)):
            if k < ahead_of:
                step_in(k)
            elif k + 1 < KC:
                pack_chunk(k + 1)
        for k, buf in enumerate(bufs):
            remote(buf.at[c], buf.at[1 - c], wc_send.at[k], wc_recv.at[k], core_peer).wait()

    with jax.named_scope("weights_spread"):

        def place(i, carry):
            rows = pl.ds(multiple(i * dr, dr), dr)
            for j in range(M):
                cols = slice(j * F, (j + 1) * F)
                w1[rows, cols] = wb[i % 2, i // 2, j, 0:dr, :]
                w2t[rows, cols] = wb[i % 2, i // 2, j, dr : 2 * dr, :]
            return carry

        lax.fori_loop(0, N, place, 0)

        def turn(i, carry):
            here = pl.ds(multiple(i * LANES, LANES), LANES)
            for j in range(D // LANES):
                there = slice(j * LANES, (j + 1) * LANES)
                w1t[there, here] = w1[here, there].astype(F32).T.astype(BF16)
                w2[there, here] = w2t[here, there].astype(F32).T.astype(BF16)
            return carry

        lax.fori_loop(0, D // LANES, turn, 0)
        for t in range(6):
            for i in range(N):
                for j in range(M):
                    stage[t, i * kb : (i + 1) * kb, j * F : (j + 1) * F] = tb[
                        i % 2, i // 2, j, t * kb : (t + 1) * kb, :
                    ]

        def table(t, carry):
            for j in range(D // LANES):
                cols = slice(j * LANES, (j + 1) * LANES)
                piece = stage[t, :, cols]
                tab[t, cols, :] = jnp.concatenate([piece] * per_mask, axis=0).T
            return carry

        lax.fori_loop(0, 6, table, 0)

    def eight(value):
        return value.reshape(ROWS // 8, 8, LANES).sum(0)

    if packed:
        early = [(C - 3, [(0, 0)]), (C - 2, [(0, 1)]), (C - 1, [(0, 2)])]
    else:
        early = [(C - 2, [(0, 0), (1, 0)]), (C - 1, [(0, 1), (1, 1)])]

    def work(i, carry):
        col = multiple(i * w, w)
        with jax.named_scope("wait_in"):
            wait_in(i)

        @pl.when((i + AHEAD >= FIRST) & (i + AHEAD < C - 1))
        def _():
            send_in(i + AHEAD)

        if C > FIRST:

            @pl.when(i + AHEAD == C - 2)
            def _():
                send_in(C - 1)

        for late, parts in early:
            for kind, k in parts:
                pl.when(i == late)(functools.partial(send_out, kind, k))

        masks = [mk[pl.ds(m * groups + i * tiles + j, 1), :] for j in range(tiles)]

        def place_of(r):
            return pl.ds(multiple(r * ROWS, ROWS), ROWS)

        def lanes_of(j):
            return pl.ds(multiple(col + j * LANES, LANES), LANES)

        def scale_rows(r, sums):
            rows = place_of(r)
            row_in = tab[0, rows, :]
            new = []
            for j in range(tiles):
                x = xb[rows, lanes_of(j)].astype(F32)
                sc[rows, j * LANES : (j + 1) * LANES] = (x * row_in).astype(BF16)
                new.append(sums[j] + eight(x * x))
            return tuple(new)

        zero = tuple(jnp.zeros((8, LANES), F32) for _ in range(tiles))
        with jax.named_scope("scale"):
            x_sums = lax.fori_loop(0, blocks, scale_rows, zero)
        with jax.named_scope("mm_one"):
            hp[...] = mm(w1t[...], sc[...])

        def curve_rows(r, carry):
            rows = place_of(r)
            gain, bias, row_mid = tab[1, rows, :], tab[2, rows, :], tab[3, rows, :]
            for j in range(tiles):
                cols = slice(j * LANES, (j + 1) * LANES)
                s = hp[rows, cols] * gain + bias
                s2 = s * s
                th = jnp.tanh(curve_a * (s + curve_b * (s2 * s)))
                cdf = 0.5 * (1.0 + th)
                h = s * cdf
                slope = cdf + (0.5 * s) * (1.0 - th * th) * (curve_a + (3.0 * curve_a * curve_b) * s2)
                hid[rows, cols] = h
                dgm[rows, cols] = slope * row_mid
                hi[rows, cols] = (h * row_mid).astype(BF16)
            return carry

        with jax.named_scope("curve"):
            lax.fori_loop(0, blocks, curve_rows, 0)
        with jax.named_scope("mm_two"):
            prod[...] = mm(w2t[...], hi[...])
        low, high_k = i // spread_by, jnp.minimum(i, KC - 1)
        if packed:
            with jax.named_scope("expand"):

                def grow(k, carry):
                    cx[...] += mm(cb[:, pl.ds(multiple(k * w, w), w)], matches(m, k, i))
                    return carry

                cx[...] = jnp.zeros_like(cx)
                lax.fori_loop(low, high_k + 1, grow, 0)

        def grad_of(rows, j):
            if packed:
                return cx[rows, j * LANES : (j + 1) * LANES]
            return cb[rows, lanes_of(j)].astype(F32) * masks[j]


        def out_rows(r, sums):
            rows = place_of(r)
            gain, bias = tab[4, rows, :], tab[5, rows, :]
            v4, v5 = vec[4, rows, :], vec[5, rows, :]
            new = []
            for j in range(tiles):
                cols = slice(j * LANES, (j + 1) * LANES)
                x = xb[rows, lanes_of(j)].astype(F32)
                projected = prod[rows, cols]
                branch = projected * gain + bias
                lgb[rows, lanes_of(j)] = (x + branch).astype(BF16)
                new.append(sums[j] + eight(branch * branch))
                go = grad_of(rows, j)
                v5 = v5 + go
                v4 = v4 + go * projected
                gp[rows, cols] = (go * gain).astype(BF16)
            vec[4, rows, :] = v4
            vec[5, rows, :] = v5
            return tuple(new)

        with jax.named_scope("out"):
            b_sums = lax.fori_loop(0, blocks, out_rows, zero)
        for j in range(tiles):
            stat[0:8, :] += x_sums[j] * masks[j]
            stat[8:16, :] += b_sums[j] * masks[j]

        with jax.named_scope("mm_three"):
            half = D // 2
            for k in range(2):
                part = slice(k * half, (k + 1) * half)
                g2t[part, :] += mm_t(gp[part, :], hi[...])
            prod[...] = mm(w2[...], gp[...])

        def back_rows(r, carry):
            rows = place_of(r)
            gain = tab[1, rows, :]
            v1, v2, v3 = vec[1, rows, :], vec[2, rows, :], vec[3, rows, :]
            for j in range(tiles):
                cols = slice(j * LANES, (j + 1) * LANES)
                gh = prod[rows, cols]
                v3 = v3 + gh * hid[rows, cols]
                gs = gh * dgm[rows, cols]
                v2 = v2 + gs
                v1 = v1 + gs * hp[rows, cols]
                gpre[rows, cols] = (gs * gain).astype(BF16)
            vec[1, rows, :] = v1
            vec[2, rows, :] = v2
            vec[3, rows, :] = v3
            return carry

        with jax.named_scope("back"):
            lax.fori_loop(0, blocks, back_rows, 0)
        with jax.named_scope("mm_four"):
            for k in range(2):
                part = slice(k * half, (k + 1) * half)
                g1[part, :] += mm_t(sc[part, :], gpre[...])
            prod[...] = mm(w1[...], gpre[...])

        def in_rows(r, carry):
            rows = place_of(r)
            row_in = tab[0, rows, :]
            v0 = vec[0, rows, :]
            for j in range(tiles):
                cols = slice(j * LANES, (j + 1) * LANES)
                gs = prod[rows, cols]
                v0 = v0 + gs * xb[rows, lanes_of(j)].astype(F32)
                go = grad_of(rows, j)
                done = (gs * row_in + go).astype(BF16)
                if packed:
                    ig[rows, lanes_of(j)] = done
                else:
                    igb[rows, lanes_of(j)] = done
            vec[0, rows, :] = v0
            return carry

        with jax.named_scope("in"):
            lax.fori_loop(0, blocks, in_rows, 0)
        if packed:
            xv[:, pl.ds(multiple(m * mine + col, w), w)] = ig[pl.ds(multiple(m * F, F), F), pl.ds(col, w)]
        return carry

    lax.fori_loop(0, C, work, 0)

    items = [item for _, parts in early for item in parts]
    already = len(items)
    if packed:
        items += [(1, k) for k in range(KC)] + [(0, i) for i in range(3, C)]
    else:
        items += [(kind, i) for i in range(2, C) for kind in range(2)]
    state = {"sent": already}

    def pump(count):
        with jax.named_scope("pump"):
            for kind, k in items[state["sent"] : state["sent"] + count]:
                if kind and packed:
                    shrink(k)
                send_out(kind, k)
            state["sent"] += count

    with jax.named_scope("pack"):

        def pack_g(i, carry):
            rows = pl.ds(multiple(i * dr, dr), dr)
            for j in range(M):
                cols = slice(j * F, (j + 1) * F)
                gb[i % 2, i // 2, j, 0:dr, :] = g1[rows, cols]
                gb[i % 2, i // 2, j, dr : 2 * dr, :] = g2t[rows, cols]
            return carry

        lax.fori_loop(0, N, pack_g, 0)

        def fold(t, carry):
            for j in range(D // LANES):
                cols = slice(j * LANES, (j + 1) * LANES)
                turned = vec[t, cols, :].T
                vt[t, :, cols] = sum(turned[k * K : (k + 1) * K, :] for k in range(per_mask))
            return carry

        lax.fori_loop(0, 6, fold, 0)
        for t in range(6):
            for i in range(N):
                for j in range(M):
                    row = 2 * dr + t * kb
                    gb[i % 2, i // 2, j, row : row + kb, :] = vt[t, i * kb : (i + 1) * kb, j * F : (j + 1) * F]
        own = mk[pl.ds(multiple(m * groups, groups), groups), :]
        totals = [stat[0:8, :], stat[8:16, :], own]
        rows8 = [jnp.sum(v, keepdims=True).reshape(1, 1) for v in totals]
        rows8.append(jnp.where(rows8[2] > cap, 1.0, 0.0))
        row_id = lax.broadcasted_iota(jnp.int32, (8, F), 0)
        lines = sum(jnp.where(row_id == k, v, 0.0) for k, v in enumerate(rows8))

        def put(i, carry):
            for j in range(M):
                gb[i % 2, i // 2, j, 2 * dr + tr : pr, :] = lines
            return carry

        lax.fori_loop(0, N, put, 0)

    with jax.named_scope("sum_core"):
        for o in xy_order + [0]:
            k = flip(q, o)
            remote(gb.at[1 - c, k], rcore.at[k], gc_send.at[o], gc_recv.at[o], core_peer).start()

        def add_core(k):
            def step(j, carry):
                gb[c, k, j] += rcore[k, j]
                return carry

            lax.fori_loop(0, M, step, 0)

        def over_xy(o):
            k = flip(q, o)
            sems = [(gx_send.at[n], gx_recv.at[n], xy_peer(o)) for n in range(2)]
            tail = gb.at[c, k, :, pl.ds(2 * dr, pr - 2 * dr), :]
            return remote(xs.at[o], rxg.at[o], *sems[0]), remote(tail, rxv.at[o], *sems[1])

        for o in xy_order + [0]:
            k = flip(q, o)
            remote(gb.at[1 - c, k], rcore.at[k], gc_send.at[o], gc_recv.at[o], core_peer).wait()
            add_core(k)
            if o:

                def round_piece(j, carry):
                    xs[o, j] = gb[c, k, j, 0 : 2 * dr, :].astype(BF16)
                    return carry

                lax.fori_loop(0, M, round_piece, 0)
                for copy in over_xy(o):
                    copy.start()
    pump(2)
    with jax.named_scope("sum_xy"):
        for n, buf in enumerate((rxg, rxv)):
            rest = buf.at[pl.ds(1, Q - 1)]
            remote(rest, rest, gx_send.at[n], gx_recv.at[n], xy_peer(1)).wait()
        for o in xy_order:

            def step(j, carry):
                gb[c, q, j, 0 : 2 * dr, :] += rxg[o, j].astype(F32)
                gb[c, q, j, 2 * dr : pr, :] += rxv[o, j]
                return carry

            lax.fori_loop(0, M, step, 0)
    with jax.named_scope("sum_z"):
        slot = 0
        for stage, bit in enumerate(bits):
            moves = []
            at = slot
            for h in range(0, M, 2 * bit):
                away = flip(m, h + bit)
                zs[slot] = gb[c, q, away, 0 : 2 * dr, :].astype(BF16)
                sems = [(gz_send.at[k, stage], gz_recv.at[k, stage], z_peer(bit)) for k in range(2)]
                tail = gb.at[c, q, away, pl.ds(2 * dr, pr - 2 * dr), :]
                moves.append((slot, h, remote(zs.at[slot], rzg.at[slot], *sems[0]), remote(tail, rzv.at[slot], *sems[1])))
                slot += 1
            for _, _, one, two in moves:
                one.start()
                two.start()
            pump(1)
            for k, buf in enumerate((rzg, rzv)):
                rest = buf.at[pl.ds(at, len(moves))]
                remote(rest, rest, gz_send.at[k, stage], gz_recv.at[k, stage], z_peer(bit)).wait()
            for k, h, _, _ in moves:
                keep = flip(m, h)
                gb[c, q, keep, 0 : 2 * dr, :] += rzg[k].astype(F32)
                gb[c, q, keep, 2 * dr : pr, :] += rzv[k]
            pump(1)

    total = gb[c, q, m]
    ga[c, q, m] = total[0 : 2 * dr, :].astype(BF16)
    with jax.named_scope("spread_z"):
        first = SpreadZ(bits[-1], (ga,), az_send, az_recv)
        first.start()
        pump(2)
        for load in loads[4:14]:
            load.wait()
        g1_out[...] = total[0:dr, :]
        g2_out[...] = total[dr : 2 * dr, :]
        corr_one = 1.0 - beta_first**STEP
        corr_two = 1.0 - beta_second**STEP
        for t in range(6):
            row = 2 * dr + t * kb
            grad = total[row : row + kb, :]
            one = beta_first * m1_v[t] + (1.0 - beta_first) * grad
            two = beta_second * m2_v[t] + (1.0 - beta_second) * grad * grad
            m1_out[t] = one
            m2_out[t] = two
            mem_out[t] = mem_v[t] - adam_rate * (one / corr_one) / (jnp.sqrt(two / corr_two) + adam_eps)
        sums_out[...] = total[2 * dr + tr : pr, 0:LANES if F >= LANES else F]
        for bit in bits[::-1]:
            if bit != bits[-1]:
                pump(1)
                first = SpreadZ(bit, (ga,), az_send, az_recv)
                first.start()
            if bit == bits[0]:
                pump(len(items))
            if packed and bit == bits[0]:
                for o in z_order[:-1]:
                    unpack_from(o)
            first.wait()
    with jax.named_scope("spread_xy"):
        for o in xy_order:
            remote(ga.at[c, q], ga.at[c, q], ax_send, ax_recv, xy_peer(o)).start()
        if packed:
            for o in z_order[-1:]:
                unpack_from(o)
            with jax.named_scope("settle"):
                deal(xv, ig_out, 0, C, seats_s)
        rest = ga.at[c, pl.ds(0, Q - 1)]
        remote(rest, rest, ax_send, ax_recv, xy_peer(1)).wait()
    with jax.named_scope("spread_core"):
        remote(ga.at[c], ga.at[c], ac_send, ac_recv, core_peer).start()
        remote(ga.at[c], ga.at[1 - c], ac_send, ac_recv, core_peer).wait()
    with jax.named_scope("shampoo"):

        def place_g(i, carry):
            rows = pl.ds(multiple(i * dr, dr), dr)
            for j in range(M):
                cols = slice(j * F, (j + 1) * F)
                g1f[rows, cols] = ga[i % 2, i // 2, j, 0:dr, :]
                g2ft[rows, cols] = ga[i % 2, i // 2, j, dr : 2 * dr, :]
            return carry

        lax.fori_loop(0, N, place_g, 0)

        def turn_g(i, carry):
            here = pl.ds(multiple(i * LANES, LANES), LANES)
            for j in range(D // LANES):
                there = slice(j * LANES, (j + 1) * LANES)
                g1ft[there, here] = g1f[here, there].astype(F32).T.astype(BF16)
                g2f[there, here] = g2ft[here, there].astype(F32).T.astype(BF16)
            return carry

        lax.fori_loop(0, D // LANES, turn_g, 0)
        by_d = pl.ds(multiple(d * dr, dr), dr)
        by_m = pl.ds(multiple(m * F, F), F)

        def renewed(old, fresh):
            return stat_decay * old + (1.0 - stat_decay) * fresh

        l1_out[...] = renewed(l1_v[...], mm_t(g1f[by_d, :], g1f[by_m, :]))
        r1_out[...] = renewed(r1_v[...], mm_t(g1ft[by_d, :], g1ft[by_m, :]))
        l2_out[...] = renewed(l2_v[...], mm_t(g2f[by_d, :], g2f[by_m, :]))
        r2_out[...] = renewed(r2_v[...], mm_t(g2ft[by_d, :], g2ft[by_m, :]))

        def stepped(weight, left, grad, right):
            inner = jnp.dot(left[...], grad[...].astype(F32), precision=high, preferred_element_type=F32)
            return weight[...] - shampoo_rate * mm_t(inner, right[...], high)

        w1_out[...] = stepped(w1_v, p1_v, g1f, q1_v)
        w2_out[...] = stepped(w2_v, q2_v, g2ft, p2_v)

    with jax.named_scope("drain"):
        for kind, out in enumerate((lg_out,) if packed else (lg_out, ig_out)):
            remote(out, out, in_send.at[kind], out_recv.at[kind, 0], z_peer(1)).wait_recv()
        for kind, buf in enumerate((lgb, igb)):
            part = buf.at[pl.ds(0, others), pl.ds(0, (mine, cap)[kind])]
            remote(part, part, out_send.at[kind], out_recv.at[0, 0], z_peer(1)).wait_send()
        for kind, buf in enumerate((xb, cb)):
            part = buf.at[pl.ds(0, others), pl.ds(0, (mine, cap)[kind])]
            remote(part, part, in_send.at[kind], out_recv.at[0, 0], z_peer(1)).wait_send()


def finish(n_out, D, tiles, sums_ref, order_ref, *refs):
    outs = refs[n_out : 2 * n_out]
    rms_out, flag_out, order_s, rms_s, flag_s, sems = refs[2 * n_out :]
    copies = [pltpu.make_async_copy(refs[i], outs[i], sems.at[i]) for i in range(n_out)]
    if tiles:
        order = pltpu.make_async_copy(order_ref, order_s, sems.at[n_out])
        order.start()
    for copy in copies[1 if tiles else 0 :]:
        copy.start()
    sums = sums_ref[...]
    ratio = jnp.sqrt(sums / (sums[2:3, :] * D))
    rms_s[0] = ratio[0, 0]
    rms_s[1] = ratio[1, 0]
    flag_s[0] = jnp.where(sums[3, 0] > 0.0, 1, 0)
    for k, (src, dst) in enumerate(((rms_s, rms_out), (flag_s, flag_out))):
        copies.append(pltpu.make_async_copy(src, dst, sems.at[n_out + 1 + k]))
        copies[-1].start()
    if tiles:
        order.wait()

        def step(g, carry):
            for j in range(8):
                t = g * 8 + j
                here = pl.ds(multiple(t * LANES, LANES), LANES)
                there = pl.ds(multiple(order_s[0, t] * LANES, LANES), LANES)
                pltpu.make_async_copy(refs[0].at[:, here], outs[0].at[:, there], sems.at[0]).start()
            return carry

        lax.fori_loop(0, tiles // 8, step, 0)
    for copy in copies:
        copy.wait()


def solution(mesh):
    N, M = mesh.shape["dp"], mesh.shape["mp"]
    Q = N // 2

    def on_device(*args):
        x, cot, mask, members, m1, m2, w1, w2, l1, r1, l2, r2, p1, q1, p2, q2 = args
        mask, w2, l2, r2 = mask.T, w2.T, l2.T, r2.T
        args = (x, cot, mask, members, m1, m2, w1, w2, l1, r1, l2, r2, p1, q1, p2, q2)
        F, R = x.shape
        D = F * M
        mine = R // M
        w = min(CHUNK, mine)
        C = mine // w
        kb = members.shape[1]
        dr = w1.shape[0]
        tr = -(-6 * kb // 8) * 8
        pr = 2 * dr + tr + 8
        groups = mine // LANES
        S = jax.ShapeDtypeStruct
        V = pltpu.VMEM
        dma = pltpu.SemaphoreType.DMA
        outs = [S(x.shape, BF16), S(x.shape, BF16), S((8, min(F, LANES)), F32), S((1, LANES), jnp.int32)]
        outs += [S(a.shape, F32) for a in (w1, w1, l1, r1, w2, w2, l2, r2, m1, m2, members)]
        anywhere = pl.BlockSpec(memory_space=pl.ANY)
        vmem = pl.BlockSpec(memory_space=pltpu.VMEM)

        def run(cap, number):
            packed = cap < mine
            KC = -(-cap // w)

            def only(shape, dtype):
                return V(shape if packed else (16, LANES), dtype)

            scratch = [V(a.shape, a.dtype) for a in (mask, members, m1, m2, w1, w2, l1, r1, l2, r2, p1, q1, p2, q2)]
            scratch += [only((F, R), BF16)] * 4
            scratch += [V((1, LANES), jnp.int32), pltpu.SMEM((1, LANES), jnp.int32)]
            scratch += [V((1, LANES), jnp.int32), pltpu.SMEM((1, LANES), jnp.int32)]
            scratch += [only((M, F, KC * w), BF16), only((w, mine), BF16), only((M, F, KC * w), BF16)]
            scratch += [V((D, mine), BF16), V((D, KC * w), BF16), V((D, mine), BF16), V((D, KC * w), BF16)]
            scratch += [V((2, Q, M, 2 * dr, F), BF16), V((2, Q, M, tr, F), F32)]
            scratch += [V((D, D), BF16)] * 4
            scratch += [V((6, D, LANES), F32), V((6, K, D), F32), V(mask.shape[::-1], jnp.int32)]
            scratch += [V((M * groups, LANES), jnp.int32)] + [V((M * groups, LANES), F32)] * 2
            scratch += [V((D, w), F32)] * 4
            scratch += [V((D, w), BF16)] * 4
            scratch += [only((D, w), F32), only((D, mine), BF16)]
            scratch += [V((D, D), F32)] * 2
            scratch += [V((6, D, LANES), F32), V((6, K, D), F32), V((16, LANES), F32)]
            scratch += [V((2, Q, M, pr, F), F32), V((Q, M, pr, F), F32)]
            scratch += [V((Q, M, 2 * dr, F), BF16), V((Q, M, 2 * dr, F), BF16), V((Q, M, pr - 2 * dr, F), F32)]
            scratch += [V((M - 1, 2 * dr, F), BF16), V((M - 1, pr - 2 * dr, F), F32), V((M - 1, 2 * dr, F), BF16)]
            scratch += [V((2, Q, M, 2 * dr, F), BF16)]
            scratch += [V((D, D), BF16)] * 4
            Z = M.bit_length() - 1
            scratch += [dma((18,)), dma((2,)), dma((C,)), dma((2,)), dma((2, M))]
            scratch += [dma((2, Z)), dma((2, Z)), dma((2,)), dma((2,)), dma((2,)), dma((2,))]
            scratch += [dma((Q,)), dma((Q,)), dma((2,)), dma((2,)), dma((2, Z)), dma((2, Z))]
            scratch += [dma((1, Z)), dma((1, Z)), dma, dma, dma, dma]
            res = pl.pallas_call(
                functools.partial(kernel, N, M, cap),
                out_shape=[V(a.shape, a.dtype) for a in outs],
                in_specs=[anywhere] * 16,
                out_specs=[vmem] * 15,
                scratch_shapes=scratch,
                compiler_params=pltpu.CompilerParams(
                    collective_id=number, has_side_effects=True, vmem_limit_bytes=46 << 20
                ),
                name="packed" if packed else "whole",
            )(*[pltpu.with_memory_space_constraint(a, pltpu.HBM) for a in args])
            kept = [*res[:2], *res[4:]]
            *done, rms, flag = pl.pallas_call(
                functools.partial(finish, len(kept), D, M * groups if packed else 0),
                out_shape=[S(a.shape, a.dtype) for a in kept] + [S((2,), F32), S((1,), jnp.int32)],
                in_specs=[vmem, anywhere] + [anywhere] * len(kept),
                out_specs=[anywhere] * (len(kept) + 2),
                scratch_shapes=[
                    pltpu.SMEM((1, LANES), jnp.int32),
                    pltpu.SMEM((2,), F32),
                    pltpu.SMEM((1,), jnp.int32),
                    dma((len(kept) + 3,)),
                ],
                compiler_params=pltpu.CompilerParams(vmem_limit_bytes=16 << 20),
                name="finish",
            )(res[2], res[3], *kept)
            return flag, (*done, rms)

        flag, fast = run(-(-mine * 11 // (16 * LANES)) * LANES, 0)
        done = lax.cond(flag[0] > 0, lambda: run(mine, 1)[1], lambda: fast)
        logits, igrad, g1, n1, l1, r1, g2, n2, l2, r2, m1, m2, new, rms = done
        return (logits, igrad, rms, g1, n1, l1, r1, g2.T, n2.T, l2.T, r2.T, m1, m2, new)

    placed = (
        P("mp", "dp"),
        P("mp", "dp"),
        P("dp", None),
        P(None, "dp", "mp"),
        P(None, "dp", "mp"),
        P(None, "dp", "mp"),
        P("dp", "mp"),
        P("mp", "dp"),
        P("dp", "mp"),
        P("dp", "mp"),
        P("mp", "dp"),
        P("mp", "dp"),
        P("dp", None),
        P("mp", None),
        P("mp", None),
        P("dp", None),
    )
    return jax.shard_map(
        on_device,
        mesh=mesh,
        in_specs=placed,
        out_specs=(
            P("mp", "dp"),
            P("mp", "dp"),
            P(),
            P("dp", "mp"),
            P("dp", "mp"),
            P("dp", "mp"),
            P("dp", "mp"),
            P("mp", "dp"),
            P("mp", "dp"),
            P("mp", "dp"),
            P("mp", "dp"),
            P(None, "dp", "mp"),
            P(None, "dp", "mp"),
            P(None, "dp", "mp"),
        ),
        check_vma=False,
    )
```

```python
import functools

import jax
import jax.numpy as jnp
from jax import lax
from jax.experimental import pallas as pl
from jax.experimental.pallas import tpu as pltpu
from jax.sharding import PartitionSpec as P

K = 32
STEP = 10
LANES = 128
CHUNK = 256
ROWS = 32
AHEAD = 2
FIRST = 4
LEAST = 8

beta_first = 0.9
beta_second = 0.999
adam_eps = 1e-08
adam_rate = 0.2
stat_decay = 0.95
shampoo_rate = 1.0
curve_a = 0.7978845608028654
curve_b = 0.044715

MESH = pl.DeviceIdType.MESH
F32 = jnp.float32
BF16 = jnp.bfloat16
over_lanes = (((1,), (1,)), ((), ()))


def flip(index, mask):
    bit = 1
    while bit <= mask:
        if mask & bit:
            index = index + bit - 2 * bit * ((index // bit) % 2)
        bit *= 2
    return index


def mm(a, b):
    return jnp.dot(a, b, preferred_element_type=F32)


def mm_t(a, b, precision=None):
    return lax.dot_general(a, b, over_lanes, precision=precision, preferred_element_type=F32)


def multiple(value, by):
    return pl.multiple_of(value, by)


def kernel(
    N,
    M,
    cap,
    x_hbm,
    cot_hbm,
    mask_hbm,
    mem_hbm,
    m1_hbm,
    m2_hbm,
    w1_hbm,
    w2_hbm,
    l1_hbm,
    r1_hbm,
    l2_hbm,
    r2_hbm,
    p1_hbm,
    q1_hbm,
    p2_hbm,
    q2_hbm,
    lg_out,
    ig_out,
    sums_out,
    order_out,
    g1_out,
    w1_out,
    l1_out,
    r1_out,
    g2_out,
    w2_out,
    l2_out,
    r2_out,
    m1_out,
    m2_out,
    mem_out,
    mask_v,
    mem_v,
    m1_v,
    m2_v,
    w1_v,
    w2_v,
    l1_v,
    r1_v,
    l2_v,
    r2_v,
    p1_v,
    q1_v,
    p2_v,
    q2_v,
    xv,
    xp,
    cv,
    cq,
    order_v,
    order_s,
    seats_v,
    seats_s,
    cp,
    st,
    igr,
    xb,
    cb,
    lgb,
    igb,
    wb,
    tb,
    w1,
    w1t,
    w2,
    w2t,
    tab,
    stage,
    mt,
    mp,
    mk,
    rk,
    hp,
    hid,
    dgm,
    prod,
    sc,
    hi,
    gp,
    gpre,
    cx,
    ig,
    g1,
    g2t,
    vec,
    vt,
    stat,
    gb,
    rcore,
    xs,
    rxg,
    rxv,
    rzg,
    rzv,
    zs,
    ga,
    g1f,
    g1ft,
    g2f,
    g2ft,
    local_sem,
    in_send,
    in_recv,
    out_send,
    out_recv,
    wz_send,
    wz_recv,
    wx_send,
    wx_recv,
    wc_send,
    wc_recv,
    gc_send,
    gc_recv,
    gx_send,
    gx_recv,
    gz_send,
    gz_recv,
    az_send,
    az_recv,
    ax_send,
    ax_recv,
    ac_send,
    ac_recv,
):
    F, R = x_hbm.shape
    D = F * M
    Q = N // 2
    mine = R // M
    w = min(CHUNK, mine)
    C = mine // w
    tiles = w // LANES
    packed = cap < mine
    KC = -(-cap // w)
    groups = mine // LANES
    kb = K // N
    dr = D // N
    tr = tb.shape[3]
    pr = gb.shape[3]
    blocks = D // ROWS
    high = lax.Precision.HIGHEST

    d, m = lax.axis_index("dp"), lax.axis_index("mp")
    c, q = d % 2, d // 2

    def z_peer(o):
        return (d, flip(m, o))

    def xy_peer(o):
        return (flip(q, o) * 2 + c, m)

    core_peer = (flip(d, 1), m)
    z_order = sorted(range(1, M), reverse=True)
    bits = [1 << k for k in range(M.bit_length() - 1)]
    xy_order = sorted(range(1, Q), reverse=True)

    def remote(src, dst, send, recv, peer):
        return pltpu.make_async_remote_copy(
            src_ref=src, dst_ref=dst, send_sem=send, recv_sem=recv, device_id=peer, device_id_type=MESH
        )

    pairs = (
        (mask_hbm, mask_v),
        (mem_hbm, mem_v),
        (w1_hbm, w1_v),
        (w2_hbm, w2_v),
        (m1_hbm, m1_v),
        (m2_hbm, m2_v),
        (l1_hbm, l1_v),
        (r1_hbm, r1_v),
        (l2_hbm, l2_v),
        (r2_hbm, r2_v),
        (p1_hbm, p1_v),
        (q1_hbm, q1_v),
        (p2_hbm, p2_v),
        (q2_hbm, q2_v),
    )
    if packed:
        pairs = (*pairs, (cot_hbm, cv), (x_hbm, xv))
    loads = [pltpu.make_async_copy(a, b, local_sem.at[i if i < 6 else max(6, i - 7)]) for i, (a, b) in enumerate(pairs)]
    for load in loads:
        load.start()

    per_mask = LANES // K
    total_tiles = M * groups

    I32 = jnp.int32

    def masks_to(ref):
        loads[0].wait()
        mt[...] = mask_v[...].T
        ref[...] = jnp.concatenate(
            [mt[pl.ds(j, total_tiles, stride=per_mask), :] for j in range(per_mask)], axis=1
        )

    def across(row):
        return jnp.broadcast_to(row, (LANES, LANES)).T

    def order_tiles():
        masks_to(mp)
        tall = jnp.concatenate([mp[...], jnp.zeros((LANES - total_tiles, LANES), I32)], axis=0)
        count = jnp.sum(tall.T, axis=0, keepdims=True)
        line_id = lax.broadcasted_iota(I32, (LANES, LANES), 0)
        lane_id = lax.broadcasted_iota(I32, (LANES, LANES), 1)
        mine_here, other = jnp.broadcast_to(count, (LANES, LANES)), across(count)
        before = (other > mine_here) | ((other == mine_here) & (line_id < lane_id))
        dealt = (line_id < total_tiles) & (line_id % groups != 0)
        rank = jnp.sum(jnp.where(before & dealt, 1, 0), axis=0, keepdims=True)
        turn, seat = rank // M, rank % M
        block = jnp.where(turn % 2 == 0, seat, M - 1 - seat)
        lane = lax.broadcasted_iota(I32, (1, LANES), 1)
        seats = jnp.where(lane % groups == 0, lane, block * groups + 1 + turn)
        seats = jnp.where(lane < total_tiles, seats, LANES)
        seats_v[...] = seats
        order_v[...] = jnp.sum(jnp.where(across(seats) == lane_id, line_id, 0), axis=0, keepdims=True)
        order_out[...] = order_v[...]
        to_scalars = pltpu.make_async_copy(order_v, order_s, local_sem.at[9])
        to_scalars.start()
        loads[15].wait()
        to_scalars.wait()
        deal(xv, xp, 0, 1)

    def deal(src, dst, start, end, order=None):
        order = order_s if order is None else order


        def step(i, carry):
            for p in range(M):
                for j in range(tiles):
                    t = p * groups + i * tiles + j
                    dst[:, pl.ds(multiple(t * LANES, LANES), LANES)] = src[
                        :, pl.ds(order[0, t] * LANES, LANES)
                    ]
            return carry

        lax.fori_loop(start, end, step, 0)

    with jax.named_scope("barrier"):
        entry = pltpu.get_barrier_semaphore()
        peers = [z_peer(o) for o in z_order] + [xy_peer(o) for o in xy_order] + [core_peer]
        for peer in peers:
            pl.semaphore_signal(entry, inc=1, device_id=peer, device_id_type=MESH)
        for load in loads[1:4]:
            load.wait()
        wb[c, q, m, 0:dr, :] = w1_v[...].astype(BF16)
        wb[c, q, m, dr : 2 * dr, :] = w2_v[...].astype(BF16)
        for t in range(6):
            tb[c, q, m, t * kb : (t + 1) * kb, :] = mem_v[t]
        pl.semaphore_wait(entry, len(peers))

    kinds_in = (xb, cb)

    def at_width(i, act):
        if not packed:
            act(w)
        elif isinstance(i, int):
            if i < KC:
                act(min(w, cap - i * w))
        elif cap % w == 0:
            pl.when(i < KC)(lambda: act(w))
        else:
            pl.when(i < KC - 1)(lambda: act(w))
            pl.when(i == KC - 1)(lambda: act(cap % w))

    def send_tile(j, src):
        here = pl.ds(multiple(m * F, F), F)
        there = xb.at[here, j * LANES : (j + 1) * LANES]

        def tile(to):
            return src.at[:, pl.ds(multiple(to * mine + j * LANES, LANES), LANES)]

        for o in z_order:
            to = flip(m, o)
            remote(tile(to), there, in_send.at[0], in_recv.at[0], (d, to)).start()
        pltpu.make_async_copy(tile(m), there, in_recv.at[0]).start()

    def send_in(i, kinds=(0, 1)):
        here = pl.ds(multiple(m * F, F), F)

        def source(kind, to, width):
            if kind and packed:
                return cp.at[to, :, pl.ds(multiple(i * w, w), width)]
            hbm = xp if packed else (x_hbm, cot_hbm)[kind]
            return hbm.at[:, pl.ds(multiple(to * mine + i * w, w), width)]

        def start(kind, width):
            there = kinds_in[kind].at[here, pl.ds(multiple(i * w, w), width)]
            for o in z_order:
                to = flip(m, o)
                remote(source(kind, to, width), there, in_send.at[kind], in_recv.at[i], (d, to)).start()
            pltpu.make_async_copy(source(kind, m, width), there, in_recv.at[i]).start()

        for kind in kinds:
            if kind:
                at_width(i, functools.partial(start, 1))
            else:
                start(0, w)

    others = (M - 1) * F

    def wait_in(i):
        def arrive(width):
            part = xb.at[:, pl.ds(0, w + width)]
            remote(part, part, in_send.at[0], in_recv.at[i], z_peer(1)).wait_recv()

        at_width(i, arrive)
        if packed:
            pl.when(i >= KC)(lambda: arrive(0))

    def width_of(kind, i):
        return min(w, cap - i * w) if kind and packed else w

    def send_out(kind, i):
        col = pl.ds(multiple(i * w, w), width_of(kind, i))
        if kind and packed:
            there = igr.at[m, :, col]
        else:
            there = (lg_out, ig_out)[kind].at[:, pl.ds(multiple(m * mine + i * w, w), w)]
        buf = (lgb, igb)[kind]
        for o in z_order[::-1]:
            to = flip(m, o)
            recv = out_recv.at[o if kind and packed else kind]
            remote(buf.at[pl.ds(multiple(to * F, F), F), col], there, out_send.at[kind], recv, (d, to)).start()
        if not (kind and packed):
            pltpu.make_async_copy(buf.at[pl.ds(multiple(m * F, F), F), col], there, out_recv.at[kind]).start()

    line = lax.broadcasted_iota(jnp.int32, (w, LANES), 0).astype(F32)

    def matches(p, k, i):
        base = (k * w) * jnp.float32(1) if isinstance(k, int) else (k * w).astype(F32)
        parts = []
        for j in range(tiles):
            row = rk[pl.ds(p * groups + i * tiles + j, 1), :] - base
            parts.append(jnp.where(line == row, 1.0, 0.0).astype(BF16))
        return jnp.concatenate(parts, axis=1)

    spread_by = K // LEAST

    def pack_block(k, p):
        def step(i, acc):
            cols = pl.ds(multiple(p * mine + i * w, w), w)
            return acc + mm_t(cq[:, cols], matches(p, k, i))

        acc = lax.fori_loop(k, min(C, spread_by * k + spread_by), step, jnp.zeros((F, w), F32))
        cp[p, :, k * w : (k + 1) * w] = acc.astype(BF16)

    def shrink(k):
        with jax.named_scope("shrink"):
            end = min(C, spread_by * k + spread_by)

            def step(i, carry):
                st[:, pl.ds(multiple(i * w, w), w)] = matches(m, k, i)
                return carry

            lax.fori_loop(k, end, step, 0)
            part = slice(k * w, end * w)
            igb[:, k * w : (k + 1) * w] = mm_t(ig[:, part], st[:, part]).astype(BF16)

    def pack_chunk(k):
        with jax.named_scope("pack_cot"):

            def step(p, carry):
                pack_block(k, p)
                return carry

            lax.fori_loop(0, M, step, 0)

    def unpack_block(p):
        with jax.named_scope("unpack"):

            def chunk(i, carry):
                def step(k, acc):
                    return acc + mm(igr[p, :, pl.ds(multiple(k * w, w), w)], matches(p, k, i))

                acc = lax.fori_loop(i // spread_by, jnp.minimum(i, KC - 1) + 1, step, jnp.zeros((F, w), F32))
                xv[:, pl.ds(multiple(p * mine + i * w, w), w)] = acc.astype(BF16)
                return carry

            lax.fori_loop(0, C, chunk, 0)

    def unpack_from(o):
        part = igr.at[0, :, pl.ds(0, cap)]
        remote(part, part, in_send.at[0], out_recv.at[o], z_peer(o)).wait_recv()
        unpack_block(flip(m, o))

    if not packed:
        order_out[...] = jnp.zeros_like(order_out)
    class SpreadZ:
        def __init__(self, bit, bufs, send, recv):
            self.go, self.come = [], []
            offsets = list(range(0, M, 2 * bit))
            for k, buf in enumerate(bufs):
                sems = (send.at[k, bits.index(bit)], recv.at[k, bits.index(bit)], z_peer(bit))
                for h in offsets:
                    slot = buf.at[c, q, flip(m, h)]
                    self.go.append(remote(slot, slot, *sems))
                both = buf.at[c, q, pl.ds(0, len(offsets))]
                self.come.append(remote(both, both, *sems))

        def start(self):
            for copy in self.go:
                copy.start()

        def wait(self):
            for copy in self.come:
                copy.wait()

    bufs = (wb, tb)
    first = SpreadZ(bits[-1], bufs, wz_send, wz_recv)
    first.start()
    if packed:
        send_tile(0, x_hbm)
        order_tiles()
        for j in range(1, tiles):
            send_tile(j, xp)
    else:
        send_in(0)
    if not packed:
        masks_to(mp)
        mk[...] = mp[...].astype(F32)
    else:
        deal(xv, xp, 1, C)
        to_seats = pltpu.make_async_copy(seats_v, seats_s, local_sem.at[10])
        to_seats.start()

        def deal_masks(t, carry):
            for j in range(8):
                mk[pl.ds(t * 8 + j, 1), :] = mp[pl.ds(order_s[0, t * 8 + j], 1), :].astype(F32)
            return carry

        lax.fori_loop(0, total_tiles // 8, deal_masks, 0)
        to_seats.wait()
        flags = mk[...]
        rows, cols = M * groups, LANES
        lower = lax.broadcasted_iota(jnp.int32, (cols, cols), 0) < lax.broadcasted_iota(jnp.int32, (cols, cols), 1)
        inside = mm(flags.astype(BF16), jnp.where(lower, 1.0, 0.0).astype(BF16))
        sums = jnp.broadcast_to(jnp.sum(flags, axis=1, keepdims=True), (rows, cols)).astype(BF16)
        one = lax.broadcasted_iota(jnp.int32, (rows, rows), 0)
        two = lax.broadcasted_iota(jnp.int32, (rows, rows), 1)
        ahead = (two < one) & (two >= one - one % groups)
        place_in = inside + mm(jnp.where(ahead, 1.0, 0.0).astype(BF16), sums)
        rk[...] = jnp.where(flags > 0.0, place_in, -1.0)
    def clear(i, carry):
        rows = pl.ds(multiple(i * ROWS, ROWS), ROWS)
        g1[rows, :] = jnp.zeros((ROWS, D), F32)
        g2t[rows, :] = jnp.zeros((ROWS, D), F32)
        for t in range(6):
            vec[t, rows, :] = jnp.zeros((ROWS, LANES), F32)
        return carry

    lax.fori_loop(0, blocks, clear, 0)
    stat[...] = jnp.zeros_like(stat)

    ahead_of = min(FIRST, C)
    if packed:
        loads[14].wait()
        deal(cv, cq, 0, C)
        if cap % w:
            cb[:, cap : KC * w] = jnp.zeros((D, KC * w - cap), BF16)
            for p in range(M):
                igr[p, :, cap : KC * w] = jnp.zeros((F, KC * w - cap), BF16)
        pack_chunk(0)

    def step_in(k):
        if packed:
            if k < KC:
                send_in(k, (1,))
            if k + 1 < ahead_of:
                send_in(k + 1, (0,))
            if k + 1 < KC:
                pack_chunk(k + 1)
        elif k + 1 < ahead_of:
            send_in(k + 1)

    with jax.named_scope("weights_z"):
        for bit in bits[::-1]:
            if bit != bits[-1]:
                first = SpreadZ(bit, bufs, wz_send, wz_recv)
                first.start()
            if bit == bits[0]:
                step_in(0)
            first.wait()
    with jax.named_scope("weights_xy"):
        for o in xy_order:
            for k, buf in enumerate(bufs):
                remote(buf.at[c, q], buf.at[c, q], wx_send.at[k], wx_recv.at[k], xy_peer(o)).start()
        step_in(1)
        step_in(2)
        for k, buf in enumerate(bufs):
            rest = buf.at[c, pl.ds(0, Q - 1)]
            remote(rest, rest, wx_send.at[k], wx_recv.at[k], xy_peer(1)).wait()
    with jax.named_scope("weights_core"):
        for k, buf in enumerate(bufs):
            remote(buf.at[c], buf.at[c], wc_send.at[k], wc_recv.at[k], core_peer).start()
        for k in range(3, max(ahead_of, KC if packed else 0)):
            if k < ahead_of:
                step_in(k)
            elif k + 1 < KC:
                pack_chunk(k + 1)
        for k, buf in enumerate(bufs):
            remote(buf.at[c], buf.at[1 - c], wc_send.at[k], wc_recv.at[k], core_peer).wait()

    with jax.named_scope("weights_spread"):

        def place(i, carry):
            rows = pl.ds(multiple(i * dr, dr), dr)
            for j in range(M):
                cols = slice(j * F, (j + 1) * F)
                w1[rows, cols] = wb[i % 2, i // 2, j, 0:dr, :]
                w2t[rows, cols] = wb[i % 2, i // 2, j, dr : 2 * dr, :]
            return carry

        lax.fori_loop(0, N, place, 0)

        def turn(i, carry):
            here = pl.ds(multiple(i * LANES, LANES), LANES)
            for j in range(D // LANES):
                there = slice(j * LANES, (j + 1) * LANES)
                w1t[there, here] = w1[here, there].astype(F32).T.astype(BF16)
                w2[there, here] = w2t[here, there].astype(F32).T.astype(BF16)
            return carry

        lax.fori_loop(0, D // LANES, turn, 0)
        for t in range(6):
            for i in range(N):
                for j in range(M):
                    stage[t, i * kb : (i + 1) * kb, j * F : (j + 1) * F] = tb[
                        i % 2, i // 2, j, t * kb : (t + 1) * kb, :
                    ]

        def table(t, carry):
            for j in range(D // LANES):
                cols = slice(j * LANES, (j + 1) * LANES)
                piece = stage[t, :, cols]
                tab[t, cols, :] = jnp.concatenate([piece] * per_mask, axis=0).T
            return carry

        lax.fori_loop(0, 6, table, 0)

    def eight(value):
        return value.reshape(ROWS // 8, 8, LANES).sum(0)

    if packed:
        early = [(C - 2, [(0, 0)]), (C - 1, [(0, 1), (0, 2)])]
    else:
        early = [(C - 2, [(0, 0), (1, 0)]), (C - 1, [(0, 1), (1, 1)])]

    def work(i, carry):
        col = multiple(i * w, w)
        with jax.named_scope("wait_in"):
            wait_in(i)

        @pl.when((i + AHEAD >= FIRST) & (i + AHEAD < C - 1))
        def _():
            send_in(i + AHEAD)

        if C > FIRST:

            @pl.when(i + AHEAD == C - 2)
            def _():
                send_in(C - 1)

        for late, parts in early:
            for kind, k in parts:
                pl.when(i == late)(functools.partial(send_out, kind, k))

        masks = [mk[pl.ds(m * groups + i * tiles + j, 1), :] for j in range(tiles)]

        def place_of(r):
            return pl.ds(multiple(r * ROWS, ROWS), ROWS)

        def lanes_of(j):
            return pl.ds(multiple(col + j * LANES, LANES), LANES)

        def scale_rows(r, sums):
            rows = place_of(r)
            row_in = tab[0, rows, :]
            new = []
            for j in range(tiles):
                x = xb[rows, lanes_of(j)].astype(F32)
                sc[rows, j * LANES : (j + 1) * LANES] = (x * row_in).astype(BF16)
                new.append(sums[j] + eight(x * x))
            return tuple(new)

        zero = tuple(jnp.zeros((8, LANES), F32) for _ in range(tiles))
        with jax.named_scope("scale"):
            x_sums = lax.fori_loop(0, blocks, scale_rows, zero)
        with jax.named_scope("mm_one"):
            hp[...] = mm(w1t[...], sc[...])

        def curve_rows(r, carry):
            rows = place_of(r)
            gain, bias, row_mid = tab[1, rows, :], tab[2, rows, :], tab[3, rows, :]
            for j in range(tiles):
                cols = slice(j * LANES, (j + 1) * LANES)
                s = hp[rows, cols] * gain + bias
                s2 = s * s
                th = jnp.tanh(curve_a * (s + curve_b * (s2 * s)))
                cdf = 0.5 * (1.0 + th)
                h = s * cdf
                slope = cdf + (0.5 * s) * (1.0 - th * th) * (curve_a + (3.0 * curve_a * curve_b) * s2)
                hid[rows, cols] = h
                dgm[rows, cols] = slope * row_mid
                hi[rows, cols] = (h * row_mid).astype(BF16)
            return carry

        with jax.named_scope("curve"):
            lax.fori_loop(0, blocks, curve_rows, 0)
        with jax.named_scope("mm_two"):
            prod[...] = mm(w2t[...], hi[...])
        low, high_k = i // spread_by, jnp.minimum(i, KC - 1)
        if packed:
            with jax.named_scope("expand"):

                def grow(k, carry):
                    cx[...] += mm(cb[:, pl.ds(multiple(k * w, w), w)], matches(m, k, i))
                    return carry

                cx[...] = jnp.zeros_like(cx)
                lax.fori_loop(low, high_k + 1, grow, 0)

        def grad_of(rows, j):
            if packed:
                return cx[rows, j * LANES : (j + 1) * LANES]
            return cb[rows, lanes_of(j)].astype(F32) * masks[j]


        def out_rows(r, sums):
            rows = place_of(r)
            gain, bias = tab[4, rows, :], tab[5, rows, :]
            v4, v5 = vec[4, rows, :], vec[5, rows, :]
            new = []
            for j in range(tiles):
                cols = slice(j * LANES, (j + 1) * LANES)
                x = xb[rows, lanes_of(j)].astype(F32)
                projected = prod[rows, cols]
                branch = projected * gain + bias
                lgb[rows, lanes_of(j)] = (x + branch).astype(BF16)
                new.append(sums[j] + eight(branch * branch))
                go = grad_of(rows, j)
                v5 = v5 + go
                v4 = v4 + go * projected
                gp[rows, cols] = (go * gain).astype(BF16)
            vec[4, rows, :] = v4
            vec[5, rows, :] = v5
            return tuple(new)

        with jax.named_scope("out"):
            b_sums = lax.fori_loop(0, blocks, out_rows, zero)
        for j in range(tiles):
            stat[0:8, :] += x_sums[j] * masks[j]
            stat[8:16, :] += b_sums[j] * masks[j]

        with jax.named_scope("mm_three"):
            half = D // 2
            for k in range(2):
                part = slice(k * half, (k + 1) * half)
                g2t[part, :] += mm_t(gp[part, :], hi[...])
            prod[...] = mm(w2[...], gp[...])

        def back_rows(r, carry):
            rows = place_of(r)
            gain = tab[1, rows, :]
            v1, v2, v3 = vec[1, rows, :], vec[2, rows, :], vec[3, rows, :]
            for j in range(tiles):
                cols = slice(j * LANES, (j + 1) * LANES)
                gh = prod[rows, cols]
                v3 = v3 + gh * hid[rows, cols]
                gs = gh * dgm[rows, cols]
                v2 = v2 + gs
                v1 = v1 + gs * hp[rows, cols]
                gpre[rows, cols] = (gs * gain).astype(BF16)
            vec[1, rows, :] = v1
            vec[2, rows, :] = v2
            vec[3, rows, :] = v3
            return carry

        with jax.named_scope("back"):
            lax.fori_loop(0, blocks, back_rows, 0)
        with jax.named_scope("mm_four"):
            for k in range(2):
                part = slice(k * half, (k + 1) * half)
                g1[part, :] += mm_t(sc[part, :], gpre[...])
            prod[...] = mm(w1[...], gpre[...])

        def in_rows(r, carry):
            rows = place_of(r)
            row_in = tab[0, rows, :]
            v0 = vec[0, rows, :]
            for j in range(tiles):
                cols = slice(j * LANES, (j + 1) * LANES)
                gs = prod[rows, cols]
                v0 = v0 + gs * xb[rows, lanes_of(j)].astype(F32)
                go = grad_of(rows, j)
                done = (gs * row_in + go).astype(BF16)
                if packed:
                    ig[rows, lanes_of(j)] = done
                else:
                    igb[rows, lanes_of(j)] = done
            vec[0, rows, :] = v0
            return carry

        with jax.named_scope("in"):
            lax.fori_loop(0, blocks, in_rows, 0)
        if packed:
            xv[:, pl.ds(multiple(m * mine + col, w), w)] = ig[pl.ds(multiple(m * F, F), F), pl.ds(col, w)]
        return carry

    lax.fori_loop(0, C, work, 0)

    items = [item for _, parts in early for item in parts]
    already = len(items)
    if packed:
        items += [(1, k) for k in range(KC)] + [(0, i) for i in range(3, C)]
    else:
        items += [(kind, i) for i in range(2, C) for kind in range(2)]
    state = {"sent": already}

    def pump(count):
        with jax.named_scope("pump"):
            for kind, k in items[state["sent"] : state["sent"] + count]:
                if kind and packed:
                    shrink(k)
                send_out(kind, k)
            state["sent"] += count

    with jax.named_scope("pack"):

        def pack_g(i, carry):
            rows = pl.ds(multiple(i * dr, dr), dr)
            for j in range(M):
                cols = slice(j * F, (j + 1) * F)
                gb[i % 2, i // 2, j, 0:dr, :] = g1[rows, cols]
                gb[i % 2, i // 2, j, dr : 2 * dr, :] = g2t[rows, cols]
            return carry

        lax.fori_loop(0, N, pack_g, 0)

        def fold(t, carry):
            for j in range(D // LANES):
                cols = slice(j * LANES, (j + 1) * LANES)
                turned = vec[t, cols, :].T
                vt[t, :, cols] = sum(turned[k * K : (k + 1) * K, :] for k in range(per_mask))
            return carry

        lax.fori_loop(0, 6, fold, 0)
        for t in range(6):
            for i in range(N):
                for j in range(M):
                    row = 2 * dr + t * kb
                    gb[i % 2, i // 2, j, row : row + kb, :] = vt[t, i * kb : (i + 1) * kb, j * F : (j + 1) * F]
        own = mk[pl.ds(multiple(m * groups, groups), groups), :]
        totals = [stat[0:8, :], stat[8:16, :], own]
        rows8 = [jnp.sum(v, keepdims=True).reshape(1, 1) for v in totals]
        rows8.append(jnp.where(rows8[2] > cap, 1.0, 0.0))
        row_id = lax.broadcasted_iota(jnp.int32, (8, F), 0)
        lines = sum(jnp.where(row_id == k, v, 0.0) for k, v in enumerate(rows8))

        def put(i, carry):
            for j in range(M):
                gb[i % 2, i // 2, j, 2 * dr + tr : pr, :] = lines
            return carry

        lax.fori_loop(0, N, put, 0)

    with jax.named_scope("sum_core"):
        for o in xy_order + [0]:
            k = flip(q, o)
            remote(gb.at[1 - c, k], rcore.at[k], gc_send, gc_recv.at[o], core_peer).start()

        def add_core(k):
            def step(j, carry):
                gb[c, k, j] += rcore[k, j]
                return carry

            lax.fori_loop(0, M, step, 0)

        def over_xy(o):
            k = flip(q, o)
            sems = [(gx_send.at[n], gx_recv.at[n], xy_peer(o)) for n in range(2)]
            tail = gb.at[c, k, :, pl.ds(2 * dr, pr - 2 * dr), :]
            return remote(xs.at[o], rxg.at[o], *sems[0]), remote(tail, rxv.at[o], *sems[1])

        for o in xy_order + [0]:
            k = flip(q, o)
            remote(gb.at[1 - c, k], rcore.at[k], gc_send, gc_recv.at[o], core_peer).wait_recv()
            add_core(k)
            if o:

                def round_piece(j, carry):
                    xs[o, j] = gb[c, k, j, 0 : 2 * dr, :].astype(BF16)
                    return carry

                lax.fori_loop(0, M, round_piece, 0)
                for copy in over_xy(o):
                    copy.start()
    pump(2)
    with jax.named_scope("sum_xy"):
        for n, buf in enumerate((rxg, rxv)):
            rest = buf.at[pl.ds(1, Q - 1)]
            remote(rest, rest, gx_send.at[n], gx_recv.at[n], xy_peer(1)).wait()
        for o in xy_order:

            def step(j, carry):
                gb[c, q, j, 0 : 2 * dr, :] += rxg[o, j].astype(F32)
                gb[c, q, j, 2 * dr : pr, :] += rxv[o, j]
                return carry

            lax.fori_loop(0, M, step, 0)
    with jax.named_scope("sum_z"):
        slot = 0
        for stage, bit in enumerate(bits):
            moves = []
            at = slot
            for h in range(0, M, 2 * bit):
                away = flip(m, h + bit)
                zs[slot] = gb[c, q, away, 0 : 2 * dr, :].astype(BF16)
                sems = [(gz_send.at[k, stage], gz_recv.at[k, stage], z_peer(bit)) for k in range(2)]
                tail = gb.at[c, q, away, pl.ds(2 * dr, pr - 2 * dr), :]
                moves.append((slot, h, remote(zs.at[slot], rzg.at[slot], *sems[0]), remote(tail, rzv.at[slot], *sems[1])))
                slot += 1
            for _, _, one, two in moves:
                one.start()
                two.start()
            pump(1)
            for k, buf in enumerate((rzg, rzv)):
                rest = buf.at[pl.ds(at, len(moves))]
                remote(rest, rest, gz_send.at[k, stage], gz_recv.at[k, stage], z_peer(bit)).wait()
            for k, h, _, _ in moves:
                keep = flip(m, h)
                gb[c, q, keep, 0 : 2 * dr, :] += rzg[k].astype(F32)
                gb[c, q, keep, 2 * dr : pr, :] += rzv[k]
            pump(1)

    total = gb[c, q, m]
    ga[c, q, m] = total[0 : 2 * dr, :].astype(BF16)
    with jax.named_scope("spread_z"):
        first = SpreadZ(bits[-1], (ga,), az_send, az_recv)
        first.start()
        pump(2)
        for load in loads[4:6]:
            load.wait()
        lines = 4 * dr * F // D + 2 * dr + 2 * F
        pltpu.make_async_copy(g1.at[0:lines], g1.at[0:lines], local_sem.at[6]).wait()
        g1_out[...] = total[0:dr, :]
        g2_out[...] = total[dr : 2 * dr, :]
        corr_one = 1.0 - beta_first**STEP
        corr_two = 1.0 - beta_second**STEP
        for t in range(6):
            row = 2 * dr + t * kb
            grad = total[row : row + kb, :]
            one = beta_first * m1_v[t] + (1.0 - beta_first) * grad
            two = beta_second * m2_v[t] + (1.0 - beta_second) * grad * grad
            m1_out[t] = one
            m2_out[t] = two
            mem_out[t] = mem_v[t] - adam_rate * (one / corr_one) / (jnp.sqrt(two / corr_two) + adam_eps)
        sums_out[...] = total[2 * dr + tr : pr, 0:LANES if F >= LANES else F]
        for bit in bits[::-1]:
            if bit != bits[-1]:
                pump(1)
                first = SpreadZ(bit, (ga,), az_send, az_recv)
                first.start()
            if bit == bits[0]:
                pump(len(items))
            if packed and bit == bits[0]:
                for o in z_order[:-1]:
                    unpack_from(o)
            first.wait()
    with jax.named_scope("spread_xy"):
        for o in xy_order:
            remote(ga.at[c, q], ga.at[c, q], ax_send, ax_recv, xy_peer(o)).start()
        if packed:
            for o in z_order[-1:]:
                unpack_from(o)
            with jax.named_scope("settle"):
                deal(xv, ig_out, 0, C, seats_s)
        rest = ga.at[c, pl.ds(0, Q - 1)]
        remote(rest, rest, ax_send, ax_recv, xy_peer(1)).wait()
    with jax.named_scope("spread_core"):
        remote(gb.at[1 - c], rcore, gc_send, gc_recv.at[0], core_peer).wait_send()
        remote(ga.at[c], ga.at[c], ac_send, ac_recv, core_peer).start()
        remote(ga.at[c], ga.at[1 - c], ac_send, ac_recv, core_peer).wait()
    with jax.named_scope("shampoo"):

        def place_g(i, carry):
            rows = pl.ds(multiple(i * dr, dr), dr)
            for j in range(M):
                cols = slice(j * F, (j + 1) * F)
                g1f[rows, cols] = ga[i % 2, i // 2, j, 0:dr, :]
                g2ft[rows, cols] = ga[i % 2, i // 2, j, dr : 2 * dr, :]
            return carry

        lax.fori_loop(0, N, place_g, 0)

        def turn_g(i, carry):
            here = pl.ds(multiple(i * LANES, LANES), LANES)
            for j in range(D // LANES):
                there = slice(j * LANES, (j + 1) * LANES)
                g1ft[there, here] = g1f[here, there].astype(F32).T.astype(BF16)
                g2f[there, here] = g2ft[here, there].astype(F32).T.astype(BF16)
            return carry

        lax.fori_loop(0, D // LANES, turn_g, 0)
        by_d = pl.ds(multiple(d * dr, dr), dr)
        by_m = pl.ds(multiple(m * F, F), F)

        def renewed(old, fresh):
            return stat_decay * old + (1.0 - stat_decay) * fresh

        l1_out[...] = renewed(l1_v[...], mm_t(g1f[by_d, :], g1f[by_m, :]))
        r1_out[...] = renewed(r1_v[...], mm_t(g1ft[by_d, :], g1ft[by_m, :]))
        l2_out[...] = renewed(l2_v[...], mm_t(g2f[by_d, :], g2f[by_m, :]))
        r2_out[...] = renewed(r2_v[...], mm_t(g2ft[by_d, :], g2ft[by_m, :]))

        def stepped(weight, left, grad, right):
            inner = jnp.dot(left[...], grad[...].astype(F32), precision=high, preferred_element_type=F32)
            return weight[...] - shampoo_rate * mm_t(inner, right[...], high)

        w1_out[...] = stepped(w1_v, p1_v, g1f, q1_v)
        w2_out[...] = stepped(w2_v, q2_v, g2ft, p2_v)

    with jax.named_scope("drain"):
        for kind, out in enumerate((lg_out,) if packed else (lg_out, ig_out)):
            remote(out, out, in_send.at[kind], out_recv.at[kind], z_peer(1)).wait_recv()
        for kind, buf in enumerate((lgb, igb)):
            part = buf.at[pl.ds(0, others), pl.ds(0, (mine, cap)[kind])]
            remote(part, part, out_send.at[kind], out_recv.at[0], z_peer(1)).wait_send()
        for kind, buf in enumerate((xb, cb)):
            part = buf.at[pl.ds(0, others), pl.ds(0, (mine, cap)[kind])]
            remote(part, part, in_send.at[kind], out_recv.at[0], z_peer(1)).wait_send()


def finish(n_out, D, tiles, sums_ref, order_ref, *refs):
    outs = refs[n_out : 2 * n_out]
    rms_out, flag_out, order_s, rms_s, flag_s, sems = refs[2 * n_out :]
    copies = [pltpu.make_async_copy(refs[i], outs[i], sems.at[i]) for i in range(n_out)]
    if tiles:
        order = pltpu.make_async_copy(order_ref, order_s, sems.at[n_out])
        order.start()
    for copy in copies[1 if tiles else 0 :]:
        copy.start()
    sums = sums_ref[...]
    ratio = jnp.sqrt(sums / (sums[2:3, :] * D))
    rms_s[0] = ratio[0, 0]
    rms_s[1] = ratio[1, 0]
    flag_s[0] = jnp.where(sums[3, 0] > 0.0, 1, 0)
    for k, (src, dst) in enumerate(((rms_s, rms_out), (flag_s, flag_out))):
        copies.append(pltpu.make_async_copy(src, dst, sems.at[n_out + 1 + k]))
        copies[-1].start()
    if tiles:
        order.wait()

        def step(g, carry):
            for j in range(8):
                t = g * 8 + j
                here = pl.ds(multiple(t * LANES, LANES), LANES)
                there = pl.ds(multiple(order_s[0, t] * LANES, LANES), LANES)
                pltpu.make_async_copy(refs[0].at[:, here], outs[0].at[:, there], sems.at[0]).start()
            return carry

        lax.fori_loop(0, tiles // 8, step, 0)
    for copy in copies:
        copy.wait()


def solution(mesh):
    N, M = mesh.shape["dp"], mesh.shape["mp"]
    Q = N // 2

    def on_device(*args):
        x, cot, mask, members, m1, m2, w1, w2, l1, r1, l2, r2, p1, q1, p2, q2 = args
        mask, w2, l2, r2 = mask.T, w2.T, l2.T, r2.T
        args = (x, cot, mask, members, m1, m2, w1, w2, l1, r1, l2, r2, p1, q1, p2, q2)
        F, R = x.shape
        D = F * M
        mine = R // M
        w = min(CHUNK, mine)
        C = mine // w
        kb = members.shape[1]
        dr = w1.shape[0]
        tr = -(-6 * kb // 8) * 8
        pr = 2 * dr + tr + 8
        groups = mine // LANES
        S = jax.ShapeDtypeStruct
        V = pltpu.VMEM
        dma = pltpu.SemaphoreType.DMA
        outs = [S(x.shape, BF16), S(x.shape, BF16), S((8, min(F, LANES)), F32), S((1, LANES), jnp.int32)]
        outs += [S(a.shape, F32) for a in (w1, w1, l1, r1, w2, w2, l2, r2, m1, m2, members)]
        anywhere = pl.BlockSpec(memory_space=pl.ANY)
        vmem = pl.BlockSpec(memory_space=pltpu.VMEM)

        def run(cap, number):
            packed = cap < mine
            KC = -(-cap // w)

            def only(shape, dtype):
                return V(shape if packed else (16, LANES), dtype)

            scratch = [V(a.shape, a.dtype) for a in (mask, members, m1, m2, w1, w2, l1, r1, l2, r2, p1, q1, p2, q2)]
            scratch += [only((F, R), BF16)] * 4
            scratch += [V((1, LANES), jnp.int32), pltpu.SMEM((1, LANES), jnp.int32)]
            scratch += [V((1, LANES), jnp.int32), pltpu.SMEM((1, LANES), jnp.int32)]
            scratch += [only((M, F, KC * w), BF16), only((w, mine), BF16), only((M, F, KC * w), BF16)]
            scratch += [V((D, mine), BF16), V((D, KC * w), BF16), V((D, mine), BF16), V((D, KC * w), BF16)]
            scratch += [V((2, Q, M, 2 * dr, F), BF16), V((2, Q, M, tr, F), F32)]
            scratch += [V((D, D), BF16)] * 4
            scratch += [V((6, D, LANES), F32), V((6, K, D), F32), V(mask.shape[::-1], jnp.int32)]
            scratch += [V((M * groups, LANES), jnp.int32)] + [V((M * groups, LANES), F32)] * 2
            scratch += [V((D, w), F32)] * 4
            scratch += [V((D, w), BF16)] * 4
            scratch += [only((D, w), F32), only((D, mine), BF16)]
            scratch += [V((D, D), F32)] * 2
            scratch += [V((6, D, LANES), F32), V((6, K, D), F32), V((16, LANES), F32)]
            scratch += [V((2, Q, M, pr, F), F32), V((Q, M, pr, F), F32)]
            scratch += [V((Q, M, 2 * dr, F), BF16), V((Q, M, 2 * dr, F), BF16), V((Q, M, pr - 2 * dr, F), F32)]
            scratch += [V((M - 1, 2 * dr, F), BF16), V((M - 1, pr - 2 * dr, F), F32), V((M - 1, 2 * dr, F), BF16)]
            scratch += [V((2, Q, M, 2 * dr, F), BF16)]
            scratch += [V((D, D), BF16)] * 4
            Z = M.bit_length() - 1
            scratch += [dma((11,)), dma((2,)), dma((C,)), dma((2,)), dma((M,))]
            scratch += [dma((2, Z)), dma((2, Z)), dma((2,)), dma((2,)), dma((2,)), dma((2,))]
            scratch += [dma, dma((Q,)), dma((2,)), dma((2,)), dma((2, Z)), dma((2, Z))]
            scratch += [dma((1, Z)), dma((1, Z)), dma, dma, dma, dma]
            res = pl.pallas_call(
                functools.partial(kernel, N, M, cap),
                out_shape=[V(a.shape, a.dtype) for a in outs],
                in_specs=[anywhere] * 16,
                out_specs=[vmem] * 15,
                scratch_shapes=scratch,
                compiler_params=pltpu.CompilerParams(
                    collective_id=number, has_side_effects=True, vmem_limit_bytes=46 << 20
                ),
                name="packed" if packed else "whole",
            )(*[pltpu.with_memory_space_constraint(a, pltpu.HBM) for a in args])
            kept = [*res[:2], *res[4:]]
            *done, rms, flag = pl.pallas_call(
                functools.partial(finish, len(kept), D, M * groups if packed else 0),
                out_shape=[S(a.shape, a.dtype) for a in kept] + [S((2,), F32), S((1,), jnp.int32)],
                in_specs=[vmem, anywhere] + [anywhere] * len(kept),
                out_specs=[anywhere] * (len(kept) + 2),
                scratch_shapes=[
                    pltpu.SMEM((1, LANES), jnp.int32),
                    pltpu.SMEM((2,), F32),
                    pltpu.SMEM((1,), jnp.int32),
                    dma((len(kept) + 3,)),
                ],
                compiler_params=pltpu.CompilerParams(vmem_limit_bytes=16 << 20),
                name="finish",
            )(res[2], res[3], *kept)
            return flag, (*done, rms)

        flag, fast = run(-(-mine * 11 // (16 * LANES)) * LANES, 0)
        done = lax.cond(flag[0] > 0, lambda: run(mine, 1)[1], lambda: fast)
        logits, igrad, g1, n1, l1, r1, g2, n2, l2, r2, m1, m2, new, rms = done
        return (logits, igrad, rms, g1, n1, l1, r1, g2.T, n2.T, l2.T, r2.T, m1, m2, new)

    placed = (
        P("mp", "dp"),
        P("mp", "dp"),
        P("dp", None),
        P(None, "dp", "mp"),
        P(None, "dp", "mp"),
        P(None, "dp", "mp"),
        P("dp", "mp"),
        P("mp", "dp"),
        P("dp", "mp"),
        P("dp", "mp"),
        P("mp", "dp"),
        P("mp", "dp"),
        P("dp", None),
        P("mp", None),
        P("mp", None),
        P("dp", None),
    )
    return jax.shard_map(
        on_device,
        mesh=mesh,
        in_specs=placed,
        out_specs=(
            P("mp", "dp"),
            P("mp", "dp"),
            P(),
            P("dp", "mp"),
            P("dp", "mp"),
            P("dp", "mp"),
            P("dp", "mp"),
            P("mp", "dp"),
            P("mp", "dp"),
            P("mp", "dp"),
            P("mp", "dp"),
            P(None, "dp", "mp"),
            P(None, "dp", "mp"),
            P(None, "dp", "mp"),
        ),
        check_vma=False,
    )
```

```python
import functools

import jax
import jax.numpy as jnp
from jax import lax
from jax.experimental import pallas as pl
from jax.experimental.pallas import tpu as pltpu
from jax.sharding import PartitionSpec as P

K = 32
STEP = 10
LANES = 128
CHUNK = 256
ROWS = 32
AHEAD = 2
FIRST = 4
LEAST = 8

beta_first = 0.9
beta_second = 0.999
adam_eps = 1e-08
adam_rate = 0.2
stat_decay = 0.95
shampoo_rate = 1.0
curve_a = 0.7978845608028654
curve_b = 0.044715

MESH = pl.DeviceIdType.MESH
F32 = jnp.float32
BF16 = jnp.bfloat16
over_lanes = (((1,), (1,)), ((), ()))


def flip(index, mask):
    bit = 1
    while bit <= mask:
        if mask & bit:
            index = index + bit - 2 * bit * ((index // bit) % 2)
        bit *= 2
    return index


def mm(a, b):
    return jnp.dot(a, b, preferred_element_type=F32)


def mm_t(a, b, precision=None):
    return lax.dot_general(a, b, over_lanes, precision=precision, preferred_element_type=F32)


def multiple(value, by):
    return pl.multiple_of(value, by)


def kernel(
    N,
    M,
    cap,
    x_hbm,
    cot_hbm,
    mask_hbm,
    mem_hbm,
    m1_hbm,
    m2_hbm,
    w1_hbm,
    w2_hbm,
    l1_hbm,
    r1_hbm,
    l2_hbm,
    r2_hbm,
    p1_hbm,
    q1_hbm,
    p2_hbm,
    q2_hbm,
    lg_out,
    ig_out,
    sums_out,
    order_out,
    g1_out,
    w1_out,
    l1_out,
    r1_out,
    g2_out,
    w2_out,
    l2_out,
    r2_out,
    m1_out,
    m2_out,
    mem_out,
    mask_v,
    mem_v,
    m1_v,
    m2_v,
    w1_v,
    w2_v,
    l1_v,
    r1_v,
    l2_v,
    r2_v,
    p1_v,
    q1_v,
    p2_v,
    q2_v,
    xv,
    xp,
    cv,
    cq,
    order_v,
    order_s,
    seats_v,
    seats_s,
    cp,
    st,
    igr,
    xb,
    cb,
    lgb,
    igb,
    wb,
    tb,
    w1,
    w1t,
    w2,
    w2t,
    tab,
    stage,
    mt,
    mp,
    mk,
    rk,
    hp,
    hid,
    dgm,
    prod,
    sc,
    hi,
    gp,
    gpre,
    cx,
    ig,
    g1,
    g2t,
    vec,
    vt,
    stat,
    gb,
    rcore,
    xs,
    rxg,
    rxv,
    rzg,
    rzv,
    zs,
    ga,
    g1f,
    g1ft,
    g2f,
    g2ft,
    local_sem,
    in_send,
    in_recv,
    out_send,
    out_recv,
    wz_send,
    wz_recv,
    wx_send,
    wx_recv,
    wc_send,
    wc_recv,
    gc_send,
    gc_recv,
    gx_send,
    gx_recv,
    gz_send,
    gz_recv,
    az_send,
    az_recv,
    ax_send,
    ax_recv,
    ac_send,
    ac_recv,
):
    F, R = x_hbm.shape
    D = F * M
    Q = N // 2
    mine = R // M
    w = min(CHUNK, mine)
    C = mine // w
    tiles = w // LANES
    packed = cap < mine
    KC = -(-cap // w)
    groups = mine // LANES
    kb = K // N
    dr = D // N
    tr = tb.shape[3]
    pr = gb.shape[3]
    blocks = D // ROWS
    high = lax.Precision.HIGHEST

    d, m = lax.axis_index("dp"), lax.axis_index("mp")
    c, q = d % 2, d // 2

    def z_peer(o):
        return (d, flip(m, o))

    def xy_peer(o):
        return (flip(q, o) * 2 + c, m)

    core_peer = (flip(d, 1), m)
    z_order = sorted(range(1, M), reverse=True)
    bits = [1 << k for k in range(M.bit_length() - 1)]
    xy_order = sorted(range(1, Q), reverse=True)

    def remote(src, dst, send, recv, peer):
        return pltpu.make_async_remote_copy(
            src_ref=src, dst_ref=dst, send_sem=send, recv_sem=recv, device_id=peer, device_id_type=MESH
        )

    pairs = (
        (mask_hbm, mask_v),
        (mem_hbm, mem_v),
        (w1_hbm, w1_v),
        (w2_hbm, w2_v),
        (m1_hbm, m1_v),
        (m2_hbm, m2_v),
        (l1_hbm, l1_v),
        (r1_hbm, r1_v),
        (l2_hbm, l2_v),
        (r2_hbm, r2_v),
        (p1_hbm, p1_v),
        (q1_hbm, q1_v),
        (p2_hbm, p2_v),
        (q2_hbm, q2_v),
    )
    if packed:
        pairs = (*pairs, (cot_hbm, cv), (x_hbm, xv))
    loads = [pltpu.make_async_copy(a, b, local_sem.at[i]) for i, (a, b) in enumerate(pairs)]
    for load in loads:
        load.start()

    per_mask = LANES // K
    total_tiles = M * groups

    I32 = jnp.int32

    def masks_to(ref):
        loads[0].wait()
        mt[...] = mask_v[...].T
        ref[...] = jnp.concatenate(
            [mt[pl.ds(j, total_tiles, stride=per_mask), :] for j in range(per_mask)], axis=1
        )

    def across(row):
        return jnp.broadcast_to(row, (LANES, LANES)).T

    def order_tiles():
        masks_to(mp)
        tall = jnp.concatenate([mp[...], jnp.zeros((LANES - total_tiles, LANES), I32)], axis=0)
        count = jnp.sum(tall.T, axis=0, keepdims=True)
        line_id = lax.broadcasted_iota(I32, (LANES, LANES), 0)
        lane_id = lax.broadcasted_iota(I32, (LANES, LANES), 1)
        mine_here, other = jnp.broadcast_to(count, (LANES, LANES)), across(count)
        before = (other > mine_here) | ((other == mine_here) & (line_id < lane_id))
        dealt = (line_id < total_tiles) & (line_id % groups != 0)
        rank = jnp.sum(jnp.where(before & dealt, 1, 0), axis=0, keepdims=True)
        turn, seat = rank // M, rank % M
        block = jnp.where(turn % 2 == 0, seat, M - 1 - seat)
        lane = lax.broadcasted_iota(I32, (1, LANES), 1)
        seats = jnp.where(lane % groups == 0, lane, block * groups + 1 + turn)
        seats = jnp.where(lane < total_tiles, seats, LANES)
        seats_v[...] = seats
        order_v[...] = jnp.sum(jnp.where(across(seats) == lane_id, line_id, 0), axis=0, keepdims=True)
        order_out[...] = order_v[...]
        to_scalars = pltpu.make_async_copy(order_v, order_s, local_sem.at[16])
        to_scalars.start()
        loads[15].wait()
        to_scalars.wait()
        deal(xv, xp, 0, 1)

    def deal(src, dst, start, end, order=None):
        order = order_s if order is None else order


        def step(i, carry):
            for p in range(M):
                for j in range(tiles):
                    t = p * groups + i * tiles + j
                    dst[:, pl.ds(multiple(t * LANES, LANES), LANES)] = src[
                        :, pl.ds(order[0, t] * LANES, LANES)
                    ]
            return carry

        lax.fori_loop(start, end, step, 0)

    with jax.named_scope("barrier"):
        entry = pltpu.get_barrier_semaphore()
        peers = [z_peer(o) for o in z_order] + [xy_peer(o) for o in xy_order] + [core_peer]
        for peer in peers:
            pl.semaphore_signal(entry, inc=1, device_id=peer, device_id_type=MESH)
        for load in loads[1:4]:
            load.wait()
        wb[c, q, m, 0:dr, :] = w1_v[...].astype(BF16)
        wb[c, q, m, dr : 2 * dr, :] = w2_v[...].astype(BF16)
        for t in range(6):
            tb[c, q, m, t * kb : (t + 1) * kb, :] = mem_v[t]
        pl.semaphore_wait(entry, len(peers))

    kinds_in = (xb, cb)

    def at_width(i, act):
        if not packed:
            act(w)
        elif isinstance(i, int):
            if i < KC:
                act(min(w, cap - i * w))
        elif cap % w == 0:
            pl.when(i < KC)(lambda: act(w))
        else:
            pl.when(i < KC - 1)(lambda: act(w))
            pl.when(i == KC - 1)(lambda: act(cap % w))

    def send_tile(j, src):
        here = pl.ds(multiple(m * F, F), F)
        there = xb.at[here, j * LANES : (j + 1) * LANES]

        def tile(to):
            return src.at[:, pl.ds(multiple(to * mine + j * LANES, LANES), LANES)]

        for o in z_order:
            to = flip(m, o)
            remote(tile(to), there, in_send.at[0], in_recv.at[0], (d, to)).start()
        pltpu.make_async_copy(tile(m), there, in_recv.at[0]).start()

    def send_in(i, kinds=(0, 1)):
        here = pl.ds(multiple(m * F, F), F)

        def source(kind, to, width):
            if kind and packed:
                return cp.at[to, :, pl.ds(multiple(i * w, w), width)]
            hbm = xp if packed else (x_hbm, cot_hbm)[kind]
            return hbm.at[:, pl.ds(multiple(to * mine + i * w, w), width)]

        def start(kind, width):
            there = kinds_in[kind].at[here, pl.ds(multiple(i * w, w), width)]
            for o in z_order:
                to = flip(m, o)
                remote(source(kind, to, width), there, in_send.at[kind], in_recv.at[i], (d, to)).start()
            pltpu.make_async_copy(source(kind, m, width), there, in_recv.at[i]).start()

        for kind in kinds:
            if kind:
                at_width(i, functools.partial(start, 1))
            else:
                start(0, w)

    others = (M - 1) * F

    def wait_in(i):
        def arrive(width):
            part = xb.at[:, pl.ds(0, w + width)]
            remote(part, part, in_send.at[0], in_recv.at[i], z_peer(1)).wait_recv()

        at_width(i, arrive)
        if packed:
            pl.when(i >= KC)(lambda: arrive(0))

    def width_of(kind, i):
        return min(w, cap - i * w) if kind and packed else w

    def send_out(kind, i):
        col = pl.ds(multiple(i * w, w), width_of(kind, i))
        if kind and packed:
            there = igr.at[m, :, col]
        else:
            there = (lg_out, ig_out)[kind].at[:, pl.ds(multiple(m * mine + i * w, w), w)]
        buf = (lgb, igb)[kind]
        for o in z_order[::-1]:
            to = flip(m, o)
            recv = out_recv.at[kind, o] if kind and packed else out_recv.at[kind, 0]
            remote(buf.at[pl.ds(multiple(to * F, F), F), col], there, out_send.at[kind], recv, (d, to)).start()
        if not (kind and packed):
            pltpu.make_async_copy(buf.at[pl.ds(multiple(m * F, F), F), col], there, out_recv.at[kind, 0]).start()

    line = lax.broadcasted_iota(jnp.int32, (w, LANES), 0).astype(F32)

    def matches(p, k, i):
        base = (k * w) * jnp.float32(1) if isinstance(k, int) else (k * w).astype(F32)
        parts = []
        for j in range(tiles):
            row = rk[pl.ds(p * groups + i * tiles + j, 1), :] - base
            parts.append(jnp.where(line == row, 1.0, 0.0).astype(BF16))
        return jnp.concatenate(parts, axis=1)

    spread_by = K // LEAST

    def pack_block(k, p):
        def step(i, acc):
            cols = pl.ds(multiple(p * mine + i * w, w), w)
            return acc + mm_t(cq[:, cols], matches(p, k, i))

        acc = lax.fori_loop(k, min(C, spread_by * k + spread_by), step, jnp.zeros((F, w), F32))
        cp[p, :, k * w : (k + 1) * w] = acc.astype(BF16)

    def shrink(k):
        with jax.named_scope("shrink"):
            end = min(C, spread_by * k + spread_by)

            def step(i, carry):
                st[:, pl.ds(multiple(i * w, w), w)] = matches(m, k, i)
                return carry

            lax.fori_loop(k, end, step, 0)
            part = slice(k * w, end * w)
            igb[:, k * w : (k + 1) * w] = mm_t(ig[:, part], st[:, part]).astype(BF16)

    def pack_chunk(k):
        with jax.named_scope("pack_cot"):

            def step(p, carry):
                pack_block(k, p)
                return carry

            lax.fori_loop(0, M, step, 0)

    def unpack_block(p):
        with jax.named_scope("unpack"):

            def chunk(i, carry):
                def step(k, acc):
                    return acc + mm(igr[p, :, pl.ds(multiple(k * w, w), w)], matches(p, k, i))

                acc = lax.fori_loop(i // spread_by, jnp.minimum(i, KC - 1) + 1, step, jnp.zeros((F, w), F32))
                xv[:, pl.ds(multiple(p * mine + i * w, w), w)] = acc.astype(BF16)
                return carry

            lax.fori_loop(0, C, chunk, 0)

    def unpack_from(o):
        part = igr.at[0, :, pl.ds(0, cap)]
        remote(part, part, in_send.at[0], out_recv.at[1, o], z_peer(o)).wait_recv()
        unpack_block(flip(m, o))

    if not packed:
        order_out[...] = jnp.zeros_like(order_out)
    class SpreadZ:
        def __init__(self, bit, bufs, send, recv):
            self.go, self.come = [], []
            offsets = list(range(0, M, 2 * bit))
            for k, buf in enumerate(bufs):
                sems = (send.at[k, bits.index(bit)], recv.at[k, bits.index(bit)], z_peer(bit))
                for h in offsets:
                    slot = buf.at[c, q, flip(m, h)]
                    self.go.append(remote(slot, slot, *sems))
                both = buf.at[c, q, pl.ds(0, len(offsets))]
                self.come.append(remote(both, both, *sems))

        def start(self):
            for copy in self.go:
                copy.start()

        def wait(self):
            for copy in self.come:
                copy.wait()

    bufs = (wb, tb)
    first = SpreadZ(bits[-1], bufs, wz_send, wz_recv)
    first.start()
    if packed:
        send_tile(0, x_hbm)
        order_tiles()
        for j in range(1, tiles):
            send_tile(j, xp)
    else:
        send_in(0)
    if not packed:
        masks_to(mp)
        mk[...] = mp[...].astype(F32)
    else:
        deal(xv, xp, 1, C)
        to_seats = pltpu.make_async_copy(seats_v, seats_s, local_sem.at[17])
        to_seats.start()

        def deal_masks(t, carry):
            for j in range(8):
                mk[pl.ds(t * 8 + j, 1), :] = mp[pl.ds(order_s[0, t * 8 + j], 1), :].astype(F32)
            return carry

        lax.fori_loop(0, total_tiles // 8, deal_masks, 0)
        to_seats.wait()
        flags = mk[...]
        rows, cols = M * groups, LANES
        lower = lax.broadcasted_iota(jnp.int32, (cols, cols), 0) < lax.broadcasted_iota(jnp.int32, (cols, cols), 1)
        inside = mm(flags.astype(BF16), jnp.where(lower, 1.0, 0.0).astype(BF16))
        sums = jnp.broadcast_to(jnp.sum(flags, axis=1, keepdims=True), (rows, cols)).astype(BF16)
        one = lax.broadcasted_iota(jnp.int32, (rows, rows), 0)
        two = lax.broadcasted_iota(jnp.int32, (rows, rows), 1)
        ahead = (two < one) & (two >= one - one % groups)
        place_in = inside + mm(jnp.where(ahead, 1.0, 0.0).astype(BF16), sums)
        rk[...] = jnp.where(flags > 0.0, place_in, -1.0)
    def clear(i, carry):
        rows = pl.ds(multiple(i * ROWS, ROWS), ROWS)
        g1[rows, :] = jnp.zeros((ROWS, D), F32)
        g2t[rows, :] = jnp.zeros((ROWS, D), F32)
        for t in range(6):
            vec[t, rows, :] = jnp.zeros((ROWS, LANES), F32)
        return carry

    lax.fori_loop(0, blocks, clear, 0)
    stat[...] = jnp.zeros_like(stat)

    ahead_of = min(FIRST, C)
    if packed:
        loads[14].wait()
        deal(cv, cq, 0, C)
        if cap % w:
            cb[:, cap : KC * w] = jnp.zeros((D, KC * w - cap), BF16)
            for p in range(M):
                igr[p, :, cap : KC * w] = jnp.zeros((F, KC * w - cap), BF16)
        pack_chunk(0)

    def step_in(k):
        if packed:
            if k < KC:
                send_in(k, (1,))
            if k + 1 < ahead_of:
                send_in(k + 1, (0,))
            if k + 1 < KC:
                pack_chunk(k + 1)
        elif k + 1 < ahead_of:
            send_in(k + 1)

    with jax.named_scope("weights_z"):
        for bit in bits[::-1]:
            if bit != bits[-1]:
                first = SpreadZ(bit, bufs, wz_send, wz_recv)
                first.start()
            if bit == bits[0]:
                step_in(0)
            first.wait()
    with jax.named_scope("weights_xy"):
        for o in xy_order:
            for k, buf in enumerate(bufs):
                remote(buf.at[c, q], buf.at[c, q], wx_send.at[k], wx_recv.at[k], xy_peer(o)).start()
        step_in(1)
        step_in(2)
        for k, buf in enumerate(bufs):
            rest = buf.at[c, pl.ds(0, Q - 1)]
            remote(rest, rest, wx_send.at[k], wx_recv.at[k], xy_peer(1)).wait()
    with jax.named_scope("weights_core"):
        for k, buf in enumerate(bufs):
            remote(buf.at[c], buf.at[c], wc_send.at[k], wc_recv.at[k], core_peer).start()
        for k in range(3, max(ahead_of, KC if packed else 0)):
            if k < ahead_of:
                step_in(k)
            elif k + 1 < KC:
                pack_chunk(k + 1)
        for k, buf in enumerate(bufs):
            remote(buf.at[c], buf.at[1 - c], wc_send.at[k], wc_recv.at[k], core_peer).wait()

    with jax.named_scope("weights_spread"):

        def place(i, carry):
            rows = pl.ds(multiple(i * dr, dr), dr)
            for j in range(M):
                cols = slice(j * F, (j + 1) * F)
                w1[rows, cols] = wb[i % 2, i // 2, j, 0:dr, :]
                w2t[rows, cols] = wb[i % 2, i // 2, j, dr : 2 * dr, :]
            return carry

        lax.fori_loop(0, N, place, 0)

        def turn(i, carry):
            here = pl.ds(multiple(i * LANES, LANES), LANES)
            for j in range(D // LANES):
                there = slice(j * LANES, (j + 1) * LANES)
                w1t[there, here] = w1[here, there].astype(F32).T.astype(BF16)
                w2[there, here] = w2t[here, there].astype(F32).T.astype(BF16)
            return carry

        lax.fori_loop(0, D // LANES, turn, 0)
        for t in range(6):
            for i in range(N):
                for j in range(M):
                    stage[t, i * kb : (i + 1) * kb, j * F : (j + 1) * F] = tb[
                        i % 2, i // 2, j, t * kb : (t + 1) * kb, :
                    ]

        def table(t, carry):
            for j in range(D // LANES):
                cols = slice(j * LANES, (j + 1) * LANES)
                piece = stage[t, :, cols]
                tab[t, cols, :] = jnp.concatenate([piece] * per_mask, axis=0).T
            return carry

        lax.fori_loop(0, 6, table, 0)

    def eight(value):
        return value.reshape(ROWS // 8, 8, LANES).sum(0)

    if packed:
        early = [(C - 3, [(0, 0)]), (C - 2, [(0, 1)]), (C - 1, [(0, 2)])]
    else:
        early = [(C - 2, [(0, 0), (1, 0)]), (C - 1, [(0, 1), (1, 1)])]

    def work(i, carry):
        col = multiple(i * w, w)
        with jax.named_scope("wait_in"):
            wait_in(i)

        @pl.when((i + AHEAD >= FIRST) & (i + AHEAD < C - 1))
        def _():
            send_in(i + AHEAD)

        if C > FIRST:

            @pl.when(i + AHEAD == C - 2)
            def _():
                send_in(C - 1)

        for late, parts in early:
            for kind, k in parts:
                pl.when(i == late)(functools.partial(send_out, kind, k))

        masks = [mk[pl.ds(m * groups + i * tiles + j, 1), :] for j in range(tiles)]

        def place_of(r):
            return pl.ds(multiple(r * ROWS, ROWS), ROWS)

        def lanes_of(j):
            return pl.ds(multiple(col + j * LANES, LANES), LANES)

        def scale_rows(r, sums):
            rows = place_of(r)
            row_in = tab[0, rows, :]
            new = []
            for j in range(tiles):
                x = xb[rows, lanes_of(j)].astype(F32)
                sc[rows, j * LANES : (j + 1) * LANES] = (x * row_in).astype(BF16)
                new.append(sums[j] + eight(x * x))
            return tuple(new)

        zero = tuple(jnp.zeros((8, LANES), F32) for _ in range(tiles))
        with jax.named_scope("scale"):
            x_sums = lax.fori_loop(0, blocks, scale_rows, zero)
        with jax.named_scope("mm_one"):
            hp[...] = mm(w1t[...], sc[...])

        def curve_rows(r, carry):
            rows = place_of(r)
            gain, bias, row_mid = tab[1, rows, :], tab[2, rows, :], tab[3, rows, :]
            for j in range(tiles):
                cols = slice(j * LANES, (j + 1) * LANES)
                s = hp[rows, cols] * gain + bias
                s2 = s * s
                th = jnp.tanh(curve_a * (s + curve_b * (s2 * s)))
                cdf = 0.5 * (1.0 + th)
                h = s * cdf
                slope = cdf + (0.5 * s) * (1.0 - th * th) * (curve_a + (3.0 * curve_a * curve_b) * s2)
                hid[rows, cols] = h
                dgm[rows, cols] = slope * row_mid
                hi[rows, cols] = (h * row_mid).astype(BF16)
            return carry

        with jax.named_scope("curve"):
            lax.fori_loop(0, blocks, curve_rows, 0)
        with jax.named_scope("mm_two"):
            prod[...] = mm(w2t[...], hi[...])
        low, high_k = i // spread_by, jnp.minimum(i, KC - 1)
        if packed:
            with jax.named_scope("expand"):

                def grow(k, carry):
                    cx[...] += mm(cb[:, pl.ds(multiple(k * w, w), w)], matches(m, k, i))
                    return carry

                cx[...] = jnp.zeros_like(cx)
                lax.fori_loop(low, high_k + 1, grow, 0)

        def grad_of(rows, j):
            if packed:
                return cx[rows, j * LANES : (j + 1) * LANES]
            return cb[rows, lanes_of(j)].astype(F32) * masks[j]


        def out_rows(r, sums):
            rows = place_of(r)
            gain, bias = tab[4, rows, :], tab[5, rows, :]
            v4, v5 = vec[4, rows, :], vec[5, rows, :]
            new = []
            for j in range(tiles):
                cols = slice(j * LANES, (j + 1) * LANES)
                x = xb[rows, lanes_of(j)].astype(F32)
                projected = prod[rows, cols]
                branch = projected * gain + bias
                lgb[rows, lanes_of(j)] = (x + branch).astype(BF16)
                new.append(sums[j] + eight(branch * branch))
                go = grad_of(rows, j)
                v5 = v5 + go
                v4 = v4 + go * projected
                gp[rows, cols] = (go * gain).astype(BF16)
            vec[4, rows, :] = v4
            vec[5, rows, :] = v5
            return tuple(new)

        with jax.named_scope("out"):
            b_sums = lax.fori_loop(0, blocks, out_rows, zero)
        for j in range(tiles):
            stat[0:8, :] += x_sums[j] * masks[j]
            stat[8:16, :] += b_sums[j] * masks[j]

        with jax.named_scope("mm_three"):
            half = D // 2
            for k in range(2):
                part = slice(k * half, (k + 1) * half)
                g2t[part, :] += mm_t(gp[part, :], hi[...])
            prod[...] = mm(w2[...], gp[...])

        def back_rows(r, carry):
            rows = place_of(r)
            gain = tab[1, rows, :]
            v1, v2, v3 = vec[1, rows, :], vec[2, rows, :], vec[3, rows, :]
            for j in range(tiles):
                cols = slice(j * LANES, (j + 1) * LANES)
                gh = prod[rows, cols]
                v3 = v3 + gh * hid[rows, cols]
                gs = gh * dgm[rows, cols]
                v2 = v2 + gs
                v1 = v1 + gs * hp[rows, cols]
                gpre[rows, cols] = (gs * gain).astype(BF16)
            vec[1, rows, :] = v1
            vec[2, rows, :] = v2
            vec[3, rows, :] = v3
            return carry

        with jax.named_scope("back"):
            lax.fori_loop(0, blocks, back_rows, 0)
        with jax.named_scope("mm_four"):
            for k in range(2):
                part = slice(k * half, (k + 1) * half)
                g1[part, :] += mm_t(sc[part, :], gpre[...])
            prod[...] = mm(w1[...], gpre[...])

        def in_rows(r, carry):
            rows = place_of(r)
            row_in = tab[0, rows, :]
            v0 = vec[0, rows, :]
            for j in range(tiles):
                cols = slice(j * LANES, (j + 1) * LANES)
                gs = prod[rows, cols]
                v0 = v0 + gs * xb[rows, lanes_of(j)].astype(F32)
                go = grad_of(rows, j)
                done = (gs * row_in + go).astype(BF16)
                if packed:
                    ig[rows, lanes_of(j)] = done
                else:
                    igb[rows, lanes_of(j)] = done
            vec[0, rows, :] = v0
            return carry

        with jax.named_scope("in"):
            lax.fori_loop(0, blocks, in_rows, 0)
        if packed:
            xv[:, pl.ds(multiple(m * mine + col, w), w)] = ig[pl.ds(multiple(m * F, F), F), pl.ds(col, w)]
        return carry

    lax.fori_loop(0, C, work, 0)

    items = [item for _, parts in early for item in parts]
    already = len(items)
    if packed:
        items += [(1, k) for k in range(KC)] + [(0, i) for i in range(3, C)]
    else:
        items += [(kind, i) for i in range(2, C) for kind in range(2)]
    state = {"sent": already}

    def pump(count):
        with jax.named_scope("pump"):
            for kind, k in items[state["sent"] : state["sent"] + count]:
                if kind and packed:
                    shrink(k)
                send_out(kind, k)
            state["sent"] += count

    with jax.named_scope("pack"):

        def pack_g(i, carry):
            rows = pl.ds(multiple(i * dr, dr), dr)
            for j in range(M):
                cols = slice(j * F, (j + 1) * F)
                gb[i % 2, i // 2, j, 0:dr, :] = g1[rows, cols]
                gb[i % 2, i // 2, j, dr : 2 * dr, :] = g2t[rows, cols]
            return carry

        lax.fori_loop(0, N, pack_g, 0)

        def fold(t, carry):
            for j in range(D // LANES):
                cols = slice(j * LANES, (j + 1) * LANES)
                turned = vec[t, cols, :].T
                vt[t, :, cols] = sum(turned[k * K : (k + 1) * K, :] for k in range(per_mask))
            return carry

        lax.fori_loop(0, 6, fold, 0)
        for t in range(6):
            for i in range(N):
                for j in range(M):
                    row = 2 * dr + t * kb
                    gb[i % 2, i // 2, j, row : row + kb, :] = vt[t, i * kb : (i + 1) * kb, j * F : (j + 1) * F]
        own = mk[pl.ds(multiple(m * groups, groups), groups), :]
        totals = [stat[0:8, :], stat[8:16, :], own]
        rows8 = [jnp.sum(v, keepdims=True).reshape(1, 1) for v in totals]
        rows8.append(jnp.where(rows8[2] > cap, 1.0, 0.0))
        row_id = lax.broadcasted_iota(jnp.int32, (8, F), 0)
        lines = sum(jnp.where(row_id == k, v, 0.0) for k, v in enumerate(rows8))

        def put(i, carry):
            for j in range(M):
                gb[i % 2, i // 2, j, 2 * dr + tr : pr, :] = lines
            return carry

        lax.fori_loop(0, N, put, 0)

    with jax.named_scope("sum_core"):
        for o in xy_order + [0]:
            k = flip(q, o)
            remote(gb.at[1 - c, k], rcore.at[k], gc_send.at[o], gc_recv.at[o], core_peer).start()

        def add_core(k):
            def step(j, carry):
                gb[c, k, j] += rcore[k, j]
                return carry

            lax.fori_loop(0, M, step, 0)

        def over_xy(o):
            k = flip(q, o)
            sems = [(gx_send.at[n], gx_recv.at[n], xy_peer(o)) for n in range(2)]
            tail = gb.at[c, k, :, pl.ds(2 * dr, pr - 2 * dr), :]
            return remote(xs.at[o], rxg.at[o], *sems[0]), remote(tail, rxv.at[o], *sems[1])

        for o in xy_order + [0]:
            k = flip(q, o)
            remote(gb.at[1 - c, k], rcore.at[k], gc_send.at[o], gc_recv.at[o], core_peer).wait()
            add_core(k)
            if o:

                def round_piece(j, carry):
                    xs[o, j] = gb[c, k, j, 0 : 2 * dr, :].astype(BF16)
                    return carry

                lax.fori_loop(0, M, round_piece, 0)
                for copy in over_xy(o):
                    copy.start()
    pump(2)
    with jax.named_scope("sum_xy"):
        for n, buf in enumerate((rxg, rxv)):
            rest = buf.at[pl.ds(1, Q - 1)]
            remote(rest, rest, gx_send.at[n], gx_recv.at[n], xy_peer(1)).wait()
        for o in xy_order:

            def step(j, carry):
                gb[c, q, j, 0 : 2 * dr, :] += rxg[o, j].astype(F32)
                gb[c, q, j, 2 * dr : pr, :] += rxv[o, j]
                return carry

            lax.fori_loop(0, M, step, 0)
    with jax.named_scope("sum_z"):
        slot = 0
        for stage, bit in enumerate(bits):
            moves = []
            at = slot
            for h in range(0, M, 2 * bit):
                away = flip(m, h + bit)
                zs[slot] = gb[c, q, away, 0 : 2 * dr, :].astype(BF16)
                sems = [(gz_send.at[k, stage], gz_recv.at[k, stage], z_peer(bit)) for k in range(2)]
                tail = gb.at[c, q, away, pl.ds(2 * dr, pr - 2 * dr), :]
                moves.append((slot, h, remote(zs.at[slot], rzg.at[slot], *sems[0]), remote(tail, rzv.at[slot], *sems[1])))
                slot += 1
            for _, _, one, two in moves:
                one.start()
                two.start()
            pump(1)
            for k, buf in enumerate((rzg, rzv)):
                rest = buf.at[pl.ds(at, len(moves))]
                remote(rest, rest, gz_send.at[k, stage], gz_recv.at[k, stage], z_peer(bit)).wait()
            for k, h, _, _ in moves:
                keep = flip(m, h)
                gb[c, q, keep, 0 : 2 * dr, :] += rzg[k].astype(F32)
                gb[c, q, keep, 2 * dr : pr, :] += rzv[k]
            pump(1)

    total = gb[c, q, m]
    ga[c, q, m] = total[0 : 2 * dr, :].astype(BF16)
    with jax.named_scope("spread_z"):
        first = SpreadZ(bits[-1], (ga,), az_send, az_recv)
        first.start()
        pump(2)
        for load in loads[4:14]:
            load.wait()
        g1_out[...] = total[0:dr, :]
        g2_out[...] = total[dr : 2 * dr, :]
        corr_one = 1.0 - beta_first**STEP
        corr_two = 1.0 - beta_second**STEP
        for t in range(6):
            row = 2 * dr + t * kb
            grad = total[row : row + kb, :]
            one = beta_first * m1_v[t] + (1.0 - beta_first) * grad
            two = beta_second * m2_v[t] + (1.0 - beta_second) * grad * grad
            m1_out[t] = one
            m2_out[t] = two
            mem_out[t] = mem_v[t] - adam_rate * (one / corr_one) / (jnp.sqrt(two / corr_two) + adam_eps)
        sums_out[...] = total[2 * dr + tr : pr, 0:LANES if F >= LANES else F]
        for bit in bits[::-1]:
            if bit != bits[-1]:
                first = SpreadZ(bit, (ga,), az_send, az_recv)
                first.start()
            if bit == bits[0]:
                pump(len(items))
            if packed and bit == bits[0]:
                for o in z_order[:-1]:
                    unpack_from(o)
            first.wait()
    with jax.named_scope("spread_xy"):
        for o in xy_order:
            remote(ga.at[c, q], ga.at[c, q], ax_send, ax_recv, xy_peer(o)).start()
        if packed:
            for o in z_order[-1:]:
                unpack_from(o)
            with jax.named_scope("settle"):
                deal(xv, ig_out, 0, C, seats_s)
        rest = ga.at[c, pl.ds(0, Q - 1)]
        remote(rest, rest, ax_send, ax_recv, xy_peer(1)).wait()
    with jax.named_scope("spread_core"):
        remote(ga.at[c], ga.at[c], ac_send, ac_recv, core_peer).start()
        remote(ga.at[c], ga.at[1 - c], ac_send, ac_recv, core_peer).wait()
    with jax.named_scope("shampoo"):

        def place_g(i, carry):
            rows = pl.ds(multiple(i * dr, dr), dr)
            for j in range(M):
                cols = slice(j * F, (j + 1) * F)
                g1f[rows, cols] = ga[i % 2, i // 2, j, 0:dr, :]
                g2ft[rows, cols] = ga[i % 2, i // 2, j, dr : 2 * dr, :]
            return carry

        lax.fori_loop(0, N, place_g, 0)

        def turn_g(i, carry):
            here = pl.ds(multiple(i * LANES, LANES), LANES)
            for j in range(D // LANES):
                there = slice(j * LANES, (j + 1) * LANES)
                g1ft[there, here] = g1f[here, there].astype(F32).T.astype(BF16)
                g2f[there, here] = g2ft[here, there].astype(F32).T.astype(BF16)
            return carry

        lax.fori_loop(0, D // LANES, turn_g, 0)
        by_d = pl.ds(multiple(d * dr, dr), dr)
        by_m = pl.ds(multiple(m * F, F), F)

        def renewed(old, fresh):
            return stat_decay * old + (1.0 - stat_decay) * fresh

        l1_out[...] = renewed(l1_v[...], mm_t(g1f[by_d, :], g1f[by_m, :]))
        r1_out[...] = renewed(r1_v[...], mm_t(g1ft[by_d, :], g1ft[by_m, :]))
        l2_out[...] = renewed(l2_v[...], mm_t(g2f[by_d, :], g2f[by_m, :]))
        r2_out[...] = renewed(r2_v[...], mm_t(g2ft[by_d, :], g2ft[by_m, :]))

        def stepped(weight, left, grad, right):
            inner = jnp.dot(left[...], grad[...].astype(F32), precision=high, preferred_element_type=F32)
            return weight[...] - shampoo_rate * mm_t(inner, right[...], high)

        w1_out[...] = stepped(w1_v, p1_v, g1f, q1_v)
        w2_out[...] = stepped(w2_v, q2_v, g2ft, p2_v)

    with jax.named_scope("drain"):
        for kind, out in enumerate((lg_out,) if packed else (lg_out, ig_out)):
            remote(out, out, in_send.at[kind], out_recv.at[kind, 0], z_peer(1)).wait_recv()
        for kind, buf in enumerate((lgb, igb)):
            part = buf.at[pl.ds(0, others), pl.ds(0, (mine, cap)[kind])]
            remote(part, part, out_send.at[kind], out_recv.at[0, 0], z_peer(1)).wait_send()
        for kind, buf in enumerate((xb, cb)):
            part = buf.at[pl.ds(0, others), pl.ds(0, (mine, cap)[kind])]
            remote(part, part, in_send.at[kind], out_recv.at[0, 0], z_peer(1)).wait_send()


def finish(n_out, D, tiles, sums_ref, order_ref, *refs):
    outs = refs[n_out : 2 * n_out]
    rms_out, flag_out, order_s, rms_s, flag_s, sems = refs[2 * n_out :]
    copies = [pltpu.make_async_copy(refs[i], outs[i], sems.at[i]) for i in range(n_out)]
    if tiles:
        order = pltpu.make_async_copy(order_ref, order_s, sems.at[n_out])
        order.start()
    for copy in copies[1 if tiles else 0 :]:
        copy.start()
    sums = sums_ref[...]
    ratio = jnp.sqrt(sums / (sums[2:3, :] * D))
    rms_s[0] = ratio[0, 0]
    rms_s[1] = ratio[1, 0]
    flag_s[0] = jnp.where(sums[3, 0] > 0.0, 1, 0)
    for k, (src, dst) in enumerate(((rms_s, rms_out), (flag_s, flag_out))):
        copies.append(pltpu.make_async_copy(src, dst, sems.at[n_out + 1 + k]))
        copies[-1].start()
    if tiles:
        order.wait()

        def step(g, carry):
            for j in range(8):
                t = g * 8 + j
                here = pl.ds(multiple(t * LANES, LANES), LANES)
                there = pl.ds(multiple(order_s[0, t] * LANES, LANES), LANES)
                pltpu.make_async_copy(refs[0].at[:, here], outs[0].at[:, there], sems.at[0]).start()
            return carry

        lax.fori_loop(0, tiles // 8, step, 0)
    for copy in copies:
        copy.wait()


def solution(mesh):
    N, M = mesh.shape["dp"], mesh.shape["mp"]
    Q = N // 2

    def on_device(*args):
        x, cot, mask, members, m1, m2, w1, w2, l1, r1, l2, r2, p1, q1, p2, q2 = args
        mask, w2, l2, r2 = mask.T, w2.T, l2.T, r2.T
        args = (x, cot, mask, members, m1, m2, w1, w2, l1, r1, l2, r2, p1, q1, p2, q2)
        F, R = x.shape
        D = F * M
        mine = R // M
        w = min(CHUNK, mine)
        C = mine // w
        kb = members.shape[1]
        dr = w1.shape[0]
        tr = -(-6 * kb // 8) * 8
        pr = 2 * dr + tr + 8
        groups = mine // LANES
        S = jax.ShapeDtypeStruct
        V = pltpu.VMEM
        dma = pltpu.SemaphoreType.DMA
        outs = [S(x.shape, BF16), S(x.shape, BF16), S((8, min(F, LANES)), F32), S((1, LANES), jnp.int32)]
        outs += [S(a.shape, F32) for a in (w1, w1, l1, r1, w2, w2, l2, r2, m1, m2, members)]
        anywhere = pl.BlockSpec(memory_space=pl.ANY)
        vmem = pl.BlockSpec(memory_space=pltpu.VMEM)

        def run(cap, number):
            packed = cap < mine
            KC = -(-cap // w)

            def only(shape, dtype):
                return V(shape if packed else (16, LANES), dtype)

            scratch = [V(a.shape, a.dtype) for a in (mask, members, m1, m2, w1, w2, l1, r1, l2, r2, p1, q1, p2, q2)]
            scratch += [only((F, R), BF16)] * 4
            scratch += [V((1, LANES), jnp.int32), pltpu.SMEM((1, LANES), jnp.int32)]
            scratch += [V((1, LANES), jnp.int32), pltpu.SMEM((1, LANES), jnp.int32)]
            scratch += [only((M, F, KC * w), BF16), only((w, mine), BF16), only((M, F, KC * w), BF16)]
            scratch += [V((D, mine), BF16), V((D, KC * w), BF16), V((D, mine), BF16), V((D, KC * w), BF16)]
            scratch += [V((2, Q, M, 2 * dr, F), BF16), V((2, Q, M, tr, F), F32)]
            scratch += [V((D, D), BF16)] * 4
            scratch += [V((6, D, LANES), F32), V((6, K, D), F32), V(mask.shape[::-1], jnp.int32)]
            scratch += [V((M * groups, LANES), jnp.int32)] + [V((M * groups, LANES), F32)] * 2
            scratch += [V((D, w), F32)] * 4
            scratch += [V((D, w), BF16)] * 4
            scratch += [only((D, w), F32), only((D, mine), BF16)]
            scratch += [V((D, D), F32)] * 2
            scratch += [V((6, D, LANES), F32), V((6, K, D), F32), V((16, LANES), F32)]
            scratch += [V((2, Q, M, pr, F), F32), V((Q, M, pr, F), F32)]
            scratch += [V((Q, M, 2 * dr, F), BF16), V((Q, M, 2 * dr, F), BF16), V((Q, M, pr - 2 * dr, F), F32)]
            scratch += [V((M - 1, 2 * dr, F), BF16), V((M - 1, pr - 2 * dr, F), F32), V((M - 1, 2 * dr, F), BF16)]
            scratch += [V((2, Q, M, 2 * dr, F), BF16)]
            scratch += [V((D, D), BF16)] * 4
            Z = M.bit_length() - 1
            scratch += [dma((18,)), dma((2,)), dma((C,)), dma((2,)), dma((2, M))]
            scratch += [dma((2, Z)), dma((2, Z)), dma((2,)), dma((2,)), dma((2,)), dma((2,))]
            scratch += [dma((Q,)), dma((Q,)), dma((2,)), dma((2,)), dma((2, Z)), dma((2, Z))]
            scratch += [dma((1, Z)), dma((1, Z)), dma, dma, dma, dma]
            res = pl.pallas_call(
                functools.partial(kernel, N, M, cap),
                out_shape=[V(a.shape, a.dtype) for a in outs],
                in_specs=[anywhere] * 16,
                out_specs=[vmem] * 15,
                scratch_shapes=scratch,
                compiler_params=pltpu.CompilerParams(
                    collective_id=number, has_side_effects=True, vmem_limit_bytes=46 << 20
                ),
                name="packed" if packed else "whole",
            )(*[pltpu.with_memory_space_constraint(a, pltpu.HBM) for a in args])
            kept = [*res[:2], *res[4:]]
            *done, rms, flag = pl.pallas_call(
                functools.partial(finish, len(kept), D, M * groups if packed else 0),
                out_shape=[S(a.shape, a.dtype) for a in kept] + [S((2,), F32), S((1,), jnp.int32)],
                in_specs=[vmem, anywhere] + [anywhere] * len(kept),
                out_specs=[anywhere] * (len(kept) + 2),
                scratch_shapes=[
                    pltpu.SMEM((1, LANES), jnp.int32),
                    pltpu.SMEM((2,), F32),
                    pltpu.SMEM((1,), jnp.int32),
                    dma((len(kept) + 3,)),
                ],
                compiler_params=pltpu.CompilerParams(vmem_limit_bytes=16 << 20),
                name="finish",
            )(res[2], res[3], *kept)
            return flag, (*done, rms)

        flag, fast = run(-(-mine * 11 // (16 * LANES)) * LANES, 0)
        done = lax.cond(flag[0] > 0, lambda: run(mine, 1)[1], lambda: fast)
        logits, igrad, g1, n1, l1, r1, g2, n2, l2, r2, m1, m2, new, rms = done
        return (logits, igrad, rms, g1, n1, l1, r1, g2.T, n2.T, l2.T, r2.T, m1, m2, new)

    placed = (
        P("mp", "dp"),
        P("mp", "dp"),
        P("dp", None),
        P(None, "dp", "mp"),
        P(None, "dp", "mp"),
        P(None, "dp", "mp"),
        P("dp", "mp"),
        P("mp", "dp"),
        P("dp", "mp"),
        P("dp", "mp"),
        P("mp", "dp"),
        P("mp", "dp"),
        P("dp", None),
        P("mp", None),
        P("mp", None),
        P("dp", None),
    )
    return jax.shard_map(
        on_device,
        mesh=mesh,
        in_specs=placed,
        out_specs=(
            P("mp", "dp"),
            P("mp", "dp"),
            P(),
            P("dp", "mp"),
            P("dp", "mp"),
            P("dp", "mp"),
            P("dp", "mp"),
            P("mp", "dp"),
            P("mp", "dp"),
            P("mp", "dp"),
            P("mp", "dp"),
            P(None, "dp", "mp"),
            P(None, "dp", "mp"),
            P(None, "dp", "mp"),
        ),
        check_vma=False,
    )
```
